128 devices in a mesh: lon: 16 (over x, z), lat: 8 (over y, core).
Axes of the slice: x: 4, y: 4, z: 4, core: 2. Of those that a mesh axis runs over, the one named last changes fastest.
Arguments:
- ocean_state: float32 [4, 20, 1024, 4096], P(None, None, 'lat', 'lon'), may hold values from -6 to 6
- canopy_type: int32 [1024, 4096], P('lat', 'lon'), may hold values from 0 to 7
- drag_table: float32 [8, 20], replicated, may hold values from 0.1 to 10
- ocean_list: int32 [128, 16384], P(('lon', 'lat')), may hold values from -1 to 32767, as said below
- ice_list: int32 [128, 16384], P(('lon', 'lat')), may hold values from -1 to 8191, as said below
- weight_list: int32 [128, 16384], P(('lon', 'lat')), may hold values from -1 to 63, as said below
- area_table: float32 [64], replicated, may hold values from 0.05 to 1
- ice_temp: float32 [128, 8192], P(('lon', 'lat')), may hold values from -6 to 6
- ice_cond: float32 [128, 8192], P(('lon', 'lat')), may hold values from 0.3 to 3
- ice_vel: float32 [128, 2, 8192], P(('lon', 'lat')), may hold values from -6 to 6
Outputs:
- ocean_next: float32 [4, 20, 1024, 4096], P(None, None, 'lat', 'lon')
- ice_temp_next: float32 [128, 8192], P(('lon', 'lat'))
The draws below stay inside these ranges and needn't reach their ends.
Inputs may be any that keep to these rules, and one draw needn't show every extreme that they name: `ocean_list`: entry [s, d * 128 + c] is the surface cell (row * 256 + column within source s's block) of slot c of the pair (s, d); used slots come first in each pair, the rest hold -1. A pair uses at most 128 slots, and some device receives 128 from every source. `ice_list`: entry [d, s * 128 + c] is the ice cell on device d of the same slot of the pair (s, d); -1 exactly where ocean_list is -1. `weight_list`: entry [d, s * 128 + c] is the area weight index of the same slot; -1 exactly where ocean_list is -1.
All inputs are finite; a program needn't handle non-finite values.
Results may differ from the reference program's by a relative error of at most 0.0001.
Values sent between devices are 32-bit elements; how exact they have to be, the bound alone decides.
A program may use at most 192 MiB of HBM per device.

```python
import math
import jax
import jax.numpy as jnp
from jax import lax

K = 20
CI = 256
CJ = 128
NTYPES = 8
NW = 64
SLOTS = 128
ICE_DEV = 8192
NLON = 4096
NLAT = 1024
N_LON = 16
N_LAT = 8
DEVICES = 128


def pair_counts(key):
    key = jax.random.fold_in(key, 977)
    base_key, hot_key = jax.random.split(key)
    base_counts = jax.random.randint(base_key, (DEVICES, DEVICES), SLOTS // 3, SLOTS // 2 + 1)
    hot_order = jax.random.permutation(hot_key, DEVICES)
    column = jnp.arange(DEVICES)[None, :]
    busy_column = (column == hot_order[0]) | (column == hot_order[1])
    return jnp.where(busy_column, SLOTS, base_counts).astype(jnp.int32)


def draw_ocean_list(key, part):
    counts = pair_counts(key)
    key = jax.random.fold_in(key, 11)
    cell_draw = jax.random.randint(key, (DEVICES, DEVICES, SLOTS), 0, CJ * CI)
    in_use = jnp.arange(SLOTS)[None, None, :] < counts[:, :, None]
    return jnp.where(in_use, cell_draw, -1).reshape(DEVICES, DEVICES * SLOTS).astype(jnp.int32)


def draw_ice_list(key, part):
    counts = pair_counts(key)
    key = jax.random.fold_in(key, 12)
    cell_draw = jax.random.randint(key, (DEVICES, DEVICES, SLOTS), 0, ICE_DEV)
    in_use = jnp.arange(SLOTS)[None, None, :] < jnp.transpose(counts)[:, :, None]
    return jnp.where(in_use, cell_draw, -1).reshape(DEVICES, DEVICES * SLOTS).astype(jnp.int32)


def draw_weight_list(key, part):
    counts = pair_counts(key)
    key = jax.random.fold_in(key, 13)
    index_draw = jax.random.randint(key, (DEVICES, DEVICES, SLOTS), 0, NW)
    in_use = jnp.arange(SLOTS)[None, None, :] < jnp.transpose(counts)[:, :, None]
    return jnp.where(in_use, index_draw, -1).reshape(DEVICES, DEVICES * SLOTS).astype(jnp.int32)


def set_ends(values, rng, least, largest):
    index_at = [jax.random.randint(jax.random.fold_in(rng, axis), (), 0, length) for axis, length in enumerate(values.shape)]
    longest = values.shape.index(max(values.shape))
    neighbour = index_at[:longest] + [(index_at[longest] + 1) % values.shape[longest]] + index_at[longest + 1:]
    return values.at[tuple(index_at)].set(least).at[tuple(neighbour)].set(largest)


def shard_levels(own_key, shape, pieces, smallest, largest):
    level = 1.0
    for axis_at, parts in pieces:
        steps = jax.random.uniform(jax.random.fold_in(jax.random.fold_in(own_key, 6), axis_at), (parts,), jnp.float32, smallest / len(pieces), largest / len(pieces))
        level = level * jnp.repeat(jnp.exp(steps), shape[axis_at] // parts).reshape((-1,) + (1,) * (len(shape) - 1 - axis_at))
    return level


def scatter_about(key, extent, spread, reach, shards=(), kind=jnp.bfloat16):
    entries = jax.random.normal(key, extent, jnp.float32) * spread
    if len(shards) > 0:
        entries = shard_levels(key, extent, shards, -0.22, 0.18) * entries
    return jnp.clip(entries, min=-reach, max=reach).astype(kind)


def setup_inputs(seed: int = 0) -> dict:
    keys = jax.random.split(jax.random.key(seed), 11)
    ocean_state = scatter_about(keys[0], (4, K, NLAT, NLON), 1.0, 6.0, ((2, 8), (3, 16)), jnp.float32)
    canopy_type = set_ends(jax.random.randint(keys[1], (NLAT, NLON), 0, NTYPES), jax.random.fold_in(keys[1], 1), 0, NTYPES - 1).astype(jnp.int32)
    drag_table = jnp.clip(jnp.exp(jax.random.uniform(keys[2], (NTYPES, K), jnp.float32, math.log(0.1), math.log(10.0))), 0.1, 10.0)
    ocean_list = draw_ocean_list(jax.random.fold_in(keys[10], 71), 0)
    ice_list = draw_ice_list(jax.random.fold_in(keys[10], 71), 0)
    weight_list = draw_weight_list(jax.random.fold_in(keys[10], 71), 0)
    area_table = jnp.clip(jnp.exp(jax.random.uniform(keys[6], (NW,), jnp.float32, math.log(0.05), math.log(1.0))), 0.05, 1.0)
    ice_temp = scatter_about(keys[7], (DEVICES, ICE_DEV), 1.0, 6.0, ((0, 128),), jnp.float32)
    ice_cond = jnp.clip(jnp.exp(math.log(3.0) - 2.3025851 * jax.random.uniform(keys[8], (DEVICES, ICE_DEV), jnp.float32) ** shard_levels(keys[8], (DEVICES, ICE_DEV), ((0, 128),), -0.2, 0.2)), 0.3, 3.0)
    ice_vel = scatter_about(keys[9], (DEVICES, 2, ICE_DEV), 1.0, 6.0, ((0, 128),), jnp.float32)
    return dict(ocean_state=ocean_state, canopy_type=canopy_type, drag_table=drag_table, ocean_list=ocean_list, ice_list=ice_list, weight_list=weight_list, area_table=area_table, ice_temp=ice_temp, ice_cond=ice_cond, ice_vel=ice_vel)


TIME_STEP = 0.1
FLUX_STEP = 0.5
DIFFUSIVITY = 0.1
VISCOSITY = 0.1
THERMAL_EXP = 0.2
HALINE_CONTRACT = 0.8
GRAV_LAYER = 0.5
CORIOLIS = 1.0
VERTICAL_MIX = 0.5
ICE_RATE = 0.25
ICE_DRAG = 0.5
BRINE_RATE = 0.5
SPEED_BACKGROUND = 0.01
FOLD_SIGNS = (1.0, 1.0, -1.0, -1.0)

def neighbours(values):
    return (values[..., 1:-1, 1:-1], values[..., 1:-1, 2:], values[..., 1:-1, :-2], values[..., 2:, 1:-1], values[..., :-2, 1:-1])

def provisional(extended, coriolis):
    centre, east_side, west_side, north_side, south_side = neighbours(extended)
    density = HALINE_CONTRACT * extended[1] - THERMAL_EXP * extended[0]
    above_sum = jnp.cumsum(density, axis=0) - density
    pressure = GRAV_LAYER * (above_sum + 0.5 * density)
    pressure_sides = neighbours(pressure)
    face_east = 0.5 * (centre[2] + east_side[2])
    face_west = 0.5 * (west_side[2] + centre[2])
    face_north = 0.5 * (centre[3] + north_side[3])
    face_south = 0.5 * (south_side[3] + centre[3])
    advection = face_east * 0.5 * (centre + east_side) - face_west * 0.5 * (west_side + centre) + face_north * 0.5 * (centre + north_side) - face_south * 0.5 * (south_side + centre)
    laplace = east_side + west_side + north_side + south_side - 4.0 * centre
    tracers = centre[0:2] + TIME_STEP * (DIFFUSIVITY * laplace[0:2] - advection[0:2])
    u_next = centre[2] + TIME_STEP * (coriolis * centre[3] - 0.5 * (pressure_sides[1] - pressure_sides[2]) + VISCOSITY * laplace[2] - advection[2])
    v_next = centre[3] + TIME_STEP * (-coriolis * centre[2] - 0.5 * (pressure_sides[3] - pressure_sides[4]) + VISCOSITY * laplace[3] - advection[3])
    return jnp.concatenate([tracers, u_next[None], v_next[None]], axis=0)

def vertical_mix(column_data):
    depth = column_data.shape[1]
    upper_terms = []
    right_terms = []
    divisor = 1.0 + VERTICAL_MIX
    upper = -VERTICAL_MIX / divisor
    right_side = column_data[:, 0] / divisor
    upper_terms.append(upper)
    right_terms.append(right_side)
    for depth_index in range(1, depth):
        diagonal = 1.0 + VERTICAL_MIX if depth_index == depth - 1 else 1.0 + 2.0 * VERTICAL_MIX
        divisor = diagonal + VERTICAL_MIX * upper
        upper = -VERTICAL_MIX / divisor
        right_side = (column_data[:, depth_index] + VERTICAL_MIX * right_side) / divisor
        upper_terms.append(upper)
        right_terms.append(right_side)
    solved = [right_terms[-1]]
    for depth_index in range(depth - 2, -1, -1):
        solved.append(right_terms[depth_index] - upper_terms[depth_index] * solved[-1])
    return jnp.stack(solved[::-1], axis=1)

def finish(provisional_state, surface_flux, drag_coef):
    forced = provisional_state.at[:, 0].add(FLUX_STEP * surface_flux)
    drift_speed = jnp.sqrt(forced[2] * forced[2] + forced[3] * forced[3] + SPEED_BACKGROUND)
    damping = 1.0 / (1.0 + TIME_STEP * drag_coef * drift_speed)
    damped = jnp.concatenate([forced[0:2], forced[2:4] * damping[None]], axis=0)
    return vertical_mix(damped)

def slot_fluxes(arrived, area_weight, temp_ice, cond_ice, u_ice, v_ice):
    drift_u = u_ice - arrived[2]
    drift_v = v_ice - arrived[3]
    drift_speed = jnp.sqrt(drift_u * drift_u + drift_v * drift_v + SPEED_BACKGROUND)
    heat_flux = area_weight * cond_ice * (temp_ice - arrived[0])
    salt_flux = -BRINE_RATE * area_weight * cond_ice * arrived[1]
    stress_u = ICE_DRAG * area_weight * drift_speed * drift_u
    stress_v = ICE_DRAG * area_weight * drift_speed * drift_v
    return jnp.stack([heat_flux, salt_flux, stress_u, stress_v])

def reference(ocean_state, canopy_type, drag_table, ocean_list, ice_list, weight_list, area_table, ice_temp, ice_cond, ice_vel):
    fold_sign = jnp.array(FOLD_SIGNS, jnp.float32)[:, None, None, None]
    fold_row = ocean_state[:, :, -1:, ::-1] * fold_sign
    south_row = jnp.zeros_like(fold_row)
    tall_state = jnp.concatenate([south_row, ocean_state, fold_row], axis=2)
    extended = jnp.concatenate([tall_state[..., -1:], tall_state, tall_state[..., :1]], axis=3)
    rows_global = jnp.arange(NLAT).astype(jnp.float32)
    coriolis = (CORIOLIS * (2.0 * (rows_global + 0.5) / NLAT - 1.0))[:, None]
    provisional_state = provisional(extended, coriolis)
    kind_mask = (canopy_type[None] == jnp.arange(NTYPES)[:, None, None]).astype(jnp.float32)
    drag_coef = jnp.einsum('tk,tji->kji', drag_table, kind_mask, precision=lax.Precision.HIGHEST)
    devices = N_LON * N_LAT
    cell_list = ocean_list.reshape(devices, devices, SLOTS)
    in_use = cell_list >= 0
    safe_cell = jnp.where(in_use, cell_list, 0)
    source = jnp.arange(devices)
    lon_of = (source // N_LAT)[:, None, None]
    lat_of = (source % N_LAT)[:, None, None]
    global_row = lat_of * CJ + safe_cell // CI
    global_col = lon_of * CI + safe_cell % CI
    flat_index = (global_row * NLON + global_col).astype(jnp.int32)
    surface = ocean_state[:, 0].reshape(4, NLAT * NLON)
    sent_values = jnp.where(in_use[None], jnp.take(surface, flat_index, axis=1), 0.0)
    arrived = jnp.transpose(sent_values, (0, 2, 1, 3))
    ice_cells = ice_list.reshape(devices, devices * SLOTS)
    safe_ice = jnp.where(ice_cells >= 0, ice_cells, 0)
    weight_index = weight_list.reshape(devices, devices * SLOTS)
    area_weight = jnp.where(weight_index >= 0, jnp.take(area_table, jnp.where(weight_index >= 0, weight_index, 0)), 0.0)
    temp_ice = jnp.take_along_axis(ice_temp, safe_ice, axis=1)
    cond_ice = jnp.take_along_axis(ice_cond, safe_ice, axis=1)
    u_ice = jnp.take_along_axis(ice_vel[:, 0], safe_ice, axis=1)
    v_ice = jnp.take_along_axis(ice_vel[:, 1], safe_ice, axis=1)
    shape_slots = (devices, devices, SLOTS)
    fluxes = slot_fluxes(arrived, area_weight.reshape(shape_slots), temp_ice.reshape(shape_slots), cond_ice.reshape(shape_slots), u_ice.reshape(shape_slots), v_ice.reshape(shape_slots))
    owner = jnp.arange(devices)[:, None] * ICE_DEV + safe_ice
    heat_sum = jax.ops.segment_sum(fluxes[0].reshape(-1), owner.reshape(-1).astype(jnp.int32), devices * ICE_DEV)
    ice_temp_next = ice_temp - ICE_RATE * heat_sum.reshape(devices, ICE_DEV)
    returned = jnp.transpose(fluxes, (0, 2, 1, 3))
    flat_cells = flat_index.reshape(-1)
    flux_parts = []
    for component in range(4):
        flux_parts.append(jax.ops.segment_sum(returned[component].reshape(-1), flat_cells, NLAT * NLON))
    surface_flux = jnp.stack(flux_parts).reshape(4, NLAT, NLON)
    ocean_next = finish(provisional_state, surface_flux, drag_coef)
    return (ocean_next, ice_temp_next)
```

```python
import functools

import jax
import jax.numpy as jnp
from jax import lax
from jax.experimental import pallas as pl
from jax.experimental.pallas import tpu as pltpu
from jax.sharding import PartitionSpec as P

f32 = jnp.float32
bf16 = jnp.bfloat16
i32 = jnp.int32
MESH = pl.DeviceIdType.MESH
K = 20
NF = 4
FK = NF * K
CJ = 128
CI = 256
NLON = 16
NLAT = 8
DEV = NLON * NLAT
SLOTS = 128
ROWS = 8
SENT = 6
SCALE = 40.0

DIAG = [1.5]
for _k in range(1, K):
    DIAG.append((1.5 if _k == K - 1 else 2.0) - 0.25 / DIAG[-1])
FWD = [0.0] + [0.5 / DIAG[_k - 1] for _k in range(1, K)]
TOP = [1.0]
for _k in range(1, K):
    TOP.append(FWD[_k] * TOP[-1])

VM = pl.BlockSpec(memory_space=pltpu.VMEM)
ANY = pl.BlockSpec(memory_space=pl.ANY)
LIMIT = 60 << 20


def lanes():
    return lax.broadcasted_iota(i32, (8, 128), 1)


def take(table, index, axis):
    return jnp.take_along_axis(table, index, axis=axis, mode="promise_in_bounds")


def split(x):
    high = x.astype(bf16)
    return high, (x - high.astype(f32)).astype(bf16)


def one_hot(index, count):
    rows = lax.broadcasted_iota(i32, (count, index.shape[1]), 0)
    return rows == jnp.broadcast_to(index, (count, index.shape[1]))


def pack(even, odd):
    left = lanes() < 64
    return (
        jnp.where(left, even, pltpu.roll(odd, 64, 1)),
        jnp.where(left, pltpu.roll(even, 64, 1), odd),
    )


def pack_list(source, packed):
    for g in range(8):
        first, second = pack(
            source[pl.ds(16 * g, 8, stride=2), :], source[pl.ds(16 * g + 1, 8, stride=2), :]
        )
        packed[8 * g : 8 * g + 8, :] = first
        packed[64 + 8 * g : 72 + 8 * g, :] = second


def long_pairs(flags, first, count):
    most = flags[first, 64]
    for i in range(1, count):
        most = jnp.maximum(most, flags[first + i, 64])
    return most >= 0


def gather_kernel(
    st, olist_any, ilist_any, olist, ilist, wlist, area, itemp, icond, ivel,
    out, tuv, rowlo, rowhi, colw, cole,
    full, otab, itab, opack, ipack, ogot, igot, oflag, iflag, sems,
):
    flags = [
        pltpu.make_async_copy(olist_any, oflag, sems.at[0]),
        pltpu.make_async_copy(ilist_any, iflag, sems.at[1]),
    ]
    loads = []
    for n, f in enumerate((0, 2, 3, 1)):
        loads.append([
            pltpu.make_async_copy(
                st.at[f * K : (f + 1) * K, :, c * 128 : (c + 1) * 128],
                full.at[c, f * K : (f + 1) * K],
                sems.at[2 + 2 * n + c],
            )
            for c in range(2)
        ])
    for copy in flags:
        copy.start()
    for pair in loads:
        for copy in pair:
            copy.start()
    pack_list(olist, opack)
    pack_list(ilist, ipack)
    ogot[...] = jnp.zeros_like(ogot)
    igot[...] = jnp.zeros_like(igot)
    for f in range(4):
        for c in range(2):
            if f < 2:
                x = (icond, itemp)[f][pl.ds(c, 32, stride=2), :]
            else:
                x = ivel[pl.ds(2 * c + f - 2, 32, stride=4), :]
            high, low = split(x)
            itab[32 * f : 32 * f + 32, c * 128 : (c + 1) * 128] = high
            itab[128 + 32 * f : 160 + 32 * f, c * 128 : (c + 1) * 128] = low

    def gather(tile, packed, table, fields, rows, got):
        hots, his = [], []
        for h in range(2):
            row = packed[pl.ds(2 * tile + h, 1), :]
            his.append(row >> 8)
            hots.append(jnp.where(one_hot(row & 255, 256), 1.0, 0.0).astype(bf16))
        res = jnp.dot(table[...], jnp.concatenate(hots, axis=1), preferred_element_type=f32)
        half = fields * rows
        res = res[:half] + res[half:]
        for h in range(2):
            mask = one_hot(his[h], rows)
            for f in range(fields):
                value = jnp.where(mask, res[f * rows : (f + 1) * rows, h * 128 : (h + 1) * 128], 0.0)
                got[pl.ds(f * 128 + 2 * tile + h, 1), :] = jnp.sum(value, axis=0, keepdims=True)

    @pl.loop(0, 32, step=4)
    def _(t):
        for j in range(4):
            gather(t + j, ipack, itab, 4, 32, igot)

    for copy in flags:
        copy.wait()

    @pl.loop(0, 32)
    def _(t):
        @pl.when(long_pairs(iflag, 4 * t, 4))
        def _():
            gather(32 + t, ipack, itab, 4, 32, igot)

    for n in range(3):
        for copy in loads[n]:
            copy.wait()
    for n, f in enumerate((0, 2, 3)):
        for c in range(2):
            high, low = split(full[c, f * K])
            otab[128 * n : 128 * n + 128, c * 128 : (c + 1) * 128] = high
            otab[384 + 128 * n : 512 + 128 * n, c * 128 : (c + 1) * 128] = low

    @pl.loop(0, 32, step=2)
    def _(t):
        for j in range(2):
            gather(t + j, opack, otab, 3, 128, ogot)

    @pl.loop(0, 32)
    def _(t):
        @pl.when(long_pairs(oflag, 4 * t, 4))
        def _():
            gather(32 + t, opack, otab, 3, 128, ogot)

    left = lanes() < 64

    def unpack(got, f, g):
        first = got[f * 128 + 8 * g : f * 128 + 8 * g + 8, :]
        second = got[f * 128 + 64 + 8 * g : f * 128 + 72 + 8 * g, :]
        return (
            jnp.where(left, first, pltpu.roll(second, 64, 1)),
            jnp.where(left, pltpu.roll(first, 64, 1), second),
        )

    areas = jnp.broadcast_to(jnp.concatenate([area[...], area[...]], axis=1), (8, 128))
    for g in range(8):
        for n in range(3):
            even, odd = unpack(ogot, n, g)
            tuv[pl.ds(128 * n + 16 * g, 8, stride=2), :] = even
            tuv[pl.ds(128 * n + 16 * g + 1, 8, stride=2), :] = odd
            if n == 0:
                out[pl.ds(128 * g, 8, stride=16), :] = even
                out[pl.ds(128 * g + 8, 8, stride=16), :] = odd
        for f in range(4):
            even, odd = unpack(igot, f, g)
            out[pl.ds(128 * g + 2 + f, 8, stride=16), :] = even
            out[pl.ds(128 * g + 10 + f, 8, stride=16), :] = odd
    for g in range(16):
        index = wlist[8 * g : 8 * g + 8, :]
        value = jnp.where(index >= 0, take(areas, index & 63, 1), 0.0)
        out[pl.ds(64 * g + 1, 8, stride=8), :] = value
        for f in range(SENT, ROWS):
            out[pl.ds(64 * g + f, 8, stride=8), :] = jnp.zeros((8, 128), f32)

    for copy in loads[3]:
        copy.wait()
    for fk in range(FK):
        for c in range(2):
            rowlo[fk : fk + 1, c * 128 : (c + 1) * 128] = full[c, fk, 0:1, :]
            rowhi[fk : fk + 1, c * 128 : (c + 1) * 128] = full[c, fk, 127:128, :]

    @pl.loop(0, 16)
    def _(m):
        lane = lanes()
        rows = pl.ds(pl.multiple_of(8 * m, 8), 8)
        west = jnp.zeros((8, 128), f32)
        east = jnp.zeros((8, 128), f32)
        for fk in range(FK):
            both = jnp.where(lane == 127, full[1, fk, rows, :], full[0, fk, rows, :])
            both = pltpu.roll(both, fk, 1) if fk else both
            west = jnp.where(lane == fk, both, west)
            east = jnp.where(lane == (fk - 1) % 128, both, east)
        colw[rows, :] = west
        cole[rows, :] = east


def stencil_row(m, buf, q, canopy, east_col, west_col, drag, lat):
    lane = lanes()
    sub = lax.broadcasted_iota(i32, (8, 128), 0)
    first, last = lane == 0, lane == 127
    rows = pl.ds(pl.multiple_of(8 * m, 8), 8)
    east_halo, west_halo = east_col[rows, :], west_col[rows, :]
    kind = [canopy[rows, c * 128 : (c + 1) * 128] for c in range(2)]
    row = (lat * CJ + 8 * m + sub).astype(f32)
    cor = 4.0 * (2.0 * (row + 0.5) / (CJ * NLAT) - 1.0)
    elim = [[None] * 2 for _ in range(NF)]
    gx, gy = [None] * 2, [None] * 2
    for k in range(K):
        C, E, W, N, S = ([[None] * 2 for _ in range(NF)] for _ in range(5))
        for f in range(NF):
            fk = f * K + k
            for c in range(2):
                C[f][c] = buf[c, fk, pl.ds(pl.multiple_of(8 + 8 * m, 8), 8), :]
                N[f][c] = buf[c, fk, pl.ds(9 + 8 * m, 8), :]
                S[f][c] = buf[c, fk, pl.ds(7 + 8 * m, 8), :]
            e0, e1 = (pltpu.roll(C[f][c], 127, 1) for c in range(2))
            w0, w1 = (pltpu.roll(C[f][c], 1, 1) for c in range(2))
            E[f][0] = jnp.where(last, e1, e0)
            E[f][1] = jnp.where(last, pltpu.roll(east_halo, (127 - fk) % 128, 1), e1)
            W[f][0] = jnp.where(first, pltpu.roll(west_halo, (1 - fk) % 128, 1), w0)
            W[f][1] = jnp.where(first, w0, w1)
        for c in range(2):
            u, v = C[2][c], C[3][c]
            eE = (0.4 - u) - E[2][c]
            eW = (0.4 + u) + W[2][c]
            eN = (0.4 - v) - N[3][c]
            eS = (0.4 + v) + S[3][c]
            mid = 36.8 + ((eE + eW) + (eN + eS))
            new = [
                (C[f][c] * mid + E[f][c] * eE) + (W[f][c] * eW + N[f][c] * eN) + S[f][c] * eS
                for f in range(NF)
            ]
            hx = 0.4 * (E[1][c] - W[1][c]) - 0.1 * (E[0][c] - W[0][c])
            hy = 0.4 * (N[1][c] - S[1][c]) - 0.1 * (N[0][c] - S[0][c])
            px = hx if k == 0 else gx[c] + hx
            py = hy if k == 0 else gy[c] + hy
            gx[c], gy[c] = px + hx, py + hy
            new[2] = new[2] + (cor * v - px)
            new[3] = new[3] - (cor * u + py)
            if k > 0:
                x = new[2] * new[2] + (new[3] * new[3] + 0.01 * SCALE * SCALE)
                damp = 1.0 / (1.0 + take(drag[k], kind[c], 0) * (x * lax.rsqrt(x)))
                new[2], new[3] = new[2] * damp, new[3] * damp
            for f in range(NF):
                if k > 1:
                    new[f] = new[f] + FWD[k] * elim[f][c]
                elim[f][c] = new[f]
                q[m, f * K + k, c * 8 : (c + 1) * 8, :] = new[f]


def drag_levels(table, drag):
    for k in range(K):
        drag[k] = jnp.broadcast_to(table[:, k : k + 1] * (0.1 / SCALE), (8, 128))


def stencil_kernel(
    st, out, canopy, table, rowlo, rowhi, colw, cole,
    q, inb,
    buf, drag, mid, north, south, east_col, west_col, sems, hops, halo_send, halo_recv,
):
    lon, lat = lax.axis_index("lon"), lax.axis_index("lat")
    loads = [
        [
            pltpu.make_async_copy(
                st.at[:, 32 * g : 32 * g + 32, c * 128 : (c + 1) * 128],
                buf.at[c, :, 8 + 32 * g : 40 + 32 * g, :],
                sems.at[g, c],
            )
            for c in range(2)
        ]
        for g in range(4)
    ]
    for pair in loads:
        for copy in pair:
            copy.start()

    barrier = pltpu.get_barrier_semaphore()
    for i in range(1, NLON):
        pl.semaphore_signal(barrier, inc=1, device_id=(lax.rem(lon + i, NLON), lat), device_id_type=MESH)
    for i in range(1, NLAT):
        pl.semaphore_signal(barrier, inc=1, device_id=(lon, lax.rem(lat + i, NLAT)), device_id_type=MESH)
    pl.semaphore_wait(barrier, NLON + NLAT - 2)

    def halo(src, dst, n, target):
        return pltpu.make_async_remote_copy(
            src_ref=src, dst_ref=dst, send_sem=halo_send.at[n], recv_sem=halo_recv.at[n],
            device_id=target, device_id_type=MESH,
        )

    to_west = halo(colw, east_col, 0, (lax.rem(lon + NLON - 1, NLON), lat))
    to_east = halo(cole, west_col, 1, (lax.rem(lon + 1, NLON), lat))
    to_north = halo(rowhi, south, 2, (lon, lax.rem(lat + 1, NLAT)))
    to_south = halo(rowlo, north, 3, (lon, lax.rem(lat + NLAT - 1, NLAT)))
    to_fold = halo(rowhi, north, 3, (NLON - 1 - lon, lat))
    to_west.start()
    to_east.start()
    to_north.start()

    @pl.when(lat > 0)
    def _():
        to_south.start()

    @pl.when(lat == NLAT - 1)
    def _():
        pltpu.make_async_remote_copy(
            src_ref=rowhi, dst_ref=north, send_sem=halo_send.at[4], recv_sem=halo_recv.at[3],
            device_id=(NLON - 1 - lon, lat), device_id_type=MESH,
        ).start()

    for i in range(1, NLON):
        peer = lax.rem(lon + i, NLON)
        pltpu.make_async_remote_copy(
            src_ref=out.at[pl.ds(peer * NLAT, NLAT)], dst_ref=mid.at[pl.ds(lon * NLAT, NLAT)],
            send_sem=hops.at[0], recv_sem=hops.at[1], device_id=(peer, lat), device_id_type=MESH,
        ).start()
    own = pltpu.make_async_copy(out.at[pl.ds(lon * NLAT, NLAT)], mid.at[pl.ds(lon * NLAT, NLAT)], hops.at[2])
    own.start()

    drag_levels(table, drag)
    to_west.wait_recv()
    to_east.wait_recv()
    to_north.wait_recv()
    to_fold.wait_recv()
    top = lat == NLAT - 1
    inside = jnp.where(lat > 0, 1.0, 0.0)
    back = 127 - lanes()
    for g in range(10):
        part = slice(8 * g, 8 * g + 8)
        sign = 1.0 if g < 5 else -1.0
        halves = [north[part, c * 128 : (c + 1) * 128] for c in range(2)]
        for c in range(2):
            turned = sign * take(halves[1 - c], back, 1)
            value = jnp.where(top, turned, halves[c])
            below = south[part, c * 128 : (c + 1) * 128] * inside
            for r in range(8):
                buf[c, 8 * g + r, 136:137, :] = value[r : r + 1]
                buf[c, 8 * g + r, 7:8, :] = below[r : r + 1]
    for copy in loads[0]:
        copy.wait()

    @pl.loop(0, 4)
    def _(g):
        @pl.when(g < 3)
        def _():
            for c in range(2):
                pltpu.make_async_copy(
                    st.at[:, 0:32, 0:128], buf.at[c, :, 8:40, :], sems.at[g + 1, c]
                ).wait()

        @pl.when(g == 2)
        def _():
            many = mid.at[0 : (NLON - 1) * NLAT]
            pltpu.make_async_copy(many, many, hops.at[1]).wait()
            own.wait()
            mid4 = mid.reshape(NLON, NLAT, ROWS, 128)
            in4 = inb.reshape(NLON, NLAT, ROWS, 128)
            for i in range(1, NLAT):
                peer = lax.rem(lat + i, NLAT)
                pltpu.make_async_remote_copy(
                    src_ref=mid4.at[:, peer], dst_ref=in4.at[:, lat],
                    send_sem=hops.at[3], recv_sem=hops.at[4], device_id=(lon, peer), device_id_type=MESH,
                ).start()
            pltpu.make_async_copy(mid4.at[:, lat], in4.at[:, lat], hops.at[2]).start()

        @pl.loop(0, 4)
        def _(j):
            stencil_row(4 * g + j, buf, q, canopy, east_col, west_col, drag, lat)

    some = inb.at[0 : (NLAT - 1) * NLON]
    pltpu.make_async_copy(some, some, hops.at[4]).wait()
    pltpu.make_async_copy(some, some, hops.at[3]).wait()
    one = inb.at[0:NLON]
    pltpu.make_async_copy(one, one, hops.at[2]).wait()
    many = mid.at[0 : (NLON - 1) * NLAT]
    pltpu.make_async_copy(many, many, hops.at[0]).wait()
    to_west.wait_send()
    to_east.wait_send()
    to_north.wait_send()

    @pl.when(lat > 0)
    def _():
        to_south.wait_send()

    @pl.when(lat == NLAT - 1)
    def _():
        pltpu.make_async_copy(rowhi, rowhi, halo_send.at[4]).wait()


def finish_kernel(
    st, olist_any, ilist_any, q, inb, out, tuv, olist, ilist, canopy, table, itemp,
    y, itemp_next,
    ybuf, salt, drag, opack, ipack, oval, ival, oacc, iacc, wide, cols, oflag, iflag, sems,
):
    flags = [
        pltpu.make_async_copy(olist_any, oflag, sems.at[0]),
        pltpu.make_async_copy(ilist_any, iflag, sems.at[1]),
    ]
    salts = [
        pltpu.make_async_copy(st.at[K, :, c * 128 : (c + 1) * 128], salt.at[c], sems.at[2 + c])
        for c in range(2)
    ]
    for copy in flags + salts:
        copy.start()
    drag_levels(table, drag)
    pack_list(olist, opack)
    pack_list(ilist, ipack)
    for g in range(8):
        sides, ices = [], []
        for odd in range(2):
            block = lambda ref, f: ref[pl.ds(128 * g + 8 * odd + f, 8, stride=16), :]
            slot = [tuv[pl.ds(128 * n + 16 * g + odd, 8, stride=2), :] for n in range(3)]
            a, cond, temp, iu, iv = (block(inb, f) for f in range(1, 6))
            du, dv = iu - slot[1], iv - slot[2]
            x = du * du + dv * dv + 0.01
            drift = 0.5 * a * (x * lax.rsqrt(x))
            heat = a * cond
            sides.append([heat * (temp - slot[0]), heat, drift * du, drift * dv])
            ices.append(block(out, 1) * block(out, 2) * (block(out, 3) - block(inb, 0)))
        for f in range(4):
            first, second = pack(sides[0][f], sides[1][f])
            oval[128 * f + 8 * g : 128 * f + 8 * g + 8, :] = first
            oval[128 * f + 64 + 8 * g : 128 * f + 72 + 8 * g, :] = second
        first, second = pack(*ices)
        ival[8 * g : 8 * g + 8, :] = first
        ival[64 + 8 * g : 72 + 8 * g, :] = second
    oacc[...] = jnp.zeros_like(oacc)
    iacc[...] = jnp.zeros_like(iacc)

    def scatter(tile, packed, values, fields, rows, width, acc):
        for h in range(4):
            index = packed[pl.ds(4 * tile + h, 1), :]
            here = slice(128 * h, 128 * h + 128)
            cols[0:width, here] = jnp.where(one_hot(index & (width - 1), width), 1.0, 0.0).astype(bf16)
            mask = one_hot(index >> (width.bit_length() - 1), rows)
            for f in range(fields):
                value = values[pl.ds(128 * f + 4 * tile + h, 1), :]
                high = value.astype(bf16).astype(f32)
                for n, part in enumerate((high, value - high)):
                    part = jnp.where(mask, jnp.broadcast_to(part, (rows, 128)), 0.0).astype(bf16)
                    wide[rows * f : rows * (f + 1), 512 * n + 128 * h : 512 * n + 128 * h + 128] = part
        hot = cols[0:width, :]
        both = jnp.concatenate([hot, hot], axis=1)
        acc[...] += lax.dot_general(
            wide[0 : rows * fields, :], both, (((1,), (1,)), ((), ())), preferred_element_type=f32
        )

    def scatter_ocean(tile):
        scatter(tile, opack, oval, 4, CJ, CI, oacc)

    def scatter_ice(tile):
        scatter(tile, ipack, ival, 1, 64, 128, iacc)

    @pl.loop(0, 16)
    def _(t):
        scatter_ocean(t)

    @pl.loop(0, 16)
    def _(t):
        scatter_ice(t)

    for copy in flags:
        copy.wait()

    @pl.loop(0, 16)
    def _(t):
        @pl.when(long_pairs(oflag, 8 * t, 8))
        def _():
            scatter_ocean(16 + t)

        @pl.when(long_pairs(iflag, 8 * t, 8))
        def _():
            scatter_ice(16 + t)

    itemp_next[...] = itemp[...] - 0.25 * iacc[...]
    for copy in salts:
        copy.wait()

    @pl.loop(0, 16)
    def _(m):
        rows = pl.ds(pl.multiple_of(8 * m, 8), 8)
        sides = []
        for c in range(2):
            here = slice(8 * c, 8 * c + 8)
            flux = [
                oacc[pl.ds(pl.multiple_of(CJ * f + 8 * m, 8), 8), c * 128 : (c + 1) * 128] for f in range(4)
            ]
            top = [q[m, f * K, here, :] for f in range(4)]
            top[0] = top[0] + 20.0 * flux[0]
            top[1] = top[1] - 10.0 * (salt[c, rows, :] * flux[1])
            top[2] = top[2] + 20.0 * flux[2]
            top[3] = top[3] + 20.0 * flux[3]
            x = top[2] * top[2] + (top[3] * top[3] + 0.01 * SCALE * SCALE)
            damp = 1.0 / (1.0 + take(drag[0], canopy[rows, c * 128 : (c + 1) * 128], 0) * (x * lax.rsqrt(x)))
            top[2], top[3] = top[2] * damp, top[3] * damp
            sides.append(top)
        solved = [[None] * 4 for _ in range(2)]
        for k in range(K - 1, -1, -1):
            for c in range(2):
                for f in range(4):
                    here = slice(8 * c, 8 * c + 8)
                    value = sides[c][f] if k == 0 else q[m, f * K + k, here, :] + TOP[k] * sides[c][f]
                    value = value * (1.0 / (SCALE * DIAG[k]))
                    if k < K - 1:
                        value = value + (0.5 / DIAG[k]) * solved[c][f]
                    solved[c][f] = value
                    ybuf[m, f * K + k, here, :] = value
        for c in range(2):
            pltpu.make_async_copy(
                ybuf.at[m, :, 8 * c : 8 * c + 8, :], y.at[:, rows, c * 128 : (c + 1) * 128], sems.at[4 + c]
            ).start()

    for c in range(2):
        part = y.at[:, :, c * 128 : (c + 1) * 128]
        pltpu.make_async_copy(part, part, sems.at[4 + c]).wait()


def shards(
    ocean_state, canopy_type, drag_table, ocean_list, ice_list, weight_list, area_table, ice_temp, ice_cond, ice_vel
):
    st = ocean_state.reshape(FK, CJ, CI)
    olist, ilist, wlist = (x.reshape(DEV, SLOTS) for x in (ocean_list, ice_list, weight_list))
    itemp, icond = (x.reshape(64, 128) for x in (ice_temp, ice_cond))
    ivel = ice_vel.reshape(2, 64, 128).transpose(1, 0, 2).reshape(128, 128)
    area = area_table.reshape(1, 64)
    S = jax.ShapeDtypeStruct
    V = pltpu.VMEM
    out, tuv, rowlo, rowhi, colw, cole = pl.pallas_call(
        gather_kernel,
        out_shape=(
            S((DEV * ROWS, 128), f32), S((3 * 128, 128), f32), S((FK, CI), f32), S((FK, CI), f32),
            S((CJ, 128), f32), S((CJ, 128), f32),
        ),
        in_specs=[ANY] * 3 + [VM] * 7,
        out_specs=(VM,) * 6,
        scratch_shapes=[
            V((2, FK, CJ, 128), f32), V((768, 256), bf16), V((256, 256), bf16),
            V((128, 128), i32), V((128, 128), i32), V((3 * 128, 128), f32), V((4 * 128, 128), f32),
            pltpu.SMEM((128, 128), i32), pltpu.SMEM((128, 128), i32), pltpu.SemaphoreType.DMA((10,)),
        ],
        compiler_params=pltpu.CompilerParams(vmem_limit_bytes=LIMIT),
        name="gather_slots",
    )(st, olist, ilist, olist, ilist, wlist, area, itemp, icond, ivel)
    out3 = out.reshape(DEV, ROWS, 128)
    q, inb = pl.pallas_call(
        stencil_kernel,
        out_shape=(S((16, FK, 16, 128), f32), S((DEV, ROWS, 128), f32)),
        in_specs=[ANY] + [VM] * 7,
        out_specs=(VM, VM),
        scratch_shapes=[
            V((2, FK, 144, 128), f32), V((K, 8, 128), f32), V((DEV, ROWS, 128), f32),
            V((FK, CI), f32), V((FK, CI), f32), V((CJ, 128), f32), V((CJ, 128), f32),
            pltpu.SemaphoreType.DMA((4, 2)), pltpu.SemaphoreType.DMA((5,)),
            pltpu.SemaphoreType.DMA((5,)), pltpu.SemaphoreType.DMA((4,)),
        ],
        compiler_params=pltpu.CompilerParams(vmem_limit_bytes=LIMIT, collective_id=0, has_side_effects=True),
        name="exchange_stencil",
    )(st, out3, canopy_type, drag_table, rowlo, rowhi, colw, cole)
    y, itemp_next = pl.pallas_call(
        finish_kernel,
        out_shape=(S((FK, CJ, CI), f32), S((64, 128), f32)),
        in_specs=[ANY] * 3 + [VM] * 9,
        out_specs=(ANY, VM),
        scratch_shapes=[
            V((16, FK, 16, 128), f32), V((2, CJ, 128), f32), V((K, 8, 128), f32),
            V((128, 128), i32), V((128, 128), i32), V((4 * 128, 128), f32), V((128, 128), f32),
            V((4 * CJ, CI), f32), V((64, 128), f32), V((4 * CJ, 1024), bf16), V((CI, 512), bf16),
            pltpu.SMEM((128, 128), i32), pltpu.SMEM((128, 128), i32), pltpu.SemaphoreType.DMA((6,)),
        ],
        compiler_params=pltpu.CompilerParams(vmem_limit_bytes=LIMIT),
        name="scatter_solve",
    )(st, olist, ilist, q, inb.reshape(DEV * ROWS, 128), out, tuv, olist, ilist, canopy_type, drag_table, itemp)
    return y.reshape(ocean_state.shape), itemp_next.reshape(ice_temp.shape)


def solution(mesh):
    return jax.shard_map(
        shards,
        mesh=mesh,
        in_specs=(
            P(None, None, "lat", "lon"),
            P("lat", "lon"),
            P(),
            P(("lon", "lat"), None),
            P(("lon", "lat"), None),
            P(("lon", "lat"), None),
            P(),
            P(("lon", "lat"), None),
            P(("lon", "lat"), None),
            P(("lon", "lat"), None, None),
        ),
        out_specs=(P(None, None, "lat", "lon"), P(("lon", "lat"), None)),
        check_vma=False,
    )
```

```python
import functools

import jax
import jax.numpy as jnp
from jax import lax
from jax.experimental import pallas as pl
from jax.experimental.pallas import tpu as pltpu
from jax.sharding import PartitionSpec as P

f32 = jnp.float32
bf16 = jnp.bfloat16
i32 = jnp.int32
MESH = pl.DeviceIdType.MESH
K = 20
NF = 4
FK = NF * K
CJ = 128
CI = 256
NLON = 16
NLAT = 8
DEV = NLON * NLAT
SLOTS = 128
ROWS = 8
SENT = 6
SCALE = 40.0

DIAG = [1.5]
for _k in range(1, K):
    DIAG.append((1.5 if _k == K - 1 else 2.0) - 0.25 / DIAG[-1])
FWD = [0.0] + [0.5 / DIAG[_k - 1] for _k in range(1, K)]
TOP = [1.0]
for _k in range(1, K):
    TOP.append(FWD[_k] * TOP[-1])

VM = pl.BlockSpec(memory_space=pltpu.VMEM)
ANY = pl.BlockSpec(memory_space=pl.ANY)
LIMIT = 60 << 20


def lanes():
    return lax.broadcasted_iota(i32, (8, 128), 1)


def take(table, index, axis):
    return jnp.take_along_axis(table, index, axis=axis, mode="promise_in_bounds")


def split(x):
    high = x.astype(bf16)
    return high, (x - high.astype(f32)).astype(bf16)


def one_hot(index, count):
    rows = lax.broadcasted_iota(i32, (count, index.shape[1]), 0)
    return rows == jnp.broadcast_to(index, (count, index.shape[1]))


def pack(even, odd):
    left = lanes() < 64
    return (
        jnp.where(left, even, pltpu.roll(odd, 64, 1)),
        jnp.where(left, pltpu.roll(even, 64, 1), odd),
    )


def pack_list(source, packed):
    for g in range(8):
        first, second = pack(
            source[pl.ds(16 * g, 8, stride=2), :], source[pl.ds(16 * g + 1, 8, stride=2), :]
        )
        packed[8 * g : 8 * g + 8, :] = first
        packed[64 + 8 * g : 72 + 8 * g, :] = second


def long_pairs(flags, first, count):
    most = flags[first, 64]
    for i in range(1, count):
        most = jnp.maximum(most, flags[first + i, 64])
    return most >= 0


def gather_kernel(
    st, olist_any, ilist_any, olist, ilist, wlist, area, itemp, icond, ivel,
    out, tuv, rowlo, rowhi, colw, cole,
    full, surf, otab, itab, opack, ipack, ogot, igot, oflag, iflag, sems,
):
    flags = [
        pltpu.make_async_copy(olist_any, oflag, sems.at[0]),
        pltpu.make_async_copy(ilist_any, iflag, sems.at[1]),
    ]
    tops = [
        pltpu.make_async_copy(st.at[f * K, :, c * 128 : (c + 1) * 128], surf.at[n, c], sems.at[2])
        for n, f in enumerate((0, 2, 3))
        for c in range(2)
    ]
    state = [
        pltpu.make_async_copy(st.at[:, :, c * 128 : (c + 1) * 128], full.at[c], sems.at[3 + c]) for c in range(2)
    ]
    for copy in tops + flags + state:
        copy.start()
    pack_list(olist, opack)
    pack_list(ilist, ipack)
    ogot[...] = jnp.zeros_like(ogot)
    igot[...] = jnp.zeros_like(igot)
    for f in range(4):
        for c in range(2):
            if f < 2:
                x = (icond, itemp)[f][pl.ds(c, 32, stride=2), :]
            else:
                x = ivel[pl.ds(2 * c + f - 2, 32, stride=4), :]
            high, low = split(x)
            itab[32 * f : 32 * f + 32, c * 128 : (c + 1) * 128] = high
            itab[128 + 32 * f : 160 + 32 * f, c * 128 : (c + 1) * 128] = low

    def gather(tile, packed, table, fields, rows, got):
        hots, his = [], []
        for h in range(2):
            row = packed[pl.ds(2 * tile + h, 1), :]
            his.append(row >> 8)
            hots.append(jnp.where(one_hot(row & 255, 256), 1.0, 0.0).astype(bf16))
        res = jnp.dot(table[...], jnp.concatenate(hots, axis=1), preferred_element_type=f32)
        half = fields * rows
        res = res[:half] + res[half:]
        for h in range(2):
            mask = one_hot(his[h], rows)
            for f in range(fields):
                value = jnp.where(mask, res[f * rows : (f + 1) * rows, h * 128 : (h + 1) * 128], 0.0)
                got[pl.ds(f * 128 + 2 * tile + h, 1), :] = jnp.sum(value, axis=0, keepdims=True)

    @pl.loop(0, 32, step=4)
    def _(t):
        for j in range(4):
            gather(t + j, ipack, itab, 4, 32, igot)

    for copy in flags:
        copy.wait()

    @pl.loop(0, 32, step=4)
    def _(t):
        @pl.when(long_pairs(iflag, 4 * t, 16))
        def _():
            for j in range(4):
                gather(32 + t + j, ipack, itab, 4, 32, igot)

    pltpu.make_async_copy(surf, surf, sems.at[2]).wait()
    for n in range(3):
        for c in range(2):
            high, low = split(surf[n, c])
            otab[128 * n : 128 * n + 128, c * 128 : (c + 1) * 128] = high
            otab[384 + 128 * n : 512 + 128 * n, c * 128 : (c + 1) * 128] = low
    for copy in state:
        copy.wait()

    def columns(m):
        lane = lanes()
        rows = pl.ds(pl.multiple_of(8 * m, 8), 8)
        west = jnp.zeros((8, 128), f32)
        east = jnp.zeros((8, 128), f32)
        for fk in range(FK):
            both = jnp.where(lane == 127, full[1, fk, rows, :], full[0, fk, rows, :])
            both = pltpu.roll(both, fk, 1) if fk else both
            west = jnp.where(lane == fk, both, west)
            east = jnp.where(lane == (fk - 1) % 128, both, east)
        colw[rows, :] = west
        cole[rows, :] = east

    @pl.loop(0, 8)
    def _(t):
        for j in range(4):
            gather(4 * t + j, opack, otab, 3, 128, ogot)
        for j in range(2):
            columns(2 * t + j)

    @pl.loop(0, 32)
    def _(t):
        @pl.when(long_pairs(oflag, 4 * t, 4))
        def _():
            gather(32 + t, opack, otab, 3, 128, ogot)

    left = lanes() < 64

    def unpack(got, f, g):
        first = got[f * 128 + 8 * g : f * 128 + 8 * g + 8, :]
        second = got[f * 128 + 64 + 8 * g : f * 128 + 72 + 8 * g, :]
        return (
            jnp.where(left, first, pltpu.roll(second, 64, 1)),
            jnp.where(left, pltpu.roll(first, 64, 1), second),
        )

    areas = jnp.broadcast_to(jnp.concatenate([area[...], area[...]], axis=1), (8, 128))
    for g in range(8):
        for n in range(3):
            even, odd = unpack(ogot, n, g)
            tuv[pl.ds(128 * n + 16 * g, 8, stride=2), :] = even
            tuv[pl.ds(128 * n + 16 * g + 1, 8, stride=2), :] = odd
            if n == 0:
                out[pl.ds(128 * g, 8, stride=16), :] = even
                out[pl.ds(128 * g + 8, 8, stride=16), :] = odd
        for f in range(4):
            even, odd = unpack(igot, f, g)
            out[pl.ds(128 * g + 2 + f, 8, stride=16), :] = even
            out[pl.ds(128 * g + 10 + f, 8, stride=16), :] = odd
    for g in range(16):
        index = wlist[8 * g : 8 * g + 8, :]
        value = jnp.where(index >= 0, take(areas, index & 63, 1), 0.0)
        out[pl.ds(64 * g + 1, 8, stride=8), :] = value
        for f in range(SENT, ROWS):
            out[pl.ds(64 * g + f, 8, stride=8), :] = jnp.zeros((8, 128), f32)

    for fk in range(FK):
        for c in range(2):
            rowlo[fk : fk + 1, c * 128 : (c + 1) * 128] = full[c, fk, 0:1, :]
            rowhi[fk : fk + 1, c * 128 : (c + 1) * 128] = full[c, fk, 127:128, :]


def stencil_row(m, buf, q, canopy, east_col, west_col, drag, lat):
    lane = lanes()
    sub = lax.broadcasted_iota(i32, (8, 128), 0)
    first, last = lane == 0, lane == 127
    rows = pl.ds(pl.multiple_of(8 * m, 8), 8)
    east_halo, west_halo = east_col[rows, :], west_col[rows, :]
    kind = [canopy[rows, c * 128 : (c + 1) * 128] for c in range(2)]
    row = (lat * CJ + 8 * m + sub).astype(f32)
    cor = 4.0 * (2.0 * (row + 0.5) / (CJ * NLAT) - 1.0)
    for c in range(2):
        elim = [None] * NF
        gx = gy = None
        for k in range(K):
            C, E, W, N, S = ([None] * NF for _ in range(5))
            for f in range(NF):
                fk = f * K + k
                mine, other = (buf[d, fk, pl.ds(pl.multiple_of(8 + 8 * m, 8), 8), :] for d in (c, 1 - c))
                C[f] = mine
                N[f] = buf[c, fk, pl.ds(9 + 8 * m, 8), :]
                S[f] = buf[c, fk, pl.ds(7 + 8 * m, 8), :]
                if c == 0:
                    E[f] = pltpu.roll(jnp.where(first, other, mine), 127, 1)
                    W[f] = jnp.where(first, pltpu.roll(west_halo, (1 - fk) % 128, 1), pltpu.roll(mine, 1, 1))
                else:
                    E[f] = jnp.where(last, pltpu.roll(east_halo, (127 - fk) % 128, 1), pltpu.roll(mine, 127, 1))
                    W[f] = pltpu.roll(jnp.where(last, other, mine), 1, 1)
            u, v = C[2], C[3]
            eE = (0.4 - u) - E[2]
            eW = (0.4 + u) + W[2]
            eN = (0.4 - v) - N[3]
            eS = (0.4 + v) + S[3]
            mid = 36.8 + ((eE + eW) + (eN + eS))
            new = [(C[f] * mid + E[f] * eE) + (W[f] * eW + N[f] * eN) + S[f] * eS for f in range(NF)]
            hx = 0.4 * (E[1] - W[1]) - 0.1 * (E[0] - W[0])
            hy = 0.4 * (N[1] - S[1]) - 0.1 * (N[0] - S[0])
            px = hx if k == 0 else gx + hx
            py = hy if k == 0 else gy + hy
            gx, gy = px + hx, py + hy
            new[2] = new[2] + (cor * v - px)
            new[3] = new[3] - (cor * u + py)
            if k > 0:
                x = new[2] * new[2] + (new[3] * new[3] + 0.01 * SCALE * SCALE)
                damp = 1.0 / (1.0 + take(drag[k], kind[c], 0) * (x * lax.rsqrt(x)))
                new[2], new[3] = new[2] * damp, new[3] * damp
            for f in range(NF):
                if k > 1:
                    new[f] = new[f] + FWD[k] * elim[f]
                elim[f] = new[f]
                q[m, f * K + k, c * 8 : (c + 1) * 8, :] = new[f]


def drag_levels(table, drag):
    for k in range(K):
        drag[k] = jnp.broadcast_to(table[:, k : k + 1] * (0.1 / SCALE), (8, 128))


def stencil_kernel(
    st, out, canopy, table, rowlo, rowhi, colw, cole,
    q_any, inb,
    buf, q, drag, mid, north, south, east_col, west_col, sems, hops, halo_send, halo_recv,
):
    lon, lat = lax.axis_index("lon"), lax.axis_index("lat")
    loads = [
        [
            pltpu.make_async_copy(
                st.at[:, 32 * g : 32 * g + 32, c * 128 : (c + 1) * 128],
                buf.at[c, :, 8 + 32 * g : 40 + 32 * g, :],
                sems.at[g, c],
            )
            for c in range(2)
        ]
        for g in range(4)
    ]
    for pair in loads:
        for copy in pair:
            copy.start()

    barrier = pltpu.get_barrier_semaphore()
    for i in range(1, NLON):
        pl.semaphore_signal(barrier, inc=1, device_id=(lax.rem(lon + i, NLON), lat), device_id_type=MESH)
    for i in range(1, NLAT):
        pl.semaphore_signal(barrier, inc=1, device_id=(lon, lax.rem(lat + i, NLAT)), device_id_type=MESH)
    pl.semaphore_wait(barrier, NLON + NLAT - 2)

    def halo(src, dst, n, target):
        return pltpu.make_async_remote_copy(
            src_ref=src, dst_ref=dst, send_sem=halo_send.at[n], recv_sem=halo_recv.at[n],
            device_id=target, device_id_type=MESH,
        )

    to_west = halo(colw, east_col, 0, (lax.rem(lon + NLON - 1, NLON), lat))
    to_east = halo(cole, west_col, 1, (lax.rem(lon + 1, NLON), lat))
    to_north = halo(rowhi, south, 2, (lon, lax.rem(lat + 1, NLAT)))
    to_south = halo(rowlo, north, 3, (lon, lax.rem(lat + NLAT - 1, NLAT)))
    to_fold = halo(rowhi, north, 3, (NLON - 1 - lon, lat))
    to_west.start()
    to_east.start()
    to_north.start()

    @pl.when(lat > 0)
    def _():
        to_south.start()

    @pl.when(lat == NLAT - 1)
    def _():
        pltpu.make_async_remote_copy(
            src_ref=rowhi, dst_ref=north, send_sem=halo_send.at[4], recv_sem=halo_recv.at[3],
            device_id=(NLON - 1 - lon, lat), device_id_type=MESH,
        ).start()

    for i in range(1, NLON):
        peer = lax.rem(lon + i, NLON)
        pltpu.make_async_remote_copy(
            src_ref=out.at[pl.ds(peer * NLAT, NLAT)], dst_ref=mid.at[pl.ds(lon * NLAT, NLAT)],
            send_sem=hops.at[0], recv_sem=hops.at[1], device_id=(peer, lat), device_id_type=MESH,
        ).start()
    own = pltpu.make_async_copy(out.at[pl.ds(lon * NLAT, NLAT)], mid.at[pl.ds(lon * NLAT, NLAT)], hops.at[2])
    own.start()

    drag_levels(table, drag)
    to_west.wait_recv()
    to_east.wait_recv()
    to_north.wait_recv()
    to_fold.wait_recv()
    top = lat == NLAT - 1
    inside = jnp.where(lat > 0, 1.0, 0.0)
    back = 127 - lanes()
    for g in range(10):
        part = slice(8 * g, 8 * g + 8)
        sign = 1.0 if g < 5 else -1.0
        halves = [north[part, c * 128 : (c + 1) * 128] for c in range(2)]
        for c in range(2):
            turned = sign * take(halves[1 - c], back, 1)
            value = jnp.where(top, turned, halves[c])
            below = south[part, c * 128 : (c + 1) * 128] * inside
            for r in range(8):
                buf[c, 8 * g + r, 136:137, :] = value[r : r + 1]
                buf[c, 8 * g + r, 7:8, :] = below[r : r + 1]
    for copy in loads[0]:
        copy.wait()

    @pl.loop(0, 4)
    def _(g):
        @pl.when(g < 3)
        def _():
            for c in range(2):
                pltpu.make_async_copy(
                    st.at[:, 0:32, 0:128], buf.at[c, :, 8:40, :], sems.at[g + 1, c]
                ).wait()

        @pl.when(g == 2)
        def _():
            many = mid.at[0 : (NLON - 1) * NLAT]
            pltpu.make_async_copy(many, many, hops.at[1]).wait()
            own.wait()
            mid4 = mid.reshape(NLON, NLAT, ROWS, 128)
            in4 = inb.reshape(NLON, NLAT, ROWS, 128)
            for i in range(1, NLAT):
                peer = lax.rem(lat + i, NLAT)
                pltpu.make_async_remote_copy(
                    src_ref=mid4.at[:, peer], dst_ref=in4.at[:, lat],
                    send_sem=hops.at[3], recv_sem=hops.at[4], device_id=(lon, peer), device_id_type=MESH,
                ).start()
            pltpu.make_async_copy(mid4.at[:, lat], in4.at[:, lat], hops.at[2]).start()

        @pl.loop(0, 4)
        def _(j):
            m = 4 * g + j
            stencil_row(m, buf, q, canopy, east_col, west_col, drag, lat)
            pltpu.make_async_copy(q.at[m], q_any.at[m], hops.at[5]).start()

    pltpu.make_async_copy(q, q_any, hops.at[5]).wait()
    some = inb.at[0 : (NLAT - 1) * NLON]
    pltpu.make_async_copy(some, some, hops.at[4]).wait()
    pltpu.make_async_copy(some, some, hops.at[3]).wait()
    one = inb.at[0:NLON]
    pltpu.make_async_copy(one, one, hops.at[2]).wait()
    many = mid.at[0 : (NLON - 1) * NLAT]
    pltpu.make_async_copy(many, many, hops.at[0]).wait()
    to_west.wait_send()
    to_east.wait_send()
    to_north.wait_send()

    @pl.when(lat > 0)
    def _():
        to_south.wait_send()

    @pl.when(lat == NLAT - 1)
    def _():
        pltpu.make_async_copy(rowhi, rowhi, halo_send.at[4]).wait()


def finish_kernel(
    st, olist_any, ilist_any, q_any, inb, out, tuv, olist, ilist, canopy, table, itemp,
    y, itemp_next,
    q, ybuf, salt, drag, opack, ipack, oval, ival, oacc, iacc, owide, ocols, iwide, icols, oflag, iflag, sems,
):
    flags = [
        pltpu.make_async_copy(olist_any, oflag, sems.at[0]),
        pltpu.make_async_copy(ilist_any, iflag, sems.at[1]),
    ]
    salts = [
        pltpu.make_async_copy(st.at[K, :, c * 128 : (c + 1) * 128], salt.at[c], sems.at[2 + c])
        for c in range(2)
    ]
    state = pltpu.make_async_copy(q_any, q, sems.at[6])
    for copy in flags + salts + [state]:
        copy.start()
    drag_levels(table, drag)
    pack_list(olist, opack)
    pack_list(ilist, ipack)
    for g in range(8):
        sides, ices = [], []
        for odd in range(2):
            block = lambda ref, f: ref[pl.ds(128 * g + 8 * odd + f, 8, stride=16), :]
            slot = [tuv[pl.ds(128 * n + 16 * g + odd, 8, stride=2), :] for n in range(3)]
            a, cond, temp, iu, iv = (block(inb, f) for f in range(1, 6))
            du, dv = iu - slot[1], iv - slot[2]
            x = du * du + dv * dv + 0.01
            drift = 0.5 * a * (x * lax.rsqrt(x))
            heat = a * cond
            sides.append([heat * (temp - slot[0]), heat, drift * du, drift * dv])
            ices.append(block(out, 1) * block(out, 2) * (block(out, 3) - block(inb, 0)))
        for f in range(4):
            first, second = pack(sides[0][f], sides[1][f])
            oval[128 * f + 8 * g : 128 * f + 8 * g + 8, :] = first
            oval[128 * f + 64 + 8 * g : 128 * f + 72 + 8 * g, :] = second
        first, second = pack(*ices)
        ival[8 * g : 8 * g + 8, :] = first
        ival[64 + 8 * g : 72 + 8 * g, :] = second
    oacc[...] = jnp.zeros_like(oacc)
    iacc[...] = jnp.zeros_like(iacc)

    def hot_columns(tile, packed, width, cols):
        for h in range(4):
            index = packed[pl.ds(4 * tile + h, 1), :] & (width - 1)
            cols[:, 128 * h : 128 * h + 128] = jnp.where(one_hot(index, width), 1.0, 0.0).astype(bf16)

    def add(wide, cols, acc):
        acc[...] += lax.dot_general(wide, cols, (((1,), (1,)), ((), ())), preferred_element_type=f32)

    def scatter_ocean(tile):
        hot_columns(tile, opack, CI, ocols)
        for h in range(4):
            mask = one_hot(opack[pl.ds(4 * tile + h, 1), :] >> 8, CJ)
            for f in range(4):
                value = oval[pl.ds(128 * f + 4 * tile + h, 1), :]
                high = value.astype(bf16).astype(f32)
                for n, part in enumerate((high, value - high)):
                    part = jnp.where(mask, jnp.broadcast_to(part, (CJ, 128)), 0.0).astype(bf16)
                    owide[CJ * f : CJ * (f + 1), 512 * n + 128 * h : 512 * n + 128 * h + 128] = part
        hot = ocols[...]
        add(owide[...], jnp.concatenate([hot, hot], axis=1), oacc)

    def scatter_ice(tile):
        hot_columns(tile, ipack, 128, icols)
        for h in range(4):
            mask = one_hot(ipack[pl.ds(4 * tile + h, 1), :] >> 7, 64)
            value = ival[pl.ds(4 * tile + h, 1), :]
            high = value.astype(bf16).astype(f32)
            for n, part in enumerate((high, value - high)):
                part = jnp.where(mask, jnp.broadcast_to(part, (64, 128)), 0.0).astype(bf16)
                iwide[64 * n : 64 * n + 64, 128 * h : 128 * h + 128] = part
        add(iwide[...], icols[...], iacc)

    @pl.loop(0, 16)
    def _(t):
        scatter_ocean(t)
        scatter_ice(t)

    for copy in flags:
        copy.wait()

    @pl.loop(0, 16)
    def _(t):
        @pl.when(long_pairs(oflag, 8 * t, 8))
        def _():
            scatter_ocean(16 + t)

        @pl.when(long_pairs(iflag, 8 * t, 8))
        def _():
            scatter_ice(16 + t)

    itemp_next[...] = itemp[...] - 0.25 * (iacc[0:64, :] + iacc[64:128, :])
    for copy in salts + [state]:
        copy.wait()

    @pl.loop(0, 16)
    def _(m):
        rows = pl.ds(pl.multiple_of(8 * m, 8), 8)
        sides = []
        for c in range(2):
            here = slice(8 * c, 8 * c + 8)
            flux = [
                oacc[pl.ds(pl.multiple_of(CJ * f + 8 * m, 8), 8), c * 128 : (c + 1) * 128] for f in range(4)
            ]
            top = [q[m, f * K, here, :] for f in range(4)]
            top[0] = top[0] + 20.0 * flux[0]
            top[1] = top[1] - 10.0 * (salt[c, rows, :] * flux[1])
            top[2] = top[2] + 20.0 * flux[2]
            top[3] = top[3] + 20.0 * flux[3]
            x = top[2] * top[2] + (top[3] * top[3] + 0.01 * SCALE * SCALE)
            damp = 1.0 / (1.0 + take(drag[0], canopy[rows, c * 128 : (c + 1) * 128], 0) * (x * lax.rsqrt(x)))
            top[2], top[3] = top[2] * damp, top[3] * damp
            sides.append(top)
        solved = [[None] * 4 for _ in range(2)]
        for k in range(K - 1, -1, -1):
            for c in range(2):
                for f in range(4):
                    here = slice(8 * c, 8 * c + 8)
                    value = sides[c][f] if k == 0 else q[m, f * K + k, here, :] + TOP[k] * sides[c][f]
                    value = value * (1.0 / (SCALE * DIAG[k]))
                    if k < K - 1:
                        value = value + (0.5 / DIAG[k]) * solved[c][f]
                    solved[c][f] = value
                    ybuf[m, f * K + k, here, :] = value
        for c in range(2):
            pltpu.make_async_copy(
                ybuf.at[m, :, 8 * c : 8 * c + 8, :], y.at[:, rows, c * 128 : (c + 1) * 128], sems.at[4 + c]
            ).start()

    for c in range(2):
        part = y.at[:, :, c * 128 : (c + 1) * 128]
        pltpu.make_async_copy(part, part, sems.at[4 + c]).wait()


def shards(
    ocean_state, canopy_type, drag_table, ocean_list, ice_list, weight_list, area_table, ice_temp, ice_cond, ice_vel
):
    st = ocean_state.reshape(FK, CJ, CI)
    olist, ilist, wlist = (x.reshape(DEV, SLOTS) for x in (ocean_list, ice_list, weight_list))
    itemp, icond = (x.reshape(64, 128) for x in (ice_temp, ice_cond))
    ivel = ice_vel.reshape(2, 64, 128).transpose(1, 0, 2).reshape(128, 128)
    area = area_table.reshape(1, 64)
    S = jax.ShapeDtypeStruct
    V = pltpu.VMEM
    out, tuv, rowlo, rowhi, colw, cole = pl.pallas_call(
        gather_kernel,
        out_shape=(
            S((DEV * ROWS, 128), f32), S((3 * 128, 128), f32), S((FK, CI), f32), S((FK, CI), f32),
            S((CJ, 128), f32), S((CJ, 128), f32),
        ),
        in_specs=[ANY] * 3 + [VM] * 7,
        out_specs=(VM,) * 6,
        scratch_shapes=[
            V((2, FK, CJ, 128), f32), V((3, 2, CJ, 128), f32), V((768, 256), bf16), V((256, 256), bf16),
            V((128, 128), i32), V((128, 128), i32), V((3 * 128, 128), f32), V((4 * 128, 128), f32),
            pltpu.SMEM((128, 128), i32), pltpu.SMEM((128, 128), i32), pltpu.SemaphoreType.DMA((5,)),
        ],
        compiler_params=pltpu.CompilerParams(vmem_limit_bytes=LIMIT),
        name="gather_slots",
    )(st, olist, ilist, olist, ilist, wlist, area, itemp, icond, ivel)
    out3 = out.reshape(DEV, ROWS, 128)
    q, inb = pl.pallas_call(
        stencil_kernel,
        out_shape=(S((16, FK, 16, 128), f32), S((DEV, ROWS, 128), f32)),
        in_specs=[ANY, ANY, VM, VM] + [ANY] * 4,
        out_specs=(ANY, ANY),
        scratch_shapes=[
            V((2, FK, 144, 128), f32), V((16, FK, 16, 128), f32), V((K, 8, 128), f32), V((DEV, ROWS, 128), f32),
            V((FK, CI), f32), V((FK, CI), f32), V((CJ, 128), f32), V((CJ, 128), f32),
            pltpu.SemaphoreType.DMA((4, 2)), pltpu.SemaphoreType.DMA((6,)),
            pltpu.SemaphoreType.DMA((5,)), pltpu.SemaphoreType.DMA((4,)),
        ],
        compiler_params=pltpu.CompilerParams(vmem_limit_bytes=LIMIT, collective_id=0, has_side_effects=True),
        name="exchange_stencil",
    )(st, out3, canopy_type, drag_table, rowlo, rowhi, colw, cole)
    y, itemp_next = pl.pallas_call(
        finish_kernel,
        out_shape=(S((FK, CJ, CI), f32), S((64, 128), f32)),
        in_specs=[ANY] * 4 + [VM] * 8,
        out_specs=(ANY, VM),
        scratch_shapes=[
            V((16, FK, 16, 128), f32), V((16, FK, 16, 128), f32), V((2, CJ, 128), f32), V((K, 8, 128), f32),
            V((128, 128), i32), V((128, 128), i32), V((4 * 128, 128), f32), V((128, 128), f32),
            V((4 * CJ, CI), f32), V((128, 128), f32), V((4 * CJ, 1024), bf16), V((CI, 512), bf16),
            V((128, 512), bf16), V((128, 512), bf16),
            pltpu.SMEM((128, 128), i32), pltpu.SMEM((128, 128), i32), pltpu.SemaphoreType.DMA((7,)),
        ],
        compiler_params=pltpu.CompilerParams(vmem_limit_bytes=LIMIT),
        name="scatter_solve",
    )(st, olist, ilist, q, inb.reshape(DEV * ROWS, 128), out, tuv, olist, ilist, canopy_type, drag_table, itemp)
    return y.reshape(ocean_state.shape), itemp_next.reshape(ice_temp.shape)


def solution(mesh):
    return jax.shard_map(
        shards,
        mesh=mesh,
        in_specs=(
            P(None, None, "lat", "lon"),
            P("lat", "lon"),
            P(),
            P(("lon", "lat"), None),
            P(("lon", "lat"), None),
            P(("lon", "lat"), None),
            P(),
            P(("lon", "lat"), None),
            P(("lon", "lat"), None),
            P(("lon", "lat"), None, None),
        ),
        out_specs=(P(None, None, "lat", "lon"), P(("lon", "lat"), None)),
        check_vma=False,
    )
```

```python
import functools

import jax
import jax.numpy as jnp
from jax import lax
from jax.experimental import pallas as pl
from jax.experimental.pallas import tpu as pltpu
from jax.sharding import PartitionSpec as P

f32 = jnp.float32
bf16 = jnp.bfloat16
i32 = jnp.int32
MESH = pl.DeviceIdType.MESH
K = 20
NF = 4
FK = NF * K
CJ = 128
CI = 256
NLON = 16
NLAT = 8
DEV = NLON * NLAT
SLOTS = 128
ROWS = 8
SENT = 6
SCALE = 40.0

DIAG = [1.5]
for _k in range(1, K):
    DIAG.append((1.5 if _k == K - 1 else 2.0) - 0.25 / DIAG[-1])
FWD = [0.0] + [0.5 / DIAG[_k - 1] for _k in range(1, K)]
TOP = [1.0]
for _k in range(1, K):
    TOP.append(FWD[_k] * TOP[-1])

VM = pl.BlockSpec(memory_space=pltpu.VMEM)
ANY = pl.BlockSpec(memory_space=pl.ANY)
LIMIT = 60 << 20


def lanes():
    return lax.broadcasted_iota(i32, (8, 128), 1)


def take(table, index, axis):
    return jnp.take_along_axis(table, index, axis=axis, mode="promise_in_bounds")


def split(x):
    high = x.astype(bf16)
    return high, (x - high.astype(f32)).astype(bf16)


def one_hot(index, count):
    rows = lax.broadcasted_iota(i32, (count, index.shape[1]), 0)
    return rows == jnp.broadcast_to(index, (count, index.shape[1]))


def pack(even, odd):
    left = lanes() < 64
    return (
        jnp.where(left, even, pltpu.roll(odd, 64, 1)),
        jnp.where(left, pltpu.roll(even, 64, 1), odd),
    )


def pack_list(source, packed):
    for g in range(8):
        first, second = pack(
            source[pl.ds(16 * g, 8, stride=2), :], source[pl.ds(16 * g + 1, 8, stride=2), :]
        )
        packed[8 * g : 8 * g + 8, :] = first
        packed[64 + 8 * g : 72 + 8 * g, :] = second


def long_pairs(flags, first, count):
    most = flags[first, 64]
    for i in range(1, count):
        most = jnp.maximum(most, flags[first + i, 64])
    return most >= 0


def gather(tile, packed, table, fields, rows, got):
    hots, his = [], []
    for h in range(2):
        row = packed[pl.ds(2 * tile + h, 1), :]
        his.append(row >> 8)
        hots.append(jnp.where(one_hot(row & 255, 256), 1.0, 0.0).astype(bf16))
    res = jnp.dot(table[...], jnp.concatenate(hots, axis=1), preferred_element_type=f32)
    half = fields * rows
    res = res[:half] + res[half:]
    for h in range(2):
        mask = one_hot(his[h], rows)
        for f in range(fields):
            value = jnp.where(mask, res[f * rows : (f + 1) * rows, h * 128 : (h + 1) * 128], 0.0)
            got[pl.ds(f * 128 + 2 * tile + h, 1), :] = jnp.sum(value, axis=0, keepdims=True)


def unpack(got, f, g):
    left = lanes() < 64
    first = got[f * 128 + 8 * g : f * 128 + 8 * g + 8, :]
    second = got[f * 128 + 64 + 8 * g : f * 128 + 72 + 8 * g, :]
    return (
        jnp.where(left, first, pltpu.roll(second, 64, 1)),
        jnp.where(left, pltpu.roll(first, 64, 1), second),
    )


def gather_kernel(
    st, olist_any, olist,
    tuv, rowlo, rowhi, colw, cole,
    full, surf, otab, opack, ogot, oflag, sems,
):
    flags = pltpu.make_async_copy(olist_any, oflag, sems.at[0])
    tops = [
        pltpu.make_async_copy(st.at[f * K, :, c * 128 : (c + 1) * 128], surf.at[n, c], sems.at[1])
        for n, f in enumerate((0, 2, 3))
        for c in range(2)
    ]
    state = [
        pltpu.make_async_copy(st.at[:, :, c * 128 : (c + 1) * 128], full.at[c], sems.at[2 + c]) for c in range(2)
    ]
    for copy in tops + [flags] + state:
        copy.start()
    pack_list(olist, opack)
    ogot[...] = jnp.zeros_like(ogot)
    pltpu.make_async_copy(surf, surf, sems.at[1]).wait()
    for n in range(3):
        for c in range(2):
            high, low = split(surf[n, c])
            otab[128 * n : 128 * n + 128, c * 128 : (c + 1) * 128] = high
            otab[384 + 128 * n : 512 + 128 * n, c * 128 : (c + 1) * 128] = low

    def columns(m):
        lane = lanes()
        rows = pl.ds(pl.multiple_of(8 * m, 8), 8)
        west = jnp.zeros((8, 128), f32)
        east = jnp.zeros((8, 128), f32)
        for fk in range(FK):
            both = jnp.where(lane == 127, full[1, fk, rows, :], full[0, fk, rows, :])
            both = pltpu.roll(both, fk, 1) if fk else both
            west = jnp.where(lane == fk, both, west)
            east = jnp.where(lane == (fk - 1) % 128, both, east)
        colw[rows, :] = west
        cole[rows, :] = east

    @pl.loop(0, 4)
    def _(t):
        for j in range(4):
            gather(4 * t + j, opack, otab, 3, 128, ogot)

    for copy in state:
        copy.wait()

    @pl.loop(4, 8)
    def _(t):
        for j in range(4):
            gather(4 * t + j, opack, otab, 3, 128, ogot)
        for j in range(4):
            columns(4 * (t - 4) + j)

    flags.wait()

    @pl.loop(0, 32)
    def _(t):
        @pl.when(long_pairs(oflag, 4 * t, 4))
        def _():
            gather(32 + t, opack, otab, 3, 128, ogot)

    for g in range(8):
        for n in range(3):
            even, odd = unpack(ogot, n, g)
            tuv[pl.ds(128 * n + 16 * g, 8, stride=2), :] = even
            tuv[pl.ds(128 * n + 16 * g + 1, 8, stride=2), :] = odd
    for fk in range(FK):
        for c in range(2):
            rowlo[fk : fk + 1, c * 128 : (c + 1) * 128] = full[c, fk, 0:1, :]
            rowhi[fk : fk + 1, c * 128 : (c + 1) * 128] = full[c, fk, 127:128, :]


def stencil_row(m, buf, q, canopy, east_col, west_col, drag, lat):
    lane = lanes()
    sub = lax.broadcasted_iota(i32, (8, 128), 0)
    first, last = lane == 0, lane == 127
    rows = pl.ds(pl.multiple_of(8 * m, 8), 8)
    east_halo, west_halo = east_col[rows, :], west_col[rows, :]
    kind = [canopy[rows, c * 128 : (c + 1) * 128] for c in range(2)]
    row = (lat * CJ + 8 * m + sub).astype(f32)
    cor = 4.0 * (2.0 * (row + 0.5) / (CJ * NLAT) - 1.0)
    for c in range(2):
        elim = [None] * NF
        gx = gy = None
        for k in range(K):
            C, E, W, N, S = ([None] * NF for _ in range(5))
            for f in range(NF):
                fk = f * K + k
                mine, other = (buf[d, fk, pl.ds(pl.multiple_of(8 + 8 * m, 8), 8), :] for d in (c, 1 - c))
                C[f] = mine
                N[f] = buf[c, fk, pl.ds(9 + 8 * m, 8), :]
                S[f] = buf[c, fk, pl.ds(7 + 8 * m, 8), :]
                if c == 0:
                    E[f] = pltpu.roll(jnp.where(first, other, mine), 127, 1)
                    W[f] = jnp.where(first, pltpu.roll(west_halo, (1 - fk) % 128, 1), pltpu.roll(mine, 1, 1))
                else:
                    E[f] = jnp.where(last, pltpu.roll(east_halo, (127 - fk) % 128, 1), pltpu.roll(mine, 127, 1))
                    W[f] = pltpu.roll(jnp.where(last, other, mine), 1, 1)
            u, v = C[2], C[3]
            eE = (0.4 - u) - E[2]
            eW = (0.4 + u) + W[2]
            eN = (0.4 - v) - N[3]
            eS = (0.4 + v) + S[3]
            mid = 36.8 + ((eE + eW) + (eN + eS))
            new = [(C[f] * mid + E[f] * eE) + (W[f] * eW + N[f] * eN) + S[f] * eS for f in range(NF)]
            hx = 0.4 * (E[1] - W[1]) - 0.1 * (E[0] - W[0])
            hy = 0.4 * (N[1] - S[1]) - 0.1 * (N[0] - S[0])
            px = hx if k == 0 else gx + hx
            py = hy if k == 0 else gy + hy
            gx, gy = px + hx, py + hy
            new[2] = new[2] + (cor * v - px)
            new[3] = new[3] - (cor * u + py)
            if k > 0:
                x = new[2] * new[2] + (new[3] * new[3] + 0.01 * SCALE * SCALE)
                damp = 1.0 / (1.0 + take(drag[k], kind[c], 0) * (x * lax.rsqrt(x)))
                new[2], new[3] = new[2] * damp, new[3] * damp
            for f in range(NF):
                if k > 1:
                    new[f] = new[f] + FWD[k] * elim[f]
                elim[f] = new[f]
                q[m, f * K + k, c * 8 : (c + 1) * 8, :] = new[f]


def drag_levels(table, drag):
    for k in range(K):
        drag[k] = jnp.broadcast_to(table[:, k : k + 1] * (0.1 / SCALE), (8, 128))


def ice_messages(ilist, wlist, area, itemp, icond, ivel, msg, itab, ipack, igot):
    @pl.loop(0, 64, step=4)
    def _(t):
        for j in range(4):
            gather(t + j, ipack, itab, 4, 32, igot)

    areas = jnp.broadcast_to(jnp.concatenate([area[...], area[...]], axis=1), (8, 128))
    for g in range(8):
        for f in range(4):
            even, odd = unpack(igot, f, g)
            msg[pl.ds(128 * g + 2 + f, 8, stride=16), :] = even
            msg[pl.ds(128 * g + 10 + f, 8, stride=16), :] = odd
    for g in range(16):
        index = wlist[8 * g : 8 * g + 8, :]
        value = jnp.where(index >= 0, take(areas, index & 63, 1), 0.0)
        msg[pl.ds(64 * g + 1, 8, stride=8), :] = value
        for f in range(SENT, ROWS):
            msg[pl.ds(64 * g + f, 8, stride=8), :] = jnp.zeros((8, 128), f32)


def stencil_kernel(
    st, tuv, ilist, wlist, area, itemp, icond, ivel, canopy, table, rowlo, rowhi, colw, cole,
    q_any, inb, out,
    buf, q, drag, msg, temps, itab, ipack, igot, mid_a, mid_b, north, south, east_col, west_col, sems, hops, halo_send, halo_recv,
):
    lon, lat = lax.axis_index("lon"), lax.axis_index("lat")
    loads = [
        [
            pltpu.make_async_copy(
                st.at[:, 32 * g : 32 * g + 32, c * 128 : (c + 1) * 128],
                buf.at[c, :, 8 + 32 * g : 40 + 32 * g, :],
                sems.at[g, c],
            )
            for c in range(2)
        ]
        for g in range(4)
    ]
    for pair in loads:
        for copy in pair:
            copy.start()

    surface = pltpu.make_async_copy(tuv.at[0:128], temps, hops.at[13])
    surface.start()
    barrier = pltpu.get_barrier_semaphore()
    for i in range(1, NLON):
        pl.semaphore_signal(barrier, inc=1, device_id=(lax.rem(lon + i, NLON), lat), device_id_type=MESH)
    for i in range(1, NLAT):
        pl.semaphore_signal(barrier, inc=1, device_id=(lon, lax.rem(lat + i, NLAT)), device_id_type=MESH)
    pack_list(ilist, ipack)
    for f in range(4):
        for c in range(2):
            if f < 2:
                x = (icond, itemp)[f][pl.ds(c, 32, stride=2), :]
            else:
                x = ivel[pl.ds(2 * c + f - 2, 32, stride=4), :]
            high, low = split(x)
            itab[32 * f : 32 * f + 32, c * 128 : (c + 1) * 128] = high
            itab[128 + 32 * f : 160 + 32 * f, c * 128 : (c + 1) * 128] = low
    pl.semaphore_wait(barrier, NLON + NLAT - 2)

    def halo(src, dst, n, target):
        return pltpu.make_async_remote_copy(
            src_ref=src, dst_ref=dst, send_sem=halo_send.at[n], recv_sem=halo_recv.at[n],
            device_id=target, device_id_type=MESH,
        )

    to_west = halo(colw, east_col, 0, (lax.rem(lon + NLON - 1, NLON), lat))
    to_east = halo(cole, west_col, 1, (lax.rem(lon + 1, NLON), lat))
    to_north = halo(rowhi, south, 2, (lon, lax.rem(lat + 1, NLAT)))
    to_south = halo(rowlo, north, 3, (lon, lax.rem(lat + NLAT - 1, NLAT)))
    to_fold = halo(rowhi, north, 3, (NLON - 1 - lon, lat))
    to_west.start()
    to_east.start()
    to_north.start()

    @pl.when(lat > 0)
    def _():
        to_south.start()

    @pl.when(lat == NLAT - 1)
    def _():
        pltpu.make_async_remote_copy(
            src_ref=rowhi, dst_ref=north, send_sem=halo_send.at[4], recv_sem=halo_recv.at[3],
            device_id=(NLON - 1 - lon, lat), device_id_type=MESH,
        ).start()

    def hop(src, dst, n, target):
        return pltpu.make_async_remote_copy(
            src_ref=src, dst_ref=dst, send_sem=hops.at[n], recv_sem=hops.at[n + 1],
            device_id=target, device_id_type=MESH,
        )

    ice_messages(ilist, wlist, area, itemp, icond, ivel, msg, itab, ipack, igot)
    surface.wait()
    for g in range(16):
        msg[pl.ds(64 * g, 8, stride=8), :] = temps[8 * g : 8 * g + 8, :]
    keep = pltpu.make_async_copy(msg, out, hops.at[12])
    keep.start()
    even = lax.rem(lon + lat, 2) == 0
    by_a = msg.reshape(NLON, NLAT // 2, 2, ROWS, 128)
    by_b = msg.reshape(NLON // 2, 2, NLAT, ROWS, 128)

    def first_a(peer):
        return by_a.at[peer, :, lax.rem(peer, 2), 0:SENT], mid_a.at[lon, :, 0:SENT]

    def first_b(peer):
        return by_b.at[:, 1 - lax.rem(peer, 2), peer, 0:SENT], mid_b.at[lat, :, 0:SENT]

    for i in range(1, NLON):
        peer = lax.rem(lon + i, NLON)
        hop(*first_a(peer), 0, (peer, lat)).start()
    for i in range(1, NLAT):
        peer = lax.rem(lat + i, NLAT)
        hop(*first_b(peer), 2, (lon, peer)).start()
    own_a = pltpu.make_async_copy(*first_a(lon), hops.at[8])
    own_b = pltpu.make_async_copy(*first_b(lat), hops.at[9])
    own_a.start()
    own_b.start()
    in4 = inb.reshape(NLON, NLAT, ROWS, 128)

    def second_a(peer):
        return mid_a.at[:, peer // 2, 0:SENT], in4.at[:, lat, 0:SENT]

    def second_b(peer):
        return mid_b.at[:, peer // 2, 0:SENT], in4.at[lon, :, 0:SENT]

    def blocks(ref, n):
        part = ref.at[0:n, 0:SENT]
        return part, part

    def taken(n, sem):
        pltpu.make_async_copy(*blocks(inb, n), hops.at[sem]).wait()

    drag_levels(table, drag)
    to_west.wait_recv()
    to_east.wait_recv()
    to_north.wait_recv()
    to_fold.wait_recv()
    top = lat == NLAT - 1
    inside = jnp.where(lat > 0, 1.0, 0.0)
    back = 127 - lanes()
    for g in range(10):
        part = slice(8 * g, 8 * g + 8)
        sign = 1.0 if g < 5 else -1.0
        halves = [north[part, c * 128 : (c + 1) * 128] for c in range(2)]
        for c in range(2):
            turned = sign * take(halves[1 - c], back, 1)
            value = jnp.where(top, turned, halves[c])
            below = south[part, c * 128 : (c + 1) * 128] * inside
            for r in range(8):
                buf[c, 8 * g + r, 136:137, :] = value[r : r + 1]
                buf[c, 8 * g + r, 7:8, :] = below[r : r + 1]
    for copy in loads[0]:
        copy.wait()

    @pl.loop(0, 8)
    def _(g):
        @pl.when(lax.rem(g, 2) - jnp.where(g > 5, 1, 0) == 1)
        def _():
            for c in range(2):
                pltpu.make_async_copy(
                    st.at[:, 0:32, 0:128], buf.at[c, :, 8:40, :], sems.at[g // 2 + 1, c]
                ).wait()

        @pl.when(g == 3)
        def _():
            taken((NLON - 1) * NLAT // 2, 1)
            taken((NLAT - 1) * NLON // 2, 3)
            own_a.wait()
            own_b.wait()

            @pl.when(even)
            def _():
                pltpu.make_async_copy(*second_a(lat), hops.at[10]).start()
                for i in range(2, NLAT, 2):
                    peer = lax.rem(lat + i, NLAT)
                    hop(*second_a(peer), 4, (lon, peer)).start()
                for i in range(1, NLON, 2):
                    peer = lax.rem(lon + i, NLON)
                    hop(*second_b(peer), 6, (peer, lat)).start()

            @pl.when(jnp.logical_not(even))
            def _():
                pltpu.make_async_copy(*second_b(lon), hops.at[11]).start()
                for i in range(1, NLAT, 2):
                    peer = lax.rem(lat + i, NLAT)
                    hop(*second_a(peer), 4, (lon, peer)).start()
                for i in range(2, NLON, 2):
                    peer = lax.rem(lon + i, NLON)
                    hop(*second_b(peer), 6, (peer, lat)).start()

        @pl.loop(0, 2)
        def _(j):
            m = 2 * g + j
            stencil_row(m, buf, q, canopy, east_col, west_col, drag, lat)
            pltpu.make_async_copy(q.at[m], q_any.at[m], hops.at[14]).start()

    pltpu.make_async_copy(q, q_any, hops.at[14]).wait()
    keep.wait()
    @pl.when(even)
    def _():
        taken((NLAT - 1) * NLON, 5)
        taken(NLON, 10)
        taken((NLAT // 2 - 1) * NLON, 4)
        taken((NLON // 2) * NLAT, 6)

    @pl.when(jnp.logical_not(even))
    def _():
        taken((NLON - 1) * NLAT, 7)
        taken(NLAT, 11)
        taken((NLAT // 2) * NLON, 4)
        taken((NLON // 2 - 1) * NLAT, 6)

    taken((NLON - 1) * NLAT // 2, 0)
    taken((NLAT - 1) * NLON // 2, 2)
    to_west.wait_send()
    to_east.wait_send()
    to_north.wait_send()

    @pl.when(lat > 0)
    def _():
        to_south.wait_send()

    @pl.when(lat == NLAT - 1)
    def _():
        pltpu.make_async_copy(rowhi, rowhi, halo_send.at[4]).wait()


def finish_kernel(
    st, olist_any, ilist_any, q_any, inb, out, tuv, olist, ilist, canopy, table, itemp,
    y, itemp_next,
    q, ybuf, salt, drag, opack, ipack, oval, ival, oacc, iacc, owide, ocols, iwide, icols, oflag, iflag, sems,
):
    flags = [
        pltpu.make_async_copy(olist_any, oflag, sems.at[0]),
        pltpu.make_async_copy(ilist_any, iflag, sems.at[1]),
    ]
    salts = [
        pltpu.make_async_copy(st.at[K, :, c * 128 : (c + 1) * 128], salt.at[c], sems.at[2 + c])
        for c in range(2)
    ]
    state = pltpu.make_async_copy(q_any, q, sems.at[6])
    for copy in flags + salts + [state]:
        copy.start()
    drag_levels(table, drag)
    pack_list(olist, opack)
    pack_list(ilist, ipack)
    for g in range(8):
        sides, ices = [], []
        for odd in range(2):
            block = lambda ref, f: ref[pl.ds(128 * g + 8 * odd + f, 8, stride=16), :]
            slot = [tuv[pl.ds(128 * n + 16 * g + odd, 8, stride=2), :] for n in range(3)]
            a, cond, temp, iu, iv = (block(inb, f) for f in range(1, 6))
            du, dv = iu - slot[1], iv - slot[2]
            x = du * du + dv * dv + 0.01
            drift = 0.5 * a * (x * lax.rsqrt(x))
            heat = a * cond
            sides.append([heat * (temp - slot[0]), heat, drift * du, drift * dv])
            ices.append(block(out, 1) * block(out, 2) * (block(out, 3) - block(inb, 0)))
        for f in range(4):
            first, second = pack(sides[0][f], sides[1][f])
            oval[128 * f + 8 * g : 128 * f + 8 * g + 8, :] = first
            oval[128 * f + 64 + 8 * g : 128 * f + 72 + 8 * g, :] = second
        first, second = pack(*ices)
        ival[8 * g : 8 * g + 8, :] = first
        ival[64 + 8 * g : 72 + 8 * g, :] = second
    oacc[...] = jnp.zeros_like(oacc)
    iacc[...] = jnp.zeros_like(iacc)

    def hot_columns(tile, packed, width, cols):
        for h in range(4):
            index = packed[pl.ds(4 * tile + h, 1), :] & (width - 1)
            cols[:, 128 * h : 128 * h + 128] = jnp.where(one_hot(index, width), 1.0, 0.0).astype(bf16)

    def add(wide, cols, acc):
        acc[...] += lax.dot_general(wide, cols, (((1,), (1,)), ((), ())), preferred_element_type=f32)

    def scatter_ocean(tile, p=0):
        hot_columns(tile, opack, CI, ocols.at[p])
        for h in range(4):
            mask = one_hot(opack[pl.ds(4 * tile + h, 1), :] >> 8, CJ)
            for f in range(4):
                value = oval[pl.ds(128 * f + 4 * tile + h, 1), :]
                high = value.astype(bf16).astype(f32)
                for n, part in enumerate((high, value - high)):
                    part = jnp.where(mask, jnp.broadcast_to(part, (CJ, 128)), 0.0).astype(bf16)
                    owide[p, 512 * n + CJ * f : 512 * n + CJ * (f + 1), 128 * h : 128 * h + 128] = part
        add(owide[p], ocols[p], oacc)

    def scatter_ice(tile):
        hot_columns(tile, ipack, 128, icols)
        for h in range(4):
            mask = one_hot(ipack[pl.ds(4 * tile + h, 1), :] >> 7, 64)
            value = ival[pl.ds(4 * tile + h, 1), :]
            high = value.astype(bf16).astype(f32)
            for n, part in enumerate((high, value - high)):
                part = jnp.where(mask, jnp.broadcast_to(part, (64, 128)), 0.0).astype(bf16)
                iwide[64 * n : 64 * n + 64, 128 * h : 128 * h + 128] = part
        add(iwide[...], icols[...], iacc)

    @pl.loop(0, 16, step=2)
    def _(t):
        scatter_ocean(t)
        scatter_ocean(t + 1, 1)
        scatter_ice(t)
        scatter_ice(t + 1)

    for copy in flags:
        copy.wait()

    @pl.loop(0, 16)
    def _(t):
        @pl.when(long_pairs(oflag, 8 * t, 8))
        def _():
            scatter_ocean(16 + t)

        @pl.when(long_pairs(iflag, 8 * t, 8))
        def _():
            scatter_ice(16 + t)

    itemp_next[...] = itemp[...] - 0.25 * (iacc[0:64, :] + iacc[64:128, :])
    for copy in salts + [state]:
        copy.wait()

    @pl.loop(0, 16)
    def _(m):
        rows = pl.ds(pl.multiple_of(8 * m, 8), 8)
        sides = []
        for c in range(2):
            here = slice(8 * c, 8 * c + 8)
            flux = []
            for f in range(4):
                high, low = (pl.ds(pl.multiple_of(part + CJ * f + 8 * m, 8), 8) for part in (0, 4 * CJ))
                flux.append(oacc[high, c * 128 : (c + 1) * 128] + oacc[low, c * 128 : (c + 1) * 128])
            top = [q[m, f * K, here, :] for f in range(4)]
            top[0] = top[0] + 20.0 * flux[0]
            top[1] = top[1] - 10.0 * (salt[c, rows, :] * flux[1])
            top[2] = top[2] + 20.0 * flux[2]
            top[3] = top[3] + 20.0 * flux[3]
            x = top[2] * top[2] + (top[3] * top[3] + 0.01 * SCALE * SCALE)
            damp = 1.0 / (1.0 + take(drag[0], canopy[rows, c * 128 : (c + 1) * 128], 0) * (x * lax.rsqrt(x)))
            top[2], top[3] = top[2] * damp, top[3] * damp
            sides.append(top)
        solved = [[None] * 4 for _ in range(2)]
        for k in range(K - 1, -1, -1):
            for c in range(2):
                for f in range(4):
                    here = slice(8 * c, 8 * c + 8)
                    value = sides[c][f] if k == 0 else q[m, f * K + k, here, :] + TOP[k] * sides[c][f]
                    value = value * (1.0 / (SCALE * DIAG[k]))
                    if k < K - 1:
                        value = value + (0.5 / DIAG[k]) * solved[c][f]
                    solved[c][f] = value
                    ybuf[m, f * K + k, here, :] = value
        for c in range(2):
            pltpu.make_async_copy(
                ybuf.at[m, :, 8 * c : 8 * c + 8, :], y.at[:, rows, c * 128 : (c + 1) * 128], sems.at[4 + c]
            ).start()

    for c in range(2):
        part = y.at[:, :, c * 128 : (c + 1) * 128]
        pltpu.make_async_copy(part, part, sems.at[4 + c]).wait()


def shards(
    ocean_state, canopy_type, drag_table, ocean_list, ice_list, weight_list, area_table, ice_temp, ice_cond, ice_vel
):
    st = ocean_state.reshape(FK, CJ, CI)
    olist, ilist, wlist = (x.reshape(DEV, SLOTS) for x in (ocean_list, ice_list, weight_list))
    itemp, icond = (x.reshape(64, 128) for x in (ice_temp, ice_cond))
    ivel = ice_vel.reshape(2, 64, 128).transpose(1, 0, 2).reshape(128, 128)
    area = area_table.reshape(1, 64)
    S = jax.ShapeDtypeStruct
    V = pltpu.VMEM
    tuv, rowlo, rowhi, colw, cole = pl.pallas_call(
        gather_kernel,
        out_shape=(
            S((3 * 128, 128), f32), S((FK, CI), f32), S((FK, CI), f32), S((CJ, 128), f32), S((CJ, 128), f32),
        ),
        in_specs=[ANY] * 2 + [VM],
        out_specs=(VM,) * 5,
        scratch_shapes=[
            V((2, FK, CJ, 128), f32), V((3, 2, CJ, 128), f32), V((768, 256), bf16), V((128, 128), i32),
            V((3 * 128, 128), f32), pltpu.SMEM((128, 128), i32), pltpu.SemaphoreType.DMA((4,)),
        ],
        compiler_params=pltpu.CompilerParams(vmem_limit_bytes=LIMIT),
        name="gather_slots",
    )(st, olist, olist)
    q, inb, out = pl.pallas_call(
        stencil_kernel,
        out_shape=(S((16, FK, 16, 128), f32), S((DEV, ROWS, 128), f32), S((DEV * ROWS, 128), f32)),
        in_specs=[ANY, ANY] + [VM] * 8 + [ANY] * 4,
        out_specs=(ANY,) * 3,
        scratch_shapes=[
            V((2, FK, 144, 128), f32), V((16, FK, 16, 128), f32), V((K, 8, 128), f32), V((DEV * ROWS, 128), f32),
            V((128, 128), f32), V((256, 256), bf16), V((128, 128), i32), V((4 * 128, 128), f32),
            V((NLON, NLAT // 2, ROWS, 128), f32), V((NLAT, NLON // 2, ROWS, 128), f32),
            V((FK, CI), f32), V((FK, CI), f32), V((CJ, 128), f32), V((CJ, 128), f32),
            pltpu.SemaphoreType.DMA((4, 2)), pltpu.SemaphoreType.DMA((15,)),
            pltpu.SemaphoreType.DMA((5,)), pltpu.SemaphoreType.DMA((4,)),
        ],
        compiler_params=pltpu.CompilerParams(vmem_limit_bytes=LIMIT, collective_id=0, has_side_effects=True),
        name="exchange_stencil",
    )(st, tuv, ilist, wlist, area, itemp, icond, ivel, canopy_type, drag_table, rowlo, rowhi, colw, cole)
    y, itemp_next = pl.pallas_call(
        finish_kernel,
        out_shape=(S((FK, CJ, CI), f32), S((64, 128), f32)),
        in_specs=[ANY] * 4 + [VM] * 8,
        out_specs=(ANY, VM),
        scratch_shapes=[
            V((16, FK, 16, 128), f32), V((16, FK, 16, 128), f32), V((2, CJ, 128), f32), V((K, 8, 128), f32),
            V((128, 128), i32), V((128, 128), i32), V((4 * 128, 128), f32), V((128, 128), f32),
            V((8 * CJ, CI), f32), V((128, 128), f32), V((2, 8 * CJ, 512), bf16), V((2, CI, 512), bf16),
            V((128, 512), bf16), V((128, 512), bf16),
            pltpu.SMEM((128, 128), i32), pltpu.SMEM((128, 128), i32), pltpu.SemaphoreType.DMA((7,)),
        ],
        compiler_params=pltpu.CompilerParams(vmem_limit_bytes=LIMIT),
        name="scatter_solve",
    )(st, olist, ilist, q, inb.reshape(DEV * ROWS, 128), out, tuv, olist, ilist, canopy_type, drag_table, itemp)
    return y.reshape(ocean_state.shape), itemp_next.reshape(ice_temp.shape)


def solution(mesh):
    return jax.shard_map(
        shards,
        mesh=mesh,
        in_specs=(
            P(None, None, "lat", "lon"),
            P("lat", "lon"),
            P(),
            P(("lon", "lat"), None),
            P(("lon", "lat"), None),
            P(("lon", "lat"), None),
            P(),
            P(("lon", "lat"), None),
            P(("lon", "lat"), None),
            P(("lon", "lat"), None, None),
        ),
        out_specs=(P(None, None, "lat", "lon"), P(("lon", "lat"), None)),
        check_vma=False,
    )
```

```python
import functools

import jax
import jax.numpy as jnp
from jax import lax
from jax.experimental import pallas as pl
from jax.experimental.pallas import tpu as pltpu
from jax.sharding import PartitionSpec as P

f32 = jnp.float32
bf16 = jnp.bfloat16
i32 = jnp.int32
MESH = pl.DeviceIdType.MESH
K = 20
NF = 4
FK = NF * K
CJ = 128
CI = 256
NLON = 16
NLAT = 8
DEV = NLON * NLAT
SLOTS = 128
ROWS = 8
SENT = 6
SCALE = 40.0

DIAG = [1.5]
for _k in range(1, K):
    DIAG.append((1.5 if _k == K - 1 else 2.0) - 0.25 / DIAG[-1])
FWD = [0.0] + [0.5 / DIAG[_k - 1] for _k in range(1, K)]
TOP = [1.0]
for _k in range(1, K):
    TOP.append(FWD[_k] * TOP[-1])

ANY = pl.BlockSpec(memory_space=pl.ANY)
LIMIT = 60 << 20


def lanes():
    return lax.broadcasted_iota(i32, (8, 128), 1)


def take(table, index, axis):
    return jnp.take_along_axis(table, index, axis=axis, mode="promise_in_bounds")


def split(x):
    high = x.astype(bf16)
    return high, (x - high.astype(f32)).astype(bf16)


def one_hot(index, count):
    rows = lax.broadcasted_iota(i32, (count, index.shape[1]), 0)
    return rows == jnp.broadcast_to(index, (count, index.shape[1]))


def pack(even, odd):
    left = lanes() < 64
    return (
        jnp.where(left, even, pltpu.roll(odd, 64, 1)),
        jnp.where(left, pltpu.roll(even, 64, 1), odd),
    )


def pack_list(source, packed):
    for g in range(8):
        first, second = pack(
            source[pl.ds(16 * g, 8, stride=2), :], source[pl.ds(16 * g + 1, 8, stride=2), :]
        )
        packed[8 * g : 8 * g + 8, :] = first
        packed[64 + 8 * g : 72 + 8 * g, :] = second


def long_pairs(flags, first, count):
    most = flags[first, 64]
    for i in range(1, count):
        most = jnp.maximum(most, flags[first + i, 64])
    return most >= 0


def gather(tile, packed, table, fields, rows, got):
    hots, his = [], []
    for h in range(2):
        row = packed[pl.ds(2 * tile + h, 1), :]
        his.append(row >> 8)
        hots.append(jnp.where(one_hot(row & 255, 256), 1.0, 0.0).astype(bf16))
    res = jnp.dot(table[...], jnp.concatenate(hots, axis=1), preferred_element_type=f32)
    half = fields * rows
    res = res[:half] + res[half:]
    for h in range(2):
        mask = one_hot(his[h], rows)
        for f in range(fields):
            value = jnp.where(mask, res[f * rows : (f + 1) * rows, h * 128 : (h + 1) * 128], 0.0)
            got[pl.ds(f * 128 + 2 * tile + h, 1), :] = jnp.sum(value, axis=0, keepdims=True)


def unpack(got, f, g):
    left = lanes() < 64
    first = got[f * 128 + 8 * g : f * 128 + 8 * g + 8, :]
    second = got[f * 128 + 64 + 8 * g : f * 128 + 72 + 8 * g, :]
    return (
        jnp.where(left, first, pltpu.roll(second, 64, 1)),
        jnp.where(left, pltpu.roll(first, 64, 1), second),
    )


def gather_kernel(
    loads, stores, st, olist_any, olist,
    tuv, rowlo, rowhi, colw, cole,
    full, surf, otab, opack, ogot, oflag, sems,
):
    flags = pltpu.make_async_copy(olist_any, oflag, sems.at[0])
    tops = [
        pltpu.make_async_copy(st.at[f * K, :, c * 128 : (c + 1) * 128], surf.at[n, c], sems.at[1])
        for n, f in enumerate((0, 2, 3))
        for c in range(2)
    ]
    state = [
        pltpu.make_async_copy(st.at[:, :, c * 128 : (c + 1) * 128], full.at[c], sems.at[2 + c]) for c in range(2)
    ]
    for copy in tops:
        copy.start()
    loads[0].wait()
    pack_list(olist, opack)
    ogot[...] = jnp.zeros_like(ogot)
    pltpu.make_async_copy(surf, surf, sems.at[1]).wait()
    for copy in [flags] + state:
        copy.start()
    for n in range(3):
        for c in range(2):
            high, low = split(surf[n, c])
            otab[128 * n : 128 * n + 128, c * 128 : (c + 1) * 128] = high
            otab[384 + 128 * n : 512 + 128 * n, c * 128 : (c + 1) * 128] = low

    def columns(m):
        lane = lanes()
        rows = pl.ds(pl.multiple_of(8 * m, 8), 8)
        west = jnp.zeros((8, 128), f32)
        east = jnp.zeros((8, 128), f32)
        for fk in range(FK):
            both = jnp.where(lane == 127, full[1, fk, rows, :], full[0, fk, rows, :])
            both = pltpu.roll(both, fk, 1) if fk else both
            west = jnp.where(lane == fk, both, west)
            east = jnp.where(lane == (fk - 1) % 128, both, east)
        colw[rows, :] = west
        cole[rows, :] = east

    @pl.loop(0, 4)
    def _(t):
        for j in range(4):
            gather(4 * t + j, opack, otab, 3, 128, ogot)

    for copy in state:
        copy.wait()

    @pl.loop(4, 8)
    def _(t):
        for j in range(4):
            gather(4 * t + j, opack, otab, 3, 128, ogot)
        for j in range(4):
            columns(4 * (t - 4) + j)

    for fk in range(FK):
        for c in range(2):
            rowlo[fk : fk + 1, c * 128 : (c + 1) * 128] = full[c, fk, 0:1, :]
            rowhi[fk : fk + 1, c * 128 : (c + 1) * 128] = full[c, fk, 127:128, :]
    for copy in stores[1:]:
        copy.start()
    flags.wait()

    @pl.loop(0, 32)
    def _(t):
        @pl.when(long_pairs(oflag, 4 * t, 4))
        def _():
            gather(32 + t, opack, otab, 3, 128, ogot)

    for g in range(8):
        for n in range(3):
            even, odd = unpack(ogot, n, g)
            tuv[pl.ds(128 * n + 16 * g, 8, stride=2), :] = even
            tuv[pl.ds(128 * n + 16 * g + 1, 8, stride=2), :] = odd
    stores[0].start()


def stencil_row(m, buf, q, canopy, east_col, west_col, drag, lat):
    lane = lanes()
    sub = lax.broadcasted_iota(i32, (8, 128), 0)
    first, last = lane == 0, lane == 127
    rows = pl.ds(pl.multiple_of(8 * m, 8), 8)
    east_halo, west_halo = east_col[rows, :], west_col[rows, :]
    kind = [canopy[rows, c * 128 : (c + 1) * 128] for c in range(2)]
    row = (lat * CJ + 8 * m + sub).astype(f32)
    cor = 4.0 * (2.0 * (row + 0.5) / (CJ * NLAT) - 1.0)
    for c in range(2):
        elim = [None] * NF
        gx = gy = None
        for k in range(K):
            C, E, W, N, S = ([None] * NF for _ in range(5))
            for f in range(NF):
                fk = f * K + k
                mine, other = (buf[d, fk, pl.ds(pl.multiple_of(8 + 8 * m, 8), 8), :] for d in (c, 1 - c))
                C[f] = mine
                N[f] = buf[c, fk, pl.ds(9 + 8 * m, 8), :]
                S[f] = buf[c, fk, pl.ds(7 + 8 * m, 8), :]
                if c == 0:
                    E[f] = pltpu.roll(jnp.where(first, other, mine), 127, 1)
                    W[f] = jnp.where(first, pltpu.roll(west_halo, (1 - fk) % 128, 1), pltpu.roll(mine, 1, 1))
                else:
                    E[f] = jnp.where(last, pltpu.roll(east_halo, (127 - fk) % 128, 1), pltpu.roll(mine, 127, 1))
                    W[f] = pltpu.roll(jnp.where(last, other, mine), 1, 1)
            u, v = C[2], C[3]
            eE = (0.4 - u) - E[2]
            eW = (0.4 + u) + W[2]
            eN = (0.4 - v) - N[3]
            eS = (0.4 + v) + S[3]
            mid = 36.8 + ((eE + eW) + (eN + eS))
            new = [(C[f] * mid + E[f] * eE) + (W[f] * eW + N[f] * eN) + S[f] * eS for f in range(NF)]
            hx = 0.4 * (E[1] - W[1]) - 0.1 * (E[0] - W[0])
            hy = 0.4 * (N[1] - S[1]) - 0.1 * (N[0] - S[0])
            px = hx if k == 0 else gx + hx
            py = hy if k == 0 else gy + hy
            gx, gy = px + hx, py + hy
            new[2] = new[2] + (cor * v - px)
            new[3] = new[3] - (cor * u + py)
            if k > 0:
                x = new[2] * new[2] + (new[3] * new[3] + 0.01 * SCALE * SCALE)
                damp = 1.0 / (1.0 + take(drag[k], kind[c], 0) * (x * lax.rsqrt(x)))
                new[2], new[3] = new[2] * damp, new[3] * damp
            for f in range(NF):
                if k > 1:
                    new[f] = new[f] + FWD[k] * elim[f]
                elim[f] = new[f]
                q[m, f * K + k, c * 8 : (c + 1) * 8, :] = new[f]


def drag_levels(table, drag):
    for k in range(K):
        drag[k] = jnp.broadcast_to(table[:, k : k + 1] * (0.1 / SCALE), (8, 128))


def ice_messages(ilist, wlist, area, itemp, icond, ivel, msg, itab, ipack, igot):
    @pl.loop(0, 64, step=8)
    def _(t):
        for j in range(8):
            gather(t + j, ipack, itab, 4, 32, igot)

    areas = jnp.broadcast_to(jnp.concatenate([area[...], area[...]], axis=1), (8, 128))
    for g in range(8):
        for f in range(4):
            even, odd = unpack(igot, f, g)
            msg[pl.ds(128 * g + 2 + f, 8, stride=16), :] = even
            msg[pl.ds(128 * g + 10 + f, 8, stride=16), :] = odd
    for g in range(16):
        index = wlist[8 * g : 8 * g + 8, :]
        value = jnp.where(index >= 0, take(areas, index & 63, 1), 0.0)
        msg[pl.ds(64 * g + 1, 8, stride=8), :] = value
        for f in range(SENT, ROWS):
            msg[pl.ds(64 * g + f, 8, stride=8), :] = jnp.zeros((8, 128), f32)


def stencil_kernel(
    operands, _, st, tuv, ilist, wlist, area, itemp, icond, ivel, canopy, table, rowlo, rowhi, colw, cole,
    q_any, inb, out,
    buf, q, drag, msg, temps, itab, ipack, igot, mid_a, mid_b, north, south, east_col, west_col, sems, hops, halo_send, halo_recv,
):
    lon, lat = lax.axis_index("lon"), lax.axis_index("lat")
    loads = [
        [
            pltpu.make_async_copy(
                st.at[:, 32 * g : 32 * g + 32, c * 128 : (c + 1) * 128],
                buf.at[c, :, 8 + 32 * g : 40 + 32 * g, :],
                sems.at[g, c],
            )
            for c in range(2)
        ]
        for g in range(4)
    ]
    surface = pltpu.make_async_copy(tuv.at[0:128], temps, hops.at[13])
    surface.start()
    barrier = pltpu.get_barrier_semaphore()
    for i in range(1, NLON):
        pl.semaphore_signal(barrier, inc=1, device_id=(lax.rem(lon + i, NLON), lat), device_id_type=MESH)
    for i in range(1, NLAT):
        pl.semaphore_signal(barrier, inc=1, device_id=(lon, lax.rem(lat + i, NLAT)), device_id_type=MESH)
    for copy in operands:
        copy.wait()
    for pair in loads:
        for copy in pair:
            copy.start()
    pack_list(ilist, ipack)
    for f in range(4):
        for c in range(2):
            if f < 2:
                x = (icond, itemp)[f][pl.ds(c, 32, stride=2), :]
            else:
                x = ivel[pl.ds(2 * c + f - 2, 32, stride=4), :]
            high, low = split(x)
            itab[32 * f : 32 * f + 32, c * 128 : (c + 1) * 128] = high
            itab[128 + 32 * f : 160 + 32 * f, c * 128 : (c + 1) * 128] = low
    pl.semaphore_wait(barrier, NLON + NLAT - 2)

    def halo(src, dst, n, target):
        return pltpu.make_async_remote_copy(
            src_ref=src, dst_ref=dst, send_sem=halo_send.at[n], recv_sem=halo_recv.at[n],
            device_id=target, device_id_type=MESH,
        )

    to_west = halo(colw, east_col, 0, (lax.rem(lon + NLON - 1, NLON), lat))
    to_east = halo(cole, west_col, 1, (lax.rem(lon + 1, NLON), lat))
    to_north = halo(rowhi, south, 2, (lon, lax.rem(lat + 1, NLAT)))
    to_south = halo(rowlo, north, 3, (lon, lax.rem(lat + NLAT - 1, NLAT)))
    to_fold = halo(rowhi, north, 3, (NLON - 1 - lon, lat))
    to_west.start()
    to_east.start()
    to_north.start()

    @pl.when(lat > 0)
    def _():
        to_south.start()

    @pl.when(lat == NLAT - 1)
    def _():
        pltpu.make_async_remote_copy(
            src_ref=rowhi, dst_ref=north, send_sem=halo_send.at[4], recv_sem=halo_recv.at[3],
            device_id=(NLON - 1 - lon, lat), device_id_type=MESH,
        ).start()

    def hop(src, dst, n, target):
        return pltpu.make_async_remote_copy(
            src_ref=src, dst_ref=dst, send_sem=hops.at[n], recv_sem=hops.at[n + 1],
            device_id=target, device_id_type=MESH,
        )

    ice_messages(ilist, wlist, area, itemp, icond, ivel, msg, itab, ipack, igot)
    surface.wait()
    for g in range(16):
        msg[pl.ds(64 * g, 8, stride=8), :] = temps[8 * g : 8 * g + 8, :]
    keep = pltpu.make_async_copy(msg, out, hops.at[12])
    keep.start()
    even = lax.rem(lon + lat, 2) == 0
    by_a = msg.reshape(NLON, NLAT // 2, 2, ROWS, 128)
    by_b = msg.reshape(NLON // 2, 2, NLAT, ROWS, 128)

    def first_a(peer):
        return by_a.at[peer, :, lax.rem(peer, 2), 0:SENT], mid_a.at[lon, :, 0:SENT]

    def first_b(peer):
        return by_b.at[:, 1 - lax.rem(peer, 2), peer, 0:SENT], mid_b.at[lat, :, 0:SENT]

    for i in range(1, NLON):
        peer = lax.rem(lon + i, NLON)
        hop(*first_a(peer), 0, (peer, lat)).start()
    for i in range(1, NLAT):
        peer = lax.rem(lat + i, NLAT)
        hop(*first_b(peer), 2, (lon, peer)).start()
    own_a = pltpu.make_async_copy(*first_a(lon), hops.at[8])
    own_b = pltpu.make_async_copy(*first_b(lat), hops.at[9])
    own_a.start()
    own_b.start()
    in4 = inb.reshape(NLON, NLAT, ROWS, 128)

    def second_a(peer):
        return mid_a.at[:, peer // 2, 0:SENT], in4.at[:, lat, 0:SENT]

    def second_b(peer):
        return mid_b.at[:, peer // 2, 0:SENT], in4.at[lon, :, 0:SENT]

    def blocks(ref, n):
        part = ref.at[0:n, 0:SENT]
        return part, part

    def taken(n, sem):
        pltpu.make_async_copy(*blocks(inb, n), hops.at[sem]).wait()

    drag_levels(table, drag)
    to_west.wait_recv()
    to_east.wait_recv()
    to_north.wait_recv()
    to_fold.wait_recv()
    top = lat == NLAT - 1
    inside = jnp.where(lat > 0, 1.0, 0.0)
    back = 127 - lanes()
    for g in range(10):
        part = slice(8 * g, 8 * g + 8)
        sign = 1.0 if g < 5 else -1.0
        halves = [north[part, c * 128 : (c + 1) * 128] for c in range(2)]
        for c in range(2):
            turned = sign * take(halves[1 - c], back, 1)
            value = jnp.where(top, turned, halves[c])
            below = south[part, c * 128 : (c + 1) * 128] * inside
            for r in range(8):
                buf[c, 8 * g + r, 136:137, :] = value[r : r + 1]
                buf[c, 8 * g + r, 7:8, :] = below[r : r + 1]
    for copy in loads[0]:
        copy.wait()

    @pl.loop(0, 8)
    def _(g):
        @pl.when(lax.rem(g, 2) - jnp.where(g > 5, 1, 0) == 1)
        def _():
            for c in range(2):
                pltpu.make_async_copy(
                    st.at[:, 0:32, 0:128], buf.at[c, :, 8:40, :], sems.at[g // 2 + 1, c]
                ).wait()

        @pl.when(g == 3)
        def _():
            taken((NLON - 1) * NLAT // 2, 1)
            taken((NLAT - 1) * NLON // 2, 3)
            own_a.wait()
            own_b.wait()

            @pl.when(even)
            def _():
                pltpu.make_async_copy(*second_a(lat), hops.at[10]).start()
                for i in range(2, NLAT, 2):
                    peer = lax.rem(lat + i, NLAT)
                    hop(*second_a(peer), 4, (lon, peer)).start()
                for i in range(1, NLON, 2):
                    peer = lax.rem(lon + i, NLON)
                    hop(*second_b(peer), 6, (peer, lat)).start()

            @pl.when(jnp.logical_not(even))
            def _():
                pltpu.make_async_copy(*second_b(lon), hops.at[11]).start()
                for i in range(1, NLAT, 2):
                    peer = lax.rem(lat + i, NLAT)
                    hop(*second_a(peer), 4, (lon, peer)).start()
                for i in range(2, NLON, 2):
                    peer = lax.rem(lon + i, NLON)
                    hop(*second_b(peer), 6, (peer, lat)).start()

        @pl.loop(0, 2)
        def _(j):
            m = 2 * g + j
            stencil_row(m, buf, q, canopy, east_col, west_col, drag, lat)
            pltpu.make_async_copy(q.at[m], q_any.at[m], hops.at[14]).start()

    pltpu.make_async_copy(q, q_any, hops.at[14]).wait()
    keep.wait()
    @pl.when(even)
    def _():
        taken((NLAT - 1) * NLON, 5)
        taken(NLON, 10)
        taken((NLAT // 2 - 1) * NLON, 4)
        taken((NLON // 2) * NLAT, 6)

    @pl.when(jnp.logical_not(even))
    def _():
        taken((NLON - 1) * NLAT, 7)
        taken(NLAT, 11)
        taken((NLAT // 2) * NLON, 4)
        taken((NLON // 2 - 1) * NLAT, 6)

    taken((NLON - 1) * NLAT // 2, 0)
    taken((NLAT - 1) * NLON // 2, 2)
    to_west.wait_send()
    to_east.wait_send()
    to_north.wait_send()

    @pl.when(lat > 0)
    def _():
        to_south.wait_send()

    @pl.when(lat == NLAT - 1)
    def _():
        pltpu.make_async_copy(rowhi, rowhi, halo_send.at[4]).wait()


def finish_kernel(
    loads, stores, st, olist_any, ilist_any, q_any, inb, out, tuv, olist, ilist, canopy, table, itemp,
    y, itemp_next,
    q, ybuf, salt, drag, opack, ipack, oval, ival, oacc, iacc, owide, ocols, iwide, icols, oflag, iflag, sems,
):
    flags = [
        pltpu.make_async_copy(olist_any, oflag, sems.at[0]),
        pltpu.make_async_copy(ilist_any, iflag, sems.at[1]),
    ]
    salts = [
        pltpu.make_async_copy(st.at[K, :, c * 128 : (c + 1) * 128], salt.at[c], sems.at[2 + c])
        for c in range(2)
    ]
    state = pltpu.make_async_copy(q_any, q, sems.at[6])
    oacc[...] = jnp.zeros_like(oacc)
    iacc[...] = jnp.zeros_like(iacc)
    for copy in loads[3:5]:
        copy.wait()
    pack_list(olist, opack)
    pack_list(ilist, ipack)
    for copy in loads[0:3] + loads[5:]:
        copy.wait()
    for copy in flags + salts + [state]:
        copy.start()
    drag_levels(table, drag)
    for g in range(8):
        sides, ices = [], []
        for odd in range(2):
            block = lambda ref, f: ref[pl.ds(128 * g + 8 * odd + f, 8, stride=16), :]
            slot = [tuv[pl.ds(128 * n + 16 * g + odd, 8, stride=2), :] for n in range(3)]
            a, cond, temp, iu, iv = (block(inb, f) for f in range(1, 6))
            du, dv = iu - slot[1], iv - slot[2]
            x = du * du + dv * dv + 0.01
            drift = 0.5 * a * (x * lax.rsqrt(x))
            heat = a * cond
            sides.append([heat * (temp - slot[0]), heat, drift * du, drift * dv])
            ices.append(block(out, 1) * block(out, 2) * (block(out, 3) - block(inb, 0)))
        for f in range(4):
            first, second = pack(sides[0][f], sides[1][f])
            oval[128 * f + 8 * g : 128 * f + 8 * g + 8, :] = first
            oval[128 * f + 64 + 8 * g : 128 * f + 72 + 8 * g, :] = second
        first, second = pack(*ices)
        ival[8 * g : 8 * g + 8, :] = first
        ival[64 + 8 * g : 72 + 8 * g, :] = second

    def hot_columns(tile, packed, width, cols):
        for h in range(4):
            index = packed[pl.ds(4 * tile + h, 1), :] & (width - 1)
            cols[:, 128 * h : 128 * h + 128] = jnp.where(one_hot(index, width), 1.0, 0.0).astype(bf16)

    def add(wide, cols, acc):
        acc[...] += lax.dot_general(wide, cols, (((1,), (1,)), ((), ())), preferred_element_type=f32)

    def scatter_ocean(tile, p=0):
        hot_columns(tile, opack, CI, ocols.at[p])
        for h in range(4):
            mask = one_hot(opack[pl.ds(4 * tile + h, 1), :] >> 8, CJ)
            for f in range(4):
                value = oval[pl.ds(128 * f + 4 * tile + h, 1), :]
                high = value.astype(bf16).astype(f32)
                for n, part in enumerate((high, value - high)):
                    part = jnp.where(mask, jnp.broadcast_to(part, (CJ, 128)), 0.0).astype(bf16)
                    owide[p, 512 * n + CJ * f : 512 * n + CJ * (f + 1), 128 * h : 128 * h + 128] = part
        add(owide[p], ocols[p], oacc)

    def scatter_ice(tile):
        hot_columns(tile, ipack, 128, icols)
        for h in range(4):
            mask = one_hot(ipack[pl.ds(4 * tile + h, 1), :] >> 7, 64)
            value = ival[pl.ds(4 * tile + h, 1), :]
            high = value.astype(bf16).astype(f32)
            for n, part in enumerate((high, value - high)):
                part = jnp.where(mask, jnp.broadcast_to(part, (64, 128)), 0.0).astype(bf16)
                iwide[64 * n : 64 * n + 64, 128 * h : 128 * h + 128] = part
        add(iwide[...], icols[...], iacc)

    @pl.loop(0, 16, step=2)
    def _(t):
        scatter_ocean(t)
        scatter_ocean(t + 1, 1)
        scatter_ice(t)
        scatter_ice(t + 1)

    for copy in flags:
        copy.wait()

    @pl.loop(0, 16)
    def _(t):
        @pl.when(long_pairs(oflag, 8 * t, 8))
        def _():
            scatter_ocean(16 + t)

        @pl.when(long_pairs(iflag, 8 * t, 8))
        def _():
            scatter_ice(16 + t)

    itemp_next[...] = itemp[...] - 0.25 * (iacc[0:64, :] + iacc[64:128, :])
    stores[0].start()
    for copy in salts + [state]:
        copy.wait()

    @pl.loop(0, 16)
    def _(m):
        rows = pl.ds(pl.multiple_of(8 * m, 8), 8)
        sides = []
        for c in range(2):
            here = slice(8 * c, 8 * c + 8)
            flux = []
            for f in range(4):
                high, low = (pl.ds(pl.multiple_of(part + CJ * f + 8 * m, 8), 8) for part in (0, 4 * CJ))
                flux.append(oacc[high, c * 128 : (c + 1) * 128] + oacc[low, c * 128 : (c + 1) * 128])
            top = [q[m, f * K, here, :] for f in range(4)]
            top[0] = top[0] + 20.0 * flux[0]
            top[1] = top[1] - 10.0 * (salt[c, rows, :] * flux[1])
            top[2] = top[2] + 20.0 * flux[2]
            top[3] = top[3] + 20.0 * flux[3]
            x = top[2] * top[2] + (top[3] * top[3] + 0.01 * SCALE * SCALE)
            damp = 1.0 / (1.0 + take(drag[0], canopy[rows, c * 128 : (c + 1) * 128], 0) * (x * lax.rsqrt(x)))
            top[2], top[3] = top[2] * damp, top[3] * damp
            sides.append(top)
        solved = [[None] * 4 for _ in range(2)]
        for k in range(K - 1, -1, -1):
            for c in range(2):
                for f in range(4):
                    here = slice(8 * c, 8 * c + 8)
                    value = sides[c][f] if k == 0 else q[m, f * K + k, here, :] + TOP[k] * sides[c][f]
                    value = value * (1.0 / (SCALE * DIAG[k]))
                    if k < K - 1:
                        value = value + (0.5 / DIAG[k]) * solved[c][f]
                    solved[c][f] = value
                    ybuf[m, f * K + k, here, :] = value
        for c in range(2):
            pltpu.make_async_copy(
                ybuf.at[m, :, 8 * c : 8 * c + 8, :], y.at[:, rows, c * 128 : (c + 1) * 128], sems.at[4 + c]
            ).start()

    for c in range(2):
        part = y.at[:, :, c * 128 : (c + 1) * 128]
        pltpu.make_async_copy(part, part, sems.at[4 + c]).wait()


def staged(kernel, args, moved, outs, kept, scratch, **options):
    count, given = len(args), len(outs)

    def body(*refs):
        ins, results, rest = list(refs[:count]), list(refs[count : count + given]), list(refs[count + given :])
        sems = rest.pop()
        loads, stores = [], []
        for i in moved:
            place = rest.pop(0)
            loads.append(pltpu.make_async_copy(ins[i], place, sems.at[len(loads)]))
            ins[i] = place
        for i in range(given):
            if i not in kept:
                place = rest.pop(0)
                stores.append(pltpu.make_async_copy(place, results[i], sems.at[len(loads) + len(stores)]))
                results[i] = place
        for copy in loads:
            copy.start()
        kernel(loads, stores, *ins, *results, *rest)
        for copy in stores:
            copy.wait()

    places = [pltpu.VMEM(args[i].shape, args[i].dtype) for i in moved]
    places += [pltpu.VMEM(o.shape, o.dtype) for i, o in enumerate(outs) if i not in kept]
    return pl.pallas_call(
        body,
        out_shape=outs,
        in_specs=[ANY] * count,
        out_specs=(ANY,) * given,
        scratch_shapes=places + scratch + [pltpu.SemaphoreType.DMA((len(places),))],
        **options,
    )(*args)


def shards(
    ocean_state, canopy_type, drag_table, ocean_list, ice_list, weight_list, area_table, ice_temp, ice_cond, ice_vel
):
    st = ocean_state.reshape(FK, CJ, CI)
    olist, ilist, wlist = (x.reshape(DEV, SLOTS) for x in (ocean_list, ice_list, weight_list))
    itemp, icond = (x.reshape(64, 128) for x in (ice_temp, ice_cond))
    ivel = ice_vel.reshape(2, 64, 128).transpose(1, 0, 2).reshape(128, 128)
    area = area_table.reshape(1, 64)
    S = jax.ShapeDtypeStruct
    V = pltpu.VMEM
    tuv, rowlo, rowhi, colw, cole = staged(
        gather_kernel,
        (st, olist, olist),
        (2,),
        (S((3 * 128, 128), f32), S((FK, CI), f32), S((FK, CI), f32), S((CJ, 128), f32), S((CJ, 128), f32)),
        (),
        [
            V((2, FK, CJ, 128), f32), V((3, 2, CJ, 128), f32), V((768, 256), bf16), V((128, 128), i32),
            V((3 * 128, 128), f32), pltpu.SMEM((128, 128), i32), pltpu.SemaphoreType.DMA((4,)),
        ],
        compiler_params=pltpu.CompilerParams(vmem_limit_bytes=LIMIT),
        name="gather_slots",
    )
    q, inb, out = staged(
        stencil_kernel,
        (st, tuv, ilist, wlist, area, itemp, icond, ivel, canopy_type, drag_table, rowlo, rowhi, colw, cole),
        range(2, 10),
        (S((16, FK, 16, 128), f32), S((DEV, ROWS, 128), f32), S((DEV * ROWS, 128), f32)),
        range(3),
        [
            V((2, FK, 144, 128), f32), V((16, FK, 16, 128), f32), V((K, 8, 128), f32), V((DEV * ROWS, 128), f32),
            V((128, 128), f32), V((256, 256), bf16), V((128, 128), i32), V((4 * 128, 128), f32),
            V((NLON, NLAT // 2, ROWS, 128), f32), V((NLAT, NLON // 2, ROWS, 128), f32),
            V((FK, CI), f32), V((FK, CI), f32), V((CJ, 128), f32), V((CJ, 128), f32),
            pltpu.SemaphoreType.DMA((4, 2)), pltpu.SemaphoreType.DMA((15,)),
            pltpu.SemaphoreType.DMA((5,)), pltpu.SemaphoreType.DMA((4,)),
        ],
        compiler_params=pltpu.CompilerParams(vmem_limit_bytes=LIMIT, collective_id=0, has_side_effects=True),
        name="exchange_stencil",
    )
    y, itemp_next = staged(
        finish_kernel,
        (st, olist, ilist, q, inb.reshape(DEV * ROWS, 128), out, tuv, olist, ilist, canopy_type, drag_table, itemp),
        range(4, 12),
        (S((FK, CJ, CI), f32), S((64, 128), f32)),
        (0,),
        [
            V((16, FK, 16, 128), f32), V((16, FK, 16, 128), f32), V((2, CJ, 128), f32), V((K, 8, 128), f32),
            V((128, 128), i32), V((128, 128), i32), V((4 * 128, 128), f32), V((128, 128), f32),
            V((8 * CJ, CI), f32), V((128, 128), f32), V((2, 8 * CJ, 512), bf16), V((2, CI, 512), bf16),
            V((128, 512), bf16), V((128, 512), bf16),
            pltpu.SMEM((128, 128), i32), pltpu.SMEM((128, 128), i32), pltpu.SemaphoreType.DMA((7,)),
        ],
        compiler_params=pltpu.CompilerParams(vmem_limit_bytes=LIMIT),
        name="scatter_solve",
    )
    return y.reshape(ocean_state.shape), itemp_next.reshape(ice_temp.shape)


def solution(mesh):
    return jax.shard_map(
        shards,
        mesh=mesh,
        in_specs=(
            P(None, None, "lat", "lon"),
            P("lat", "lon"),
            P(),
            P(("lon", "lat"), None),
            P(("lon", "lat"), None),
            P(("lon", "lat"), None),
            P(),
            P(("lon", "lat"), None),
            P(("lon", "lat"), None),
            P(("lon", "lat"), None, None),
        ),
        out_specs=(P(None, None, "lat", "lon"), P(("lon", "lat"), None)),
        check_vma=False,
    )
```

```python
import functools

import jax
import jax.numpy as jnp
from jax import lax
from jax.experimental import pallas as pl
from jax.experimental.pallas import tpu as pltpu
from jax.sharding import PartitionSpec as P

f32 = jnp.float32
bf16 = jnp.bfloat16
i32 = jnp.int32
MESH = pl.DeviceIdType.MESH
K = 20
NF = 4
FK = NF * K
CJ = 128
CI = 256
NLON = 16
NLAT = 8
DEV = NLON * NLAT
SLOTS = 128
ROWS = 8
SENT = 6
SCALE = 40.0

DIAG = [1.5]
for _k in range(1, K):
    DIAG.append((1.5 if _k == K - 1 else 2.0) - 0.25 / DIAG[-1])
FWD = [0.0] + [0.5 / DIAG[_k - 1] for _k in range(1, K)]
TOP = [1.0]
for _k in range(1, K):
    TOP.append(FWD[_k] * TOP[-1])

ANY = pl.BlockSpec(memory_space=pl.ANY)
LIMIT = 60 << 20


def lanes():
    return lax.broadcasted_iota(i32, (8, 128), 1)


def take(table, index, axis):
    return jnp.take_along_axis(table, index, axis=axis, mode="promise_in_bounds")


def split(x):
    high = x.astype(bf16)
    return high, (x - high.astype(f32)).astype(bf16)


def one_hot(index, count):
    rows = lax.broadcasted_iota(i32, (count, index.shape[1]), 0)
    return rows == jnp.broadcast_to(index, (count, index.shape[1]))


def pack(even, odd):
    left = lanes() < 64
    return (
        jnp.where(left, even, pltpu.roll(odd, 64, 1)),
        jnp.where(left, pltpu.roll(even, 64, 1), odd),
    )


def pack_list(source, packed):
    for g in range(8):
        first, second = pack(
            source[pl.ds(16 * g, 8, stride=2), :], source[pl.ds(16 * g + 1, 8, stride=2), :]
        )
        packed[8 * g : 8 * g + 8, :] = first
        packed[64 + 8 * g : 72 + 8 * g, :] = second


def long_pairs(flags, first, count):
    most = flags[first, 64]
    for i in range(1, count):
        most = jnp.maximum(most, flags[first + i, 64])
    return most >= 0


def gather(tile, packed, table, fields, rows, got):
    hots, his = [], []
    for h in range(2):
        row = packed[pl.ds(2 * tile + h, 1), :]
        his.append(row >> 8)
        hots.append(jnp.where(one_hot(row & 255, 256), 1.0, 0.0).astype(bf16))
    res = jnp.dot(table[...], jnp.concatenate(hots, axis=1), preferred_element_type=f32)
    half = fields * rows
    res = res[:half] + res[half:]
    for h in range(2):
        mask = one_hot(his[h], rows)
        for f in range(fields):
            value = jnp.where(mask, res[f * rows : (f + 1) * rows, h * 128 : (h + 1) * 128], 0.0)
            got[pl.ds(f * 128 + 2 * tile + h, 1), :] = jnp.sum(value, axis=0, keepdims=True)


def unpack(got, f, g):
    left = lanes() < 64
    first = got[f * 128 + 8 * g : f * 128 + 8 * g + 8, :]
    second = got[f * 128 + 64 + 8 * g : f * 128 + 72 + 8 * g, :]
    return (
        jnp.where(left, first, pltpu.roll(second, 64, 1)),
        jnp.where(left, pltpu.roll(first, 64, 1), second),
    )


def gather_kernel(
    loads, stores, st, olist_any, olist,
    tuv, rowlo, rowhi, colw, cole,
    full, surf, otab, opack, ogot, oflag, sems,
):
    flags = pltpu.make_async_copy(olist_any, oflag, sems.at[0])
    tops = [
        pltpu.make_async_copy(st.at[f * K, :, c * 128 : (c + 1) * 128], surf.at[n, c], sems.at[1])
        for n, f in enumerate((0, 2, 3))
        for c in range(2)
    ]
    state = [
        pltpu.make_async_copy(st.at[:, :, c * 128 : (c + 1) * 128], full.at[c], sems.at[2 + c]) for c in range(2)
    ]
    for copy in tops:
        copy.start()
    loads[0].wait()
    pack_list(olist, opack)
    ogot[...] = jnp.zeros_like(ogot)
    pltpu.make_async_copy(surf, surf, sems.at[1]).wait()
    for copy in [flags] + state:
        copy.start()
    for n in range(3):
        for c in range(2):
            high, low = split(surf[n, c])
            otab[128 * n : 128 * n + 128, c * 128 : (c + 1) * 128] = high
            otab[384 + 128 * n : 512 + 128 * n, c * 128 : (c + 1) * 128] = low

    def columns(m):
        lane = lanes()
        rows = pl.ds(pl.multiple_of(8 * m, 8), 8)
        west = jnp.zeros((8, 128), f32)
        east = jnp.zeros((8, 128), f32)
        for fk in range(FK):
            both = jnp.where(lane == 127, full[1, fk, rows, :], full[0, fk, rows, :])
            both = pltpu.roll(both, fk, 1) if fk else both
            west = jnp.where(lane == fk, both, west)
            east = jnp.where(lane == (fk - 1) % 128, both, east)
        colw[rows, :] = west
        cole[rows, :] = east

    @pl.loop(0, 4)
    def _(t):
        for j in range(4):
            gather(4 * t + j, opack, otab, 3, 128, ogot)

    for copy in state:
        copy.wait()

    @pl.loop(4, 8)
    def _(t):
        for j in range(4):
            gather(4 * t + j, opack, otab, 3, 128, ogot)
        for j in range(4):
            columns(4 * (t - 4) + j)

    for fk in range(FK):
        for c in range(2):
            rowlo[fk : fk + 1, c * 128 : (c + 1) * 128] = full[c, fk, 0:1, :]
            rowhi[fk : fk + 1, c * 128 : (c + 1) * 128] = full[c, fk, 127:128, :]
    for copy in stores[1:]:
        copy.start()
    flags.wait()

    @pl.loop(0, 32)
    def _(t):
        @pl.when(long_pairs(oflag, 4 * t, 4))
        def _():
            gather(32 + t, opack, otab, 3, 128, ogot)

    for g in range(8):
        for n in range(3):
            even, odd = unpack(ogot, n, g)
            tuv[pl.ds(128 * n + 16 * g, 8, stride=2), :] = even
            tuv[pl.ds(128 * n + 16 * g + 1, 8, stride=2), :] = odd
    stores[0].start()


def stencil_row(m, buf, q, canopy, east_col, west_col, drag, lat):
    lane = lanes()
    sub = lax.broadcasted_iota(i32, (8, 128), 0)
    first, last = lane == 0, lane == 127
    rows = pl.ds(pl.multiple_of(8 * m, 8), 8)
    east_halo, west_halo = east_col[rows, :], west_col[rows, :]
    kind = [canopy[rows, c * 128 : (c + 1) * 128] for c in range(2)]
    row = (lat * CJ + 8 * m + sub).astype(f32)
    cor = 4.0 * (2.0 * (row + 0.5) / (CJ * NLAT) - 1.0)
    for c in range(2):
        elim = [None] * NF
        gx = gy = None
        for k in range(K):
            C, E, W, N, S = ([None] * NF for _ in range(5))
            for f in range(NF):
                fk = f * K + k
                mine, other = (buf[d, fk, pl.ds(pl.multiple_of(8 + 8 * m, 8), 8), :] for d in (c, 1 - c))
                C[f] = mine
                N[f] = buf[c, fk, pl.ds(9 + 8 * m, 8), :]
                S[f] = buf[c, fk, pl.ds(7 + 8 * m, 8), :]
                if c == 0:
                    E[f] = pltpu.roll(jnp.where(first, other, mine), 127, 1)
                    W[f] = jnp.where(first, pltpu.roll(west_halo, (1 - fk) % 128, 1), pltpu.roll(mine, 1, 1))
                else:
                    E[f] = jnp.where(last, pltpu.roll(east_halo, (127 - fk) % 128, 1), pltpu.roll(mine, 127, 1))
                    W[f] = pltpu.roll(jnp.where(last, other, mine), 1, 1)
            u, v = C[2], C[3]
            eE = (0.4 - u) - E[2]
            eW = (0.4 + u) + W[2]
            eN = (0.4 - v) - N[3]
            eS = (0.4 + v) + S[3]
            mid = 36.8 + ((eE + eW) + (eN + eS))
            new = [(C[f] * mid + E[f] * eE) + (W[f] * eW + N[f] * eN) + S[f] * eS for f in range(NF)]
            hx = 0.4 * (E[1] - W[1]) - 0.1 * (E[0] - W[0])
            hy = 0.4 * (N[1] - S[1]) - 0.1 * (N[0] - S[0])
            px = hx if k == 0 else gx + hx
            py = hy if k == 0 else gy + hy
            gx, gy = px + hx, py + hy
            new[2] = new[2] + (cor * v - px)
            new[3] = new[3] - (cor * u + py)
            if k > 0:
                x = new[2] * new[2] + (new[3] * new[3] + 0.01 * SCALE * SCALE)
                damp = 1.0 / (1.0 + take(drag[k], kind[c], 0) * (x * lax.rsqrt(x)))
                new[2], new[3] = new[2] * damp, new[3] * damp
            for f in range(NF):
                if k > 1:
                    new[f] = new[f] + FWD[k] * elim[f]
                elim[f] = new[f]
                q[m, f * K + k, c * 8 : (c + 1) * 8, :] = new[f]


def drag_levels(table, drag):
    for k in range(K):
        drag[k] = jnp.broadcast_to(table[:, k : k + 1] * (0.1 / SCALE), (8, 128))


def ice_messages(ilist, wlist, area, itemp, icond, ivel, msg, itab, ipack, igot):
    @pl.loop(0, 64, step=8)
    def _(t):
        for j in range(8):
            gather(t + j, ipack, itab, 4, 32, igot)

    areas = jnp.broadcast_to(jnp.concatenate([area[...], area[...]], axis=1), (8, 128))
    for g in range(8):
        for f in range(4):
            even, odd = unpack(igot, f, g)
            msg[pl.ds(128 * g + 2 + f, 8, stride=16), :] = even
            msg[pl.ds(128 * g + 10 + f, 8, stride=16), :] = odd
    for g in range(16):
        index = wlist[8 * g : 8 * g + 8, :]
        value = jnp.where(index >= 0, take(areas, index & 63, 1), 0.0)
        msg[pl.ds(64 * g + 1, 8, stride=8), :] = value
        for f in range(SENT, ROWS):
            msg[pl.ds(64 * g + f, 8, stride=8), :] = jnp.zeros((8, 128), f32)


def stencil_kernel(
    operands, _, st, tuv, ilist, wlist, area, itemp, icond, ivel, canopy, table, rowlo, rowhi, colw, cole,
    q_any, inb, out,
    buf, q, drag, msg, temps, itab, ipack, igot, mid_a, mid_b, north, south, east_col, west_col, sems, hops, halo_send, halo_recv,
):
    lon, lat = lax.axis_index("lon"), lax.axis_index("lat")
    loads = [
        [
            pltpu.make_async_copy(
                st.at[:, 32 * g : 32 * g + 32, c * 128 : (c + 1) * 128],
                buf.at[c, :, 8 + 32 * g : 40 + 32 * g, :],
                sems.at[g, c],
            )
            for c in range(2)
        ]
        for g in range(4)
    ]
    surface = pltpu.make_async_copy(tuv.at[0:128], temps, hops.at[13])
    surface.start()
    barrier = pltpu.get_barrier_semaphore()
    for i in range(1, NLON):
        pl.semaphore_signal(barrier, inc=1, device_id=(lax.rem(lon + i, NLON), lat), device_id_type=MESH)
    for i in range(1, NLAT):
        pl.semaphore_signal(barrier, inc=1, device_id=(lon, lax.rem(lat + i, NLAT)), device_id_type=MESH)
    for copy in operands:
        copy.wait()
    for pair in loads:
        for copy in pair:
            copy.start()
    pack_list(ilist, ipack)
    for f in range(4):
        for c in range(2):
            if f < 2:
                x = (icond, itemp)[f][pl.ds(c, 32, stride=2), :]
            else:
                x = ivel[pl.ds(2 * c + f - 2, 32, stride=4), :]
            high, low = split(x)
            itab[32 * f : 32 * f + 32, c * 128 : (c + 1) * 128] = high
            itab[128 + 32 * f : 160 + 32 * f, c * 128 : (c + 1) * 128] = low
    pl.semaphore_wait(barrier, NLON + NLAT - 2)

    def halo(src, dst, n, target):
        return pltpu.make_async_remote_copy(
            src_ref=src, dst_ref=dst, send_sem=halo_send.at[n], recv_sem=halo_recv.at[n],
            device_id=target, device_id_type=MESH,
        )

    to_west = halo(colw, east_col, 0, (lax.rem(lon + NLON - 1, NLON), lat))
    to_east = halo(cole, west_col, 1, (lax.rem(lon + 1, NLON), lat))
    to_north = halo(rowhi, south, 2, (lon, lax.rem(lat + 1, NLAT)))
    to_south = halo(rowlo, north, 3, (lon, lax.rem(lat + NLAT - 1, NLAT)))
    to_fold = halo(rowhi, north, 3, (NLON - 1 - lon, lat))
    to_west.start()
    to_east.start()
    to_north.start()

    @pl.when(lat > 0)
    def _():
        to_south.start()

    @pl.when(lat == NLAT - 1)
    def _():
        pltpu.make_async_remote_copy(
            src_ref=rowhi, dst_ref=north, send_sem=halo_send.at[4], recv_sem=halo_recv.at[3],
            device_id=(NLON - 1 - lon, lat), device_id_type=MESH,
        ).start()

    def hop(src, dst, n, target):
        return pltpu.make_async_remote_copy(
            src_ref=src, dst_ref=dst, send_sem=hops.at[n], recv_sem=hops.at[n + 1],
            device_id=target, device_id_type=MESH,
        )

    ice_messages(ilist, wlist, area, itemp, icond, ivel, msg, itab, ipack, igot)
    surface.wait()
    for g in range(16):
        msg[pl.ds(64 * g, 8, stride=8), :] = temps[8 * g : 8 * g + 8, :]
    keep = pltpu.make_async_copy(msg, out, hops.at[12])
    keep.start()
    even = lax.rem(lon + lat, 2) == 0
    by_a = msg.reshape(NLON, NLAT // 2, 2, ROWS, 128)
    by_b = msg.reshape(NLON // 2, 2, NLAT, ROWS, 128)

    def first_a(peer):
        return by_a.at[peer, :, lax.rem(peer, 2), 0:SENT], mid_a.at[lon, :, 0:SENT]

    def first_b(peer):
        return by_b.at[:, 1 - lax.rem(peer, 2), peer, 0:SENT], mid_b.at[lat, :, 0:SENT]

    for i in range(1, NLON):
        peer = lax.rem(lon + i, NLON)
        hop(*first_a(peer), 0, (peer, lat)).start()
    for i in range(1, NLAT):
        peer = lax.rem(lat + i, NLAT)
        hop(*first_b(peer), 2, (lon, peer)).start()
    own_a = pltpu.make_async_copy(*first_a(lon), hops.at[8])
    own_b = pltpu.make_async_copy(*first_b(lat), hops.at[9])
    own_a.start()
    own_b.start()
    in4 = inb.reshape(NLON, NLAT, ROWS, 128)

    def second_a(peer):
        return mid_a.at[:, peer // 2, 0:SENT], in4.at[:, lat, 0:SENT]

    def second_b(peer):
        return mid_b.at[:, peer // 2, 0:SENT], in4.at[lon, :, 0:SENT]

    def blocks(ref, n):
        part = ref.at[0:n, 0:SENT]
        return part, part

    def taken(n, sem):
        pltpu.make_async_copy(*blocks(inb, n), hops.at[sem]).wait()

    drag_levels(table, drag)
    to_west.wait_recv()
    to_east.wait_recv()
    to_north.wait_recv()
    to_fold.wait_recv()
    top = lat == NLAT - 1
    inside = jnp.where(lat > 0, 1.0, 0.0)
    back = 127 - lanes()
    for g in range(10):
        part = slice(8 * g, 8 * g + 8)
        sign = 1.0 if g < 5 else -1.0
        halves = [north[part, c * 128 : (c + 1) * 128] for c in range(2)]
        for c in range(2):
            turned = sign * take(halves[1 - c], back, 1)
            value = jnp.where(top, turned, halves[c])
            below = south[part, c * 128 : (c + 1) * 128] * inside
            for r in range(8):
                buf[c, 8 * g + r, 136:137, :] = value[r : r + 1]
                buf[c, 8 * g + r, 7:8, :] = below[r : r + 1]
    for copy in loads[0]:
        copy.wait()

    @pl.loop(0, 8)
    def _(g):
        @pl.when(lax.rem(g, 2) - jnp.where(g > 5, 1, 0) == 1)
        def _():
            for c in range(2):
                pltpu.make_async_copy(
                    st.at[:, 0:32, 0:128], buf.at[c, :, 8:40, :], sems.at[g // 2 + 1, c]
                ).wait()

        @pl.when(g == 3)
        def _():
            taken((NLON - 1) * NLAT // 2, 1)
            taken((NLAT - 1) * NLON // 2, 3)
            own_a.wait()
            own_b.wait()

            @pl.when(even)
            def _():
                pltpu.make_async_copy(*second_a(lat), hops.at[10]).start()
                for i in range(2, NLAT, 2):
                    peer = lax.rem(lat + i, NLAT)
                    hop(*second_a(peer), 4, (lon, peer)).start()
                for i in range(1, NLON, 2):
                    peer = lax.rem(lon + i, NLON)
                    hop(*second_b(peer), 6, (peer, lat)).start()

            @pl.when(jnp.logical_not(even))
            def _():
                pltpu.make_async_copy(*second_b(lon), hops.at[11]).start()
                for i in range(1, NLAT, 2):
                    peer = lax.rem(lat + i, NLAT)
                    hop(*second_a(peer), 4, (lon, peer)).start()
                for i in range(2, NLON, 2):
                    peer = lax.rem(lon + i, NLON)
                    hop(*second_b(peer), 6, (peer, lat)).start()

        for j in range(2):
            stencil_row(2 * g + j, buf, q, canopy, east_col, west_col, drag, lat)
        for j in range(2):
            pltpu.make_async_copy(q.at[2 * g + j], q_any.at[2 * g + j], hops.at[14]).start()

    pltpu.make_async_copy(q, q_any, hops.at[14]).wait()
    keep.wait()
    @pl.when(even)
    def _():
        taken((NLAT - 1) * NLON, 5)
        taken(NLON, 10)
        taken((NLAT // 2 - 1) * NLON, 4)
        taken((NLON // 2) * NLAT, 6)

    @pl.when(jnp.logical_not(even))
    def _():
        taken((NLON - 1) * NLAT, 7)
        taken(NLAT, 11)
        taken((NLAT // 2) * NLON, 4)
        taken((NLON // 2 - 1) * NLAT, 6)

    taken((NLON - 1) * NLAT // 2, 0)
    taken((NLAT - 1) * NLON // 2, 2)
    to_west.wait_send()
    to_east.wait_send()
    to_north.wait_send()

    @pl.when(lat > 0)
    def _():
        to_south.wait_send()

    @pl.when(lat == NLAT - 1)
    def _():
        pltpu.make_async_copy(rowhi, rowhi, halo_send.at[4]).wait()


def finish_kernel(
    loads, stores, st, olist_any, ilist_any, q_any, inb, out, tuv, olist, ilist, canopy, table, itemp,
    y, itemp_next,
    q, ybuf, salt, drag, opack, ipack, oval, ival, oacc, iacc, owide, ocols, iwide, icols, oflag, iflag, sems,
):
    flags = [
        pltpu.make_async_copy(olist_any, oflag, sems.at[0]),
        pltpu.make_async_copy(ilist_any, iflag, sems.at[1]),
    ]
    salts = [
        pltpu.make_async_copy(st.at[K, :, c * 128 : (c + 1) * 128], salt.at[c], sems.at[2 + c])
        for c in range(2)
    ]
    state = pltpu.make_async_copy(q_any, q, sems.at[6])
    oacc[...] = jnp.zeros_like(oacc)
    iacc[...] = jnp.zeros_like(iacc)
    for copy in loads[3:5]:
        copy.wait()
    pack_list(olist, opack)
    pack_list(ilist, ipack)
    for copy in loads[0:3] + loads[5:]:
        copy.wait()
    for copy in flags + salts + [state]:
        copy.start()
    drag_levels(table, drag)
    for g in range(8):
        sides, ices = [], []
        for odd in range(2):
            block = lambda ref, f: ref[pl.ds(128 * g + 8 * odd + f, 8, stride=16), :]
            slot = [tuv[pl.ds(128 * n + 16 * g + odd, 8, stride=2), :] for n in range(3)]
            a, cond, temp, iu, iv = (block(inb, f) for f in range(1, 6))
            du, dv = iu - slot[1], iv - slot[2]
            x = du * du + dv * dv + 0.01
            drift = 0.5 * a * (x * lax.rsqrt(x))
            heat = a * cond
            sides.append([heat * (temp - slot[0]), heat, drift * du, drift * dv])
            ices.append(block(out, 1) * block(out, 2) * (block(out, 3) - block(inb, 0)))
        for f in range(4):
            first, second = pack(sides[0][f], sides[1][f])
            oval[128 * f + 8 * g : 128 * f + 8 * g + 8, :] = first
            oval[128 * f + 64 + 8 * g : 128 * f + 72 + 8 * g, :] = second
        first, second = pack(*ices)
        ival[8 * g : 8 * g + 8, :] = first
        ival[64 + 8 * g : 72 + 8 * g, :] = second

    def hot_columns(tile, packed, width, cols):
        for h in range(4):
            index = packed[pl.ds(4 * tile + h, 1), :] & (width - 1)
            cols[:, 128 * h : 128 * h + 128] = jnp.where(one_hot(index, width), 1.0, 0.0).astype(bf16)

    def add(wide, cols, acc):
        acc[...] += lax.dot_general(wide, cols, (((1,), (1,)), ((), ())), preferred_element_type=f32)

    def scatter_ocean(tile, p=0):
        hot_columns(tile, opack, CI, ocols.at[p])
        for h in range(4):
            mask = one_hot(opack[pl.ds(4 * tile + h, 1), :] >> 8, CJ)
            for f in range(4):
                value = oval[pl.ds(128 * f + 4 * tile + h, 1), :]
                high = value.astype(bf16).astype(f32)
                for n, part in enumerate((high, value - high)):
                    part = jnp.where(mask, jnp.broadcast_to(part, (CJ, 128)), 0.0).astype(bf16)
                    owide[p, 512 * n + CJ * f : 512 * n + CJ * (f + 1), 128 * h : 128 * h + 128] = part
        add(owide[p], ocols[p], oacc)

    def scatter_ice(tile, p=0):
        hot_columns(tile, ipack, 128, icols.at[p])
        for h in range(4):
            mask = one_hot(ipack[pl.ds(4 * tile + h, 1), :] >> 7, 64)
            value = ival[pl.ds(4 * tile + h, 1), :]
            high = value.astype(bf16).astype(f32)
            for n, part in enumerate((high, value - high)):
                part = jnp.where(mask, jnp.broadcast_to(part, (64, 128)), 0.0).astype(bf16)
                iwide[p, 64 * n : 64 * n + 64, 128 * h : 128 * h + 128] = part
        add(iwide[p], icols[p], iacc)

    @pl.loop(0, 16, step=4)
    def _(t):
        for j in range(4):
            scatter_ocean(t + j, j)
            scatter_ice(t + j, j)

    for copy in flags:
        copy.wait()

    @pl.loop(0, 16)
    def _(t):
        @pl.when(long_pairs(oflag, 8 * t, 8))
        def _():
            scatter_ocean(16 + t)


    @pl.loop(0, 16, step=4)
    def _(t):
        @pl.when(long_pairs(iflag, 8 * t, 32))
        def _():
            for j in range(4):
                scatter_ice(16 + t + j, j)

    itemp_next[...] = itemp[...] - 0.25 * (iacc[0:64, :] + iacc[64:128, :])
    stores[0].start()
    for copy in salts + [state]:
        copy.wait()

    @pl.loop(0, 16)
    def _(m):
        rows = pl.ds(pl.multiple_of(8 * m, 8), 8)
        sides = []
        for c in range(2):
            here = slice(8 * c, 8 * c + 8)
            flux = []
            for f in range(4):
                high, low = (pl.ds(pl.multiple_of(part + CJ * f + 8 * m, 8), 8) for part in (0, 4 * CJ))
                flux.append(oacc[high, c * 128 : (c + 1) * 128] + oacc[low, c * 128 : (c + 1) * 128])
            top = [q[m, f * K, here, :] for f in range(4)]
            top[0] = top[0] + 20.0 * flux[0]
            top[1] = top[1] - 10.0 * (salt[c, rows, :] * flux[1])
            top[2] = top[2] + 20.0 * flux[2]
            top[3] = top[3] + 20.0 * flux[3]
            x = top[2] * top[2] + (top[3] * top[3] + 0.01 * SCALE * SCALE)
            damp = 1.0 / (1.0 + take(drag[0], canopy[rows, c * 128 : (c + 1) * 128], 0) * (x * lax.rsqrt(x)))
            top[2], top[3] = top[2] * damp, top[3] * damp
            sides.append(top)
        solved = [[None] * 4 for _ in range(2)]
        for k in range(K - 1, -1, -1):
            for c in range(2):
                for f in range(4):
                    here = slice(8 * c, 8 * c + 8)
                    value = sides[c][f] if k == 0 else q[m, f * K + k, here, :] + TOP[k] * sides[c][f]
                    value = value * (1.0 / (SCALE * DIAG[k]))
                    if k < K - 1:
                        value = value + (0.5 / DIAG[k]) * solved[c][f]
                    solved[c][f] = value
                    ybuf[m, f * K + k, here, :] = value
        for c in range(2):
            pltpu.make_async_copy(
                ybuf.at[m, :, 8 * c : 8 * c + 8, :], y.at[:, rows, c * 128 : (c + 1) * 128], sems.at[4 + c]
            ).start()

    for c in range(2):
        part = y.at[:, :, c * 128 : (c + 1) * 128]
        pltpu.make_async_copy(part, part, sems.at[4 + c]).wait()


def staged(kernel, args, moved, outs, kept, scratch, **options):
    count, given = len(args), len(outs)

    def body(*refs):
        ins, results, rest = list(refs[:count]), list(refs[count : count + given]), list(refs[count + given :])
        sems = rest.pop()
        loads, stores = [], []
        for i in moved:
            place = rest.pop(0)
            loads.append(pltpu.make_async_copy(ins[i], place, sems.at[len(loads)]))
            ins[i] = place
        for i in range(given):
            if i not in kept:
                place = rest.pop(0)
                stores.append(pltpu.make_async_copy(place, results[i], sems.at[len(loads) + len(stores)]))
                results[i] = place
        for copy in loads:
            copy.start()
        kernel(loads, stores, *ins, *results, *rest)
        for copy in stores:
            copy.wait()

    places = [pltpu.VMEM(args[i].shape, args[i].dtype) for i in moved]
    places += [pltpu.VMEM(o.shape, o.dtype) for i, o in enumerate(outs) if i not in kept]
    return pl.pallas_call(
        body,
        out_shape=outs,
        in_specs=[ANY] * count,
        out_specs=(ANY,) * given,
        scratch_shapes=places + scratch + [pltpu.SemaphoreType.DMA((len(places),))],
        **options,
    )(*args)


def shards(
    ocean_state, canopy_type, drag_table, ocean_list, ice_list, weight_list, area_table, ice_temp, ice_cond, ice_vel
):
    st = ocean_state.reshape(FK, CJ, CI)
    olist, ilist, wlist = (x.reshape(DEV, SLOTS) for x in (ocean_list, ice_list, weight_list))
    itemp, icond = (x.reshape(64, 128) for x in (ice_temp, ice_cond))
    ivel = ice_vel.reshape(2, 64, 128).transpose(1, 0, 2).reshape(128, 128)
    area = area_table.reshape(1, 64)
    S = jax.ShapeDtypeStruct
    V = pltpu.VMEM
    tuv, rowlo, rowhi, colw, cole = staged(
        gather_kernel,
        (st, olist, olist),
        (2,),
        (S((3 * 128, 128), f32), S((FK, CI), f32), S((FK, CI), f32), S((CJ, 128), f32), S((CJ, 128), f32)),
        (),
        [
            V((2, FK, CJ, 128), f32), V((3, 2, CJ, 128), f32), V((768, 256), bf16), V((128, 128), i32),
            V((3 * 128, 128), f32), pltpu.SMEM((128, 128), i32), pltpu.SemaphoreType.DMA((4,)),
        ],
        compiler_params=pltpu.CompilerParams(vmem_limit_bytes=LIMIT),
        name="gather_slots",
    )
    q, inb, out = staged(
        stencil_kernel,
        (st, tuv, ilist, wlist, area, itemp, icond, ivel, canopy_type, drag_table, rowlo, rowhi, colw, cole),
        range(2, 10),
        (S((16, FK, 16, 128), f32), S((DEV, ROWS, 128), f32), S((DEV * ROWS, 128), f32)),
        range(3),
        [
            V((2, FK, 144, 128), f32), V((16, FK, 16, 128), f32), V((K, 8, 128), f32), V((DEV * ROWS, 128), f32),
            V((128, 128), f32), V((256, 256), bf16), V((128, 128), i32), V((4 * 128, 128), f32),
            V((NLON, NLAT // 2, ROWS, 128), f32), V((NLAT, NLON // 2, ROWS, 128), f32),
            V((FK, CI), f32), V((FK, CI), f32), V((CJ, 128), f32), V((CJ, 128), f32),
            pltpu.SemaphoreType.DMA((4, 2)), pltpu.SemaphoreType.DMA((15,)),
            pltpu.SemaphoreType.DMA((5,)), pltpu.SemaphoreType.DMA((4,)),
        ],
        compiler_params=pltpu.CompilerParams(vmem_limit_bytes=LIMIT, collective_id=0, has_side_effects=True),
        name="exchange_stencil",
    )
    y, itemp_next = staged(
        finish_kernel,
        (st, olist, ilist, q, inb.reshape(DEV * ROWS, 128), out, tuv, olist, ilist, canopy_type, drag_table, itemp),
        range(4, 12),
        (S((FK, CJ, CI), f32), S((64, 128), f32)),
        (0,),
        [
            V((16, FK, 16, 128), f32), V((16, FK, 16, 128), f32), V((2, CJ, 128), f32), V((K, 8, 128), f32),
            V((128, 128), i32), V((128, 128), i32), V((4 * 128, 128), f32), V((128, 128), f32),
            V((8 * CJ, CI), f32), V((128, 128), f32), V((4, 8 * CJ, 512), bf16), V((4, CI, 512), bf16),
            V((4, 128, 512), bf16), V((4, 128, 512), bf16),
            pltpu.SMEM((128, 128), i32), pltpu.SMEM((128, 128), i32), pltpu.SemaphoreType.DMA((7,)),
        ],
        compiler_params=pltpu.CompilerParams(vmem_limit_bytes=LIMIT),
        name="scatter_solve",
    )
    return y.reshape(ocean_state.shape), itemp_next.reshape(ice_temp.shape)


def solution(mesh):
    return jax.shard_map(
        shards,
        mesh=mesh,
        in_specs=(
            P(None, None, "lat", "lon"),
            P("lat", "lon"),
            P(),
            P(("lon", "lat"), None),
            P(("lon", "lat"), None),
            P(("lon", "lat"), None),
            P(),
            P(("lon", "lat"), None),
            P(("lon", "lat"), None),
            P(("lon", "lat"), None, None),
        ),
        out_specs=(P(None, None, "lat", "lon"), P(("lon", "lat"), None)),
        check_vma=False,
    )
```

```python
import functools

import jax
import jax.numpy as jnp
from jax import lax
from jax.experimental import pallas as pl
from jax.experimental.pallas import tpu as pltpu
from jax.sharding import PartitionSpec as P

f32 = jnp.float32
bf16 = jnp.bfloat16
i32 = jnp.int32
MESH = pl.DeviceIdType.MESH
K = 20
NF = 4
FK = NF * K
CJ = 128
CI = 256
NLON = 16
NLAT = 8
DEV = NLON * NLAT
SLOTS = 128
ROWS = 8
SENT = 6
SCALE = 40.0

DIAG = [1.5]
for _k in range(1, K):
    DIAG.append((1.5 if _k == K - 1 else 2.0) - 0.25 / DIAG[-1])
FWD = [0.0] + [0.5 / DIAG[_k - 1] for _k in range(1, K)]
TOP = [1.0]
for _k in range(1, K):
    TOP.append(FWD[_k] * TOP[-1])

ANY = pl.BlockSpec(memory_space=pl.ANY)
LIMIT = 60 << 20


def lanes():
    return lax.broadcasted_iota(i32, (8, 128), 1)


def take(table, index, axis):
    return jnp.take_along_axis(table, index, axis=axis, mode="promise_in_bounds")


def split(x):
    high = x.astype(bf16)
    return high, (x - high.astype(f32)).astype(bf16)


def one_hot(index, count):
    rows = lax.broadcasted_iota(i32, (count, index.shape[1]), 0)
    return rows == jnp.broadcast_to(index, (count, index.shape[1]))


def pack(even, odd):
    left = lanes() < 64
    return (
        jnp.where(left, even, pltpu.roll(odd, 64, 1)),
        jnp.where(left, pltpu.roll(even, 64, 1), odd),
    )


def pack_list(source, packed):
    for g in range(8):
        first, second = pack(
            source[pl.ds(16 * g, 8, stride=2), :], source[pl.ds(16 * g + 1, 8, stride=2), :]
        )
        packed[8 * g : 8 * g + 8, :] = first
        packed[64 + 8 * g : 72 + 8 * g, :] = second


def long_pairs(flags, first, count):
    most = flags[first, 64]
    for i in range(1, count):
        most = jnp.maximum(most, flags[first + i, 64])
    return most >= 0


def gather(tile, packed, table, fields, rows, got):
    hots, his = [], []
    for h in range(2):
        row = packed[pl.ds(2 * tile + h, 1), :]
        his.append(row >> 8)
        hots.append(jnp.where(one_hot(row & 255, 256), 1.0, 0.0).astype(bf16))
    res = jnp.dot(table[...], jnp.concatenate(hots, axis=1), preferred_element_type=f32)
    half = fields * rows
    res = res[:half] + res[half:]
    for h in range(2):
        mask = one_hot(his[h], rows)
        for f in range(fields):
            value = jnp.where(mask, res[f * rows : (f + 1) * rows, h * 128 : (h + 1) * 128], 0.0)
            got[pl.ds(f * 128 + 2 * tile + h, 1), :] = jnp.sum(value, axis=0, keepdims=True)


def unpack(got, f, g):
    left = lanes() < 64
    first = got[f * 128 + 8 * g : f * 128 + 8 * g + 8, :]
    second = got[f * 128 + 64 + 8 * g : f * 128 + 72 + 8 * g, :]
    return (
        jnp.where(left, first, pltpu.roll(second, 64, 1)),
        jnp.where(left, pltpu.roll(first, 64, 1), second),
    )


def gather_kernel(
    loads, stores, st, olist_any, olist,
    tuv, rowlo, rowhi, colw, cole,
    full, surf, otab, opack, ogot, oflag, sems,
):
    flags = pltpu.make_async_copy(olist_any, oflag, sems.at[0])
    tops = [
        pltpu.make_async_copy(st.at[f * K, :, c * 128 : (c + 1) * 128], surf.at[n, c], sems.at[1])
        for n, f in enumerate((0, 2, 3))
        for c in range(2)
    ]
    state = [
        pltpu.make_async_copy(st.at[:, :, c * 128 : (c + 1) * 128], full.at[c], sems.at[2 + c]) for c in range(2)
    ]
    for copy in tops:
        copy.start()
    loads[0].wait()
    pack_list(olist, opack)
    ogot[...] = jnp.zeros_like(ogot)
    pltpu.make_async_copy(surf, surf, sems.at[1]).wait()
    for copy in [flags] + state:
        copy.start()
    for n in range(3):
        for c in range(2):
            high, low = split(surf[n, c])
            otab[128 * n : 128 * n + 128, c * 128 : (c + 1) * 128] = high
            otab[384 + 128 * n : 512 + 128 * n, c * 128 : (c + 1) * 128] = low

    def columns(m):
        lane = lanes()
        rows = pl.ds(pl.multiple_of(8 * m, 8), 8)
        west = jnp.zeros((8, 128), f32)
        east = jnp.zeros((8, 128), f32)
        for fk in range(FK):
            both = jnp.where(lane == 127, full[1, fk, rows, :], full[0, fk, rows, :])
            both = pltpu.roll(both, fk, 1) if fk else both
            west = jnp.where(lane == fk, both, west)
            east = jnp.where(lane == (fk - 1) % 128, both, east)
        colw[rows, :] = west
        cole[rows, :] = east

    @pl.loop(0, 4)
    def _(t):
        for j in range(4):
            gather(4 * t + j, opack, otab, 3, 128, ogot)

    for copy in state:
        copy.wait()

    @pl.loop(4, 8)
    def _(t):
        for j in range(4):
            gather(4 * t + j, opack, otab, 3, 128, ogot)
        for j in range(4):
            columns(4 * (t - 4) + j)

    for fk in range(FK):
        for c in range(2):
            rowlo[fk : fk + 1, c * 128 : (c + 1) * 128] = full[c, fk, 0:1, :]
            rowhi[fk : fk + 1, c * 128 : (c + 1) * 128] = full[c, fk, 127:128, :]
    for copy in stores[1:]:
        copy.start()
    flags.wait()

    @pl.loop(0, 32)
    def _(t):
        @pl.when(long_pairs(oflag, 4 * t, 4))
        def _():
            gather(32 + t, opack, otab, 3, 128, ogot)

    for g in range(8):
        for n in range(3):
            even, odd = unpack(ogot, n, g)
            tuv[pl.ds(128 * n + 16 * g, 8, stride=2), :] = even
            tuv[pl.ds(128 * n + 16 * g + 1, 8, stride=2), :] = odd
    stores[0].start()


def stencil_row(m, buf, q, canopy, east_col, west_col, drag, lat):
    lane = lanes()
    sub = lax.broadcasted_iota(i32, (8, 128), 0)
    first, last = lane == 0, lane == 127
    rows = pl.ds(pl.multiple_of(8 * m, 8), 8)
    east_halo, west_halo = east_col[rows, :], west_col[rows, :]
    kind = [canopy[rows, c * 128 : (c + 1) * 128] for c in range(2)]
    row = (lat * CJ + 8 * m + sub).astype(f32)
    cor = 4.0 * (2.0 * (row + 0.5) / (CJ * NLAT) - 1.0)
    for c in range(2):
        elim = [None] * NF
        gx = gy = None
        for k in range(K):
            C, E, W, N, S = ([None] * NF for _ in range(5))
            for f in range(NF):
                fk = f * K + k
                mine, other = (buf[d, fk, pl.ds(pl.multiple_of(8 + 8 * m, 8), 8), :] for d in (c, 1 - c))
                C[f] = mine
                N[f] = buf[c, fk, pl.ds(9 + 8 * m, 8), :]
                S[f] = buf[c, fk, pl.ds(7 + 8 * m, 8), :]
                if c == 0:
                    E[f] = pltpu.roll(jnp.where(first, other, mine), 127, 1)
                    W[f] = jnp.where(first, pltpu.roll(west_halo, (1 - fk) % 128, 1), pltpu.roll(mine, 1, 1))
                else:
                    E[f] = jnp.where(last, pltpu.roll(east_halo, (127 - fk) % 128, 1), pltpu.roll(mine, 127, 1))
                    W[f] = pltpu.roll(jnp.where(last, other, mine), 1, 1)
            u, v = C[2], C[3]
            eE = (0.4 - u) - E[2]
            eW = (0.4 + u) + W[2]
            eN = (0.4 - v) - N[3]
            eS = (0.4 + v) + S[3]
            mid = 36.8 + ((eE + eW) + (eN + eS))
            new = [(C[f] * mid + E[f] * eE) + (W[f] * eW + N[f] * eN) + S[f] * eS for f in range(NF)]
            hx = 0.4 * (E[1] - W[1]) - 0.1 * (E[0] - W[0])
            hy = 0.4 * (N[1] - S[1]) - 0.1 * (N[0] - S[0])
            px = hx if k == 0 else gx + hx
            py = hy if k == 0 else gy + hy
            gx, gy = px + hx, py + hy
            new[2] = new[2] + (cor * v - px)
            new[3] = new[3] - (cor * u + py)
            if k > 0:
                x = new[2] * new[2] + (new[3] * new[3] + 0.01 * SCALE * SCALE)
                damp = 1.0 / (1.0 + take(drag[k], kind[c], 0) * (x * lax.rsqrt(x)))
                new[2], new[3] = new[2] * damp, new[3] * damp
            for f in range(NF):
                if k > 1:
                    new[f] = new[f] + FWD[k] * elim[f]
                elim[f] = new[f]
                q[m, f * K + k, c * 8 : (c + 1) * 8, :] = new[f]


def drag_levels(table, drag):
    for k in range(K):
        drag[k] = jnp.broadcast_to(table[:, k : k + 1] * (0.1 / SCALE), (8, 128))


def ice_messages(ilist, wlist, area, itemp, icond, ivel, msg, itab, ipack, igot):
    @pl.loop(0, 64, step=8)
    def _(t):
        for j in range(8):
            gather(t + j, ipack, itab, 4, 32, igot)

    areas = jnp.broadcast_to(jnp.concatenate([area[...], area[...]], axis=1), (8, 128))
    for g in range(8):
        for f in range(4):
            even, odd = unpack(igot, f, g)
            msg[pl.ds(128 * g + 2 + f, 8, stride=16), :] = even
            msg[pl.ds(128 * g + 10 + f, 8, stride=16), :] = odd
    for g in range(16):
        index = wlist[8 * g : 8 * g + 8, :]
        value = jnp.where(index >= 0, take(areas, index & 63, 1), 0.0)
        msg[pl.ds(64 * g + 1, 8, stride=8), :] = value
        for f in range(SENT, ROWS):
            msg[pl.ds(64 * g + f, 8, stride=8), :] = jnp.zeros((8, 128), f32)


def stencil_kernel(
    operands, _, st, tuv, ilist, wlist, area, itemp, icond, ivel, canopy, table, rowlo, rowhi, colw, cole,
    q_any, inb, out,
    buf, q, drag, msg, temps, itab, ipack, igot, mid_a, mid_b, north, south, east_col, west_col, sems, hops, halo_send, halo_recv,
):
    lon, lat = lax.axis_index("lon"), lax.axis_index("lat")
    loads = [
        [
            pltpu.make_async_copy(
                st.at[:, 32 * g : 32 * g + 32, c * 128 : (c + 1) * 128],
                buf.at[c, :, 8 + 32 * g : 40 + 32 * g, :],
                sems.at[g, c],
            )
            for c in range(2)
        ]
        for g in range(4)
    ]
    surface = pltpu.make_async_copy(tuv.at[0:128], temps, hops.at[13])
    surface.start()
    barrier = pltpu.get_barrier_semaphore()
    for i in range(1, NLON):
        pl.semaphore_signal(barrier, inc=1, device_id=(lax.rem(lon + i, NLON), lat), device_id_type=MESH)
    for i in range(1, NLAT):
        pl.semaphore_signal(barrier, inc=1, device_id=(lon, lax.rem(lat + i, NLAT)), device_id_type=MESH)
    for copy in operands:
        copy.wait()
    for pair in loads:
        for copy in pair:
            copy.start()
    pack_list(ilist, ipack)
    for f in range(4):
        for c in range(2):
            if f < 2:
                x = (icond, itemp)[f][pl.ds(c, 32, stride=2), :]
            else:
                x = ivel[pl.ds(2 * c + f - 2, 32, stride=4), :]
            high, low = split(x)
            itab[32 * f : 32 * f + 32, c * 128 : (c + 1) * 128] = high
            itab[128 + 32 * f : 160 + 32 * f, c * 128 : (c + 1) * 128] = low
    pl.semaphore_wait(barrier, NLON + NLAT - 2)

    def halo(src, dst, n, target):
        return pltpu.make_async_remote_copy(
            src_ref=src, dst_ref=dst, send_sem=halo_send.at[n], recv_sem=halo_recv.at[n],
            device_id=target, device_id_type=MESH,
        )

    to_west = halo(colw, east_col, 0, (lax.rem(lon + NLON - 1, NLON), lat))
    to_east = halo(cole, west_col, 1, (lax.rem(lon + 1, NLON), lat))
    to_north = halo(rowhi, south, 2, (lon, lax.rem(lat + 1, NLAT)))
    to_south = halo(rowlo, north, 3, (lon, lax.rem(lat + NLAT - 1, NLAT)))
    to_fold = halo(rowhi, north, 3, (NLON - 1 - lon, lat))
    to_west.start()
    to_east.start()
    to_north.start()

    @pl.when(lat > 0)
    def _():
        to_south.start()

    @pl.when(lat == NLAT - 1)
    def _():
        pltpu.make_async_remote_copy(
            src_ref=rowhi, dst_ref=north, send_sem=halo_send.at[4], recv_sem=halo_recv.at[3],
            device_id=(NLON - 1 - lon, lat), device_id_type=MESH,
        ).start()

    def hop(src, dst, n, target):
        return pltpu.make_async_remote_copy(
            src_ref=src, dst_ref=dst, send_sem=hops.at[n], recv_sem=hops.at[n + 1],
            device_id=target, device_id_type=MESH,
        )

    ice_messages(ilist, wlist, area, itemp, icond, ivel, msg, itab, ipack, igot)
    surface.wait()
    for g in range(16):
        msg[pl.ds(64 * g, 8, stride=8), :] = temps[8 * g : 8 * g + 8, :]
    keep = pltpu.make_async_copy(msg, out, hops.at[12])
    keep.start()
    even = lax.rem(lon + lat, 2) == 0
    by_a = msg.reshape(NLON, NLAT // 2, 2, ROWS, 128)
    by_b = msg.reshape(NLON // 2, 2, NLAT, ROWS, 128)

    def first_a(peer):
        return by_a.at[peer, :, lax.rem(peer, 2), 0:SENT], mid_a.at[lon, :, 0:SENT]

    def first_b(peer):
        return by_b.at[:, 1 - lax.rem(peer, 2), peer, 0:SENT], mid_b.at[lat, :, 0:SENT]

    for i in range(1, NLON):
        peer = lax.rem(lon + i, NLON)
        hop(*first_a(peer), 0, (peer, lat)).start()
    for i in range(1, NLAT):
        peer = lax.rem(lat + i, NLAT)
        hop(*first_b(peer), 2, (lon, peer)).start()
    own_a = pltpu.make_async_copy(*first_a(lon), hops.at[8])
    own_b = pltpu.make_async_copy(*first_b(lat), hops.at[9])
    own_a.start()
    own_b.start()
    in4 = inb.reshape(NLON, NLAT, ROWS, 128)

    def second_a(peer):
        return mid_a.at[:, peer // 2, 0:SENT], in4.at[:, lat, 0:SENT]

    def second_b(peer):
        return mid_b.at[:, peer // 2, 0:SENT], in4.at[lon, :, 0:SENT]

    def blocks(ref, n):
        part = ref.at[0:n, 0:SENT]
        return part, part

    def taken(n, sem):
        pltpu.make_async_copy(*blocks(inb, n), hops.at[sem]).wait()

    drag_levels(table, drag)
    to_west.wait_recv()
    to_east.wait_recv()
    to_north.wait_recv()
    to_fold.wait_recv()
    top = lat == NLAT - 1
    inside = jnp.where(lat > 0, 1.0, 0.0)
    back = 127 - lanes()
    for g in range(10):
        part = slice(8 * g, 8 * g + 8)
        sign = 1.0 if g < 5 else -1.0
        halves = [north[part, c * 128 : (c + 1) * 128] for c in range(2)]
        for c in range(2):
            turned = sign * take(halves[1 - c], back, 1)
            value = jnp.where(top, turned, halves[c])
            below = south[part, c * 128 : (c + 1) * 128] * inside
            for r in range(8):
                buf[c, 8 * g + r, 136:137, :] = value[r : r + 1]
                buf[c, 8 * g + r, 7:8, :] = below[r : r + 1]
    for copy in loads[0]:
        copy.wait()

    @pl.loop(0, 8)
    def _(g):
        @pl.when(lax.rem(g, 2) - jnp.where(g > 5, 1, 0) == 1)
        def _():
            for c in range(2):
                pltpu.make_async_copy(
                    st.at[:, 0:32, 0:128], buf.at[c, :, 8:40, :], sems.at[g // 2 + 1, c]
                ).wait()

        @pl.when(g == 2)
        def _():
            taken((NLON - 1) * NLAT // 2, 1)
            taken((NLAT - 1) * NLON // 2, 3)
            own_a.wait()
            own_b.wait()

            @pl.when(even)
            def _():
                pltpu.make_async_copy(*second_a(lat), hops.at[10]).start()
                for i in range(2, NLAT, 2):
                    peer = lax.rem(lat + i, NLAT)
                    hop(*second_a(peer), 4, (lon, peer)).start()
                for i in range(1, NLON, 2):
                    peer = lax.rem(lon + i, NLON)
                    hop(*second_b(peer), 6, (peer, lat)).start()

            @pl.when(jnp.logical_not(even))
            def _():
                pltpu.make_async_copy(*second_b(lon), hops.at[11]).start()
                for i in range(1, NLAT, 2):
                    peer = lax.rem(lat + i, NLAT)
                    hop(*second_a(peer), 4, (lon, peer)).start()
                for i in range(2, NLON, 2):
                    peer = lax.rem(lon + i, NLON)
                    hop(*second_b(peer), 6, (peer, lat)).start()

        for j in range(2):
            stencil_row(2 * g + j, buf, q, canopy, east_col, west_col, drag, lat)
        for j in range(2):
            pltpu.make_async_copy(q.at[2 * g + j], q_any.at[2 * g + j], hops.at[14]).start()

    pltpu.make_async_copy(q, q_any, hops.at[14]).wait()
    keep.wait()
    @pl.when(even)
    def _():
        taken((NLAT - 1) * NLON, 5)
        taken(NLON, 10)
        taken((NLAT // 2 - 1) * NLON, 4)
        taken((NLON // 2) * NLAT, 6)

    @pl.when(jnp.logical_not(even))
    def _():
        taken((NLON - 1) * NLAT, 7)
        taken(NLAT, 11)
        taken((NLAT // 2) * NLON, 4)
        taken((NLON // 2 - 1) * NLAT, 6)

    taken((NLON - 1) * NLAT // 2, 0)
    taken((NLAT - 1) * NLON // 2, 2)
    to_west.wait_send()
    to_east.wait_send()
    to_north.wait_send()

    @pl.when(lat > 0)
    def _():
        to_south.wait_send()

    @pl.when(lat == NLAT - 1)
    def _():
        pltpu.make_async_copy(rowhi, rowhi, halo_send.at[4]).wait()


def finish_kernel(
    loads, stores, st, olist_any, ilist_any, q_any, inb, out, tuv, olist, ilist, canopy, table, itemp,
    y, itemp_next,
    q, ybuf, salt, drag, opack, ipack, oval, ival, oacc, iacc, owide, ocols, iwide, icols, oflag, iflag, sems,
):
    flags = [
        pltpu.make_async_copy(olist_any, oflag, sems.at[0]),
        pltpu.make_async_copy(ilist_any, iflag, sems.at[1]),
    ]
    salts = [
        pltpu.make_async_copy(st.at[K, :, c * 128 : (c + 1) * 128], salt.at[c], sems.at[2 + c])
        for c in range(2)
    ]
    state = pltpu.make_async_copy(q_any, q, sems.at[6])
    oacc[...] = jnp.zeros_like(oacc)
    iacc[...] = jnp.zeros_like(iacc)
    for copy in loads[3:5]:
        copy.wait()
    pack_list(olist, opack)
    pack_list(ilist, ipack)
    for copy in loads[0:3] + loads[5:]:
        copy.wait()
    for copy in flags + salts + [state]:
        copy.start()
    drag_levels(table, drag)
    for g in range(8):
        sides, ices = [], []
        for odd in range(2):
            block = lambda ref, f: ref[pl.ds(128 * g + 8 * odd + f, 8, stride=16), :]
            slot = [tuv[pl.ds(128 * n + 16 * g + odd, 8, stride=2), :] for n in range(3)]
            a, cond, temp, iu, iv = (block(inb, f) for f in range(1, 6))
            du, dv = iu - slot[1], iv - slot[2]
            x = du * du + dv * dv + 0.01
            drift = 0.5 * a * (x * lax.rsqrt(x))
            heat = a * cond
            sides.append([heat * (temp - slot[0]), heat, drift * du, drift * dv])
            ices.append(block(out, 1) * block(out, 2) * (block(out, 3) - block(inb, 0)))
        for f in range(4):
            first, second = pack(sides[0][f], sides[1][f])
            oval[128 * f + 8 * g : 128 * f + 8 * g + 8, :] = first
            oval[128 * f + 64 + 8 * g : 128 * f + 72 + 8 * g, :] = second
        first, second = pack(*ices)
        ival[8 * g : 8 * g + 8, :] = first
        ival[64 + 8 * g : 72 + 8 * g, :] = second

    def hot_columns(tile, packed, width, cols):
        for h in range(4):
            index = packed[pl.ds(4 * tile + h, 1), :] & (width - 1)
            cols[:, 128 * h : 128 * h + 128] = jnp.where(one_hot(index, width), 1.0, 0.0).astype(bf16)

    def add(wide, cols, acc):
        acc[...] += lax.dot_general(wide, cols, (((1,), (1,)), ((), ())), preferred_element_type=f32)

    def scatter_ocean(tile, p=0):
        hot_columns(tile, opack, CI, ocols.at[p])
        for h in range(4):
            mask = one_hot(opack[pl.ds(4 * tile + h, 1), :] >> 8, CJ)
            for f in range(4):
                value = oval[pl.ds(128 * f + 4 * tile + h, 1), :]
                high = value.astype(bf16).astype(f32)
                for n, part in enumerate((high, value - high)):
                    part = jnp.where(mask, jnp.broadcast_to(part, (CJ, 128)), 0.0).astype(bf16)
                    owide[p, 512 * n + CJ * f : 512 * n + CJ * (f + 1), 128 * h : 128 * h + 128] = part
        add(owide[p], ocols[p], oacc)

    def scatter_ice(tile, p=0):
        hot_columns(tile, ipack, 128, icols.at[p])
        for h in range(4):
            mask = one_hot(ipack[pl.ds(4 * tile + h, 1), :] >> 7, 64)
            value = ival[pl.ds(4 * tile + h, 1), :]
            high = value.astype(bf16).astype(f32)
            for n, part in enumerate((high, value - high)):
                part = jnp.where(mask, jnp.broadcast_to(part, (64, 128)), 0.0).astype(bf16)
                iwide[p, 64 * n : 64 * n + 64, 128 * h : 128 * h + 128] = part
        add(iwide[p], icols[p], iacc)

    @pl.loop(0, 16, step=4)
    def _(t):
        for j in range(4):
            scatter_ocean(t + j, j)
            scatter_ice(t + j, j)

    for copy in flags:
        copy.wait()

    @pl.loop(0, 16)
    def _(t):
        @pl.when(long_pairs(oflag, 8 * t, 8))
        def _():
            scatter_ocean(16 + t)


    @pl.loop(0, 16, step=4)
    def _(t):
        @pl.when(long_pairs(iflag, 8 * t, 32))
        def _():
            for j in range(4):
                scatter_ice(16 + t + j, j)

    itemp_next[...] = itemp[...] - 0.25 * (iacc[0:64, :] + iacc[64:128, :])
    stores[0].start()
    for copy in salts + [state]:
        copy.wait()

    @pl.loop(0, 16)
    def _(m):
        rows = pl.ds(pl.multiple_of(8 * m, 8), 8)
        sides = []
        for c in range(2):
            here = slice(8 * c, 8 * c + 8)
            flux = []
            for f in range(4):
                high, low = (pl.ds(pl.multiple_of(part + CJ * f + 8 * m, 8), 8) for part in (0, 4 * CJ))
                flux.append(oacc[high, c * 128 : (c + 1) * 128] + oacc[low, c * 128 : (c + 1) * 128])
            top = [q[m, f * K, here, :] for f in range(4)]
            top[0] = top[0] + 20.0 * flux[0]
            top[1] = top[1] - 10.0 * (salt[c, rows, :] * flux[1])
            top[2] = top[2] + 20.0 * flux[2]
            top[3] = top[3] + 20.0 * flux[3]
            x = top[2] * top[2] + (top[3] * top[3] + 0.01 * SCALE * SCALE)
            damp = 1.0 / (1.0 + take(drag[0], canopy[rows, c * 128 : (c + 1) * 128], 0) * (x * lax.rsqrt(x)))
            top[2], top[3] = top[2] * damp, top[3] * damp
            sides.append(top)
        solved = [[None] * 4 for _ in range(2)]
        for k in range(K - 1, -1, -1):
            for c in range(2):
                for f in range(4):
                    here = slice(8 * c, 8 * c + 8)
                    value = sides[c][f] if k == 0 else q[m, f * K + k, here, :] + TOP[k] * sides[c][f]
                    value = value * (1.0 / (SCALE * DIAG[k]))
                    if k < K - 1:
                        value = value + (0.5 / DIAG[k]) * solved[c][f]
                    solved[c][f] = value
                    ybuf[m, f * K + k, here, :] = value
        for c in range(2):
            pltpu.make_async_copy(
                ybuf.at[m, :, 8 * c : 8 * c + 8, :], y.at[:, rows, c * 128 : (c + 1) * 128], sems.at[4 + c]
            ).start()

    for c in range(2):
        part = y.at[:, :, c * 128 : (c + 1) * 128]
        pltpu.make_async_copy(part, part, sems.at[4 + c]).wait()


def staged(kernel, args, moved, outs, kept, scratch, **options):
    count, given = len(args), len(outs)

    def body(*refs):
        ins, results, rest = list(refs[:count]), list(refs[count : count + given]), list(refs[count + given :])
        sems = rest.pop()
        loads, stores = [], []
        for i in moved:
            place = rest.pop(0)
            loads.append(pltpu.make_async_copy(ins[i], place, sems.at[len(loads)]))
            ins[i] = place
        for i in range(given):
            if i not in kept:
                place = rest.pop(0)
                stores.append(pltpu.make_async_copy(place, results[i], sems.at[len(loads) + len(stores)]))
                results[i] = place
        for copy in loads:
            copy.start()
        kernel(loads, stores, *ins, *results, *rest)
        for copy in stores:
            copy.wait()

    places = [pltpu.VMEM(args[i].shape, args[i].dtype) for i in moved]
    places += [pltpu.VMEM(o.shape, o.dtype) for i, o in enumerate(outs) if i not in kept]
    return pl.pallas_call(
        body,
        out_shape=outs,
        in_specs=[ANY] * count,
        out_specs=(ANY,) * given,
        scratch_shapes=places + scratch + [pltpu.SemaphoreType.DMA((len(places),))],
        **options,
    )(*args)


def shards(
    ocean_state, canopy_type, drag_table, ocean_list, ice_list, weight_list, area_table, ice_temp, ice_cond, ice_vel
):
    st = ocean_state.reshape(FK, CJ, CI)
    olist, ilist, wlist = (x.reshape(DEV, SLOTS) for x in (ocean_list, ice_list, weight_list))
    itemp, icond = (x.reshape(64, 128) for x in (ice_temp, ice_cond))
    ivel = ice_vel.reshape(2, 64, 128).transpose(1, 0, 2).reshape(128, 128)
    area = area_table.reshape(1, 64)
    S = jax.ShapeDtypeStruct
    V = pltpu.VMEM
    tuv, rowlo, rowhi, colw, cole = staged(
        gather_kernel,
        (st, olist, olist),
        (2,),
        (S((3 * 128, 128), f32), S((FK, CI), f32), S((FK, CI), f32), S((CJ, 128), f32), S((CJ, 128), f32)),
        (),
        [
            V((2, FK, CJ, 128), f32), V((3, 2, CJ, 128), f32), V((768, 256), bf16), V((128, 128), i32),
            V((3 * 128, 128), f32), pltpu.SMEM((128, 128), i32), pltpu.SemaphoreType.DMA((4,)),
        ],
        compiler_params=pltpu.CompilerParams(vmem_limit_bytes=LIMIT),
        name="gather_slots",
    )
    q, inb, out = staged(
        stencil_kernel,
        (st, tuv, ilist, wlist, area, itemp, icond, ivel, canopy_type, drag_table, rowlo, rowhi, colw, cole),
        range(2, 10),
        (S((16, FK, 16, 128), f32), S((DEV, ROWS, 128), f32), S((DEV * ROWS, 128), f32)),
        range(3),
        [
            V((2, FK, 144, 128), f32), V((16, FK, 16, 128), f32), V((K, 8, 128), f32), V((DEV * ROWS, 128), f32),
            V((128, 128), f32), V((256, 256), bf16), V((128, 128), i32), V((4 * 128, 128), f32),
            V((NLON, NLAT // 2, ROWS, 128), f32), V((NLAT, NLON // 2, ROWS, 128), f32),
            V((FK, CI), f32), V((FK, CI), f32), V((CJ, 128), f32), V((CJ, 128), f32),
            pltpu.SemaphoreType.DMA((4, 2)), pltpu.SemaphoreType.DMA((15,)),
            pltpu.SemaphoreType.DMA((5,)), pltpu.SemaphoreType.DMA((4,)),
        ],
        compiler_params=pltpu.CompilerParams(vmem_limit_bytes=LIMIT, collective_id=0, has_side_effects=True),
        name="exchange_stencil",
    )
    y, itemp_next = staged(
        finish_kernel,
        (st, olist, ilist, q, inb.reshape(DEV * ROWS, 128), out, tuv, olist, ilist, canopy_type, drag_table, itemp),
        range(4, 12),
        (S((FK, CJ, CI), f32), S((64, 128), f32)),
        (0,),
        [
            V((16, FK, 16, 128), f32), V((16, FK, 16, 128), f32), V((2, CJ, 128), f32), V((K, 8, 128), f32),
            V((128, 128), i32), V((128, 128), i32), V((4 * 128, 128), f32), V((128, 128), f32),
            V((8 * CJ, CI), f32), V((128, 128), f32), V((4, 8 * CJ, 512), bf16), V((4, CI, 512), bf16),
            V((4, 128, 512), bf16), V((4, 128, 512), bf16),
            pltpu.SMEM((128, 128), i32), pltpu.SMEM((128, 128), i32), pltpu.SemaphoreType.DMA((7,)),
        ],
        compiler_params=pltpu.CompilerParams(vmem_limit_bytes=LIMIT),
        name="scatter_solve",
    )
    return y.reshape(ocean_state.shape), itemp_next.reshape(ice_temp.shape)


def solution(mesh):
    return jax.shard_map(
        shards,
        mesh=mesh,
        in_specs=(
            P(None, None, "lat", "lon"),
            P("lat", "lon"),
            P(),
            P(("lon", "lat"), None),
            P(("lon", "lat"), None),
            P(("lon", "lat"), None),
            P(),
            P(("lon", "lat"), None),
            P(("lon", "lat"), None),
            P(("lon", "lat"), None, None),
        ),
        out_specs=(P(None, None, "lat", "lon"), P(("lon", "lat"), None)),
        check_vma=False,
    )
```

```python
import functools

import jax
import jax.numpy as jnp
from jax import lax
from jax.experimental import pallas as pl
from jax.experimental.pallas import tpu as pltpu
from jax.sharding import PartitionSpec as P

f32 = jnp.float32
bf16 = jnp.bfloat16
i32 = jnp.int32
MESH = pl.DeviceIdType.MESH
K = 20
NF = 4
FK = NF * K
CJ = 128
CI = 256
NLON = 16
NLAT = 8
DEV = NLON * NLAT
SLOTS = 128
ROWS = 8
SENT = 6
SCALE = 40.0

DIAG = [1.5]
for _k in range(1, K):
    DIAG.append((1.5 if _k == K - 1 else 2.0) - 0.25 / DIAG[-1])
FWD = [0.0] + [0.5 / DIAG[_k - 1] for _k in range(1, K)]
TOP = [1.0]
for _k in range(1, K):
    TOP.append(FWD[_k] * TOP[-1])

ANY = pl.BlockSpec(memory_space=pl.ANY)
LIMIT = 60 << 20


def lanes():
    return lax.broadcasted_iota(i32, (8, 128), 1)


def take(table, index, axis):
    return jnp.take_along_axis(table, index, axis=axis, mode="promise_in_bounds")


def split(x):
    high = x.astype(bf16)
    return high, (x - high.astype(f32)).astype(bf16)


def one_hot(index, count):
    rows = lax.broadcasted_iota(i32, (count, index.shape[1]), 0)
    return rows == jnp.broadcast_to(index, (count, index.shape[1]))


def pack(even, odd):
    left = lanes() < 64
    return (
        jnp.where(left, even, pltpu.roll(odd, 64, 1)),
        jnp.where(left, pltpu.roll(even, 64, 1), odd),
    )


def pack_list(source, packed):
    for g in range(8):
        first, second = pack(
            source[pl.ds(16 * g, 8, stride=2), :], source[pl.ds(16 * g + 1, 8, stride=2), :]
        )
        packed[8 * g : 8 * g + 8, :] = first
        packed[64 + 8 * g : 72 + 8 * g, :] = second


def long_pairs(flags, first, count):
    most = flags[first, 64]
    for i in range(1, count):
        most = jnp.maximum(most, flags[first + i, 64])
    return most >= 0


def gather(tile, packed, table, fields, rows, got):
    hots, his = [], []
    for h in range(2):
        row = packed[pl.ds(2 * tile + h, 1), :]
        his.append(row >> 8)
        hots.append(jnp.where(one_hot(row & 255, 256), 1.0, 0.0).astype(bf16))
    res = jnp.dot(table[...], jnp.concatenate(hots, axis=1), preferred_element_type=f32)
    half = fields * rows
    res = res[:half] + res[half:]
    for h in range(2):
        mask = one_hot(his[h], rows)
        for f in range(fields):
            value = jnp.where(mask, res[f * rows : (f + 1) * rows, h * 128 : (h + 1) * 128], 0.0)
            got[pl.ds(f * 128 + 2 * tile + h, 1), :] = jnp.sum(value, axis=0, keepdims=True)


def unpack(got, f, g):
    left = lanes() < 64
    first = got[f * 128 + 8 * g : f * 128 + 8 * g + 8, :]
    second = got[f * 128 + 64 + 8 * g : f * 128 + 72 + 8 * g, :]
    return (
        jnp.where(left, first, pltpu.roll(second, 64, 1)),
        jnp.where(left, pltpu.roll(first, 64, 1), second),
    )


def gather_kernel(
    loads, stores, st, olist_any, olist,
    tuv, rowlo, rowhi, colw, cole,
    full, surf, otab, opack, ogot, oflag, sems,
):
    flags = pltpu.make_async_copy(olist_any, oflag, sems.at[0])
    tops = [
        pltpu.make_async_copy(st.at[f * K, :, c * 128 : (c + 1) * 128], surf.at[n, c], sems.at[1])
        for n, f in enumerate((0, 2, 3))
        for c in range(2)
    ]
    state = [
        pltpu.make_async_copy(st.at[:, :, c * 128 : (c + 1) * 128], full.at[c], sems.at[2 + c]) for c in range(2)
    ]
    for copy in tops:
        copy.start()
    loads[0].wait()
    pack_list(olist, opack)
    ogot[...] = jnp.zeros_like(ogot)
    pltpu.make_async_copy(surf, surf, sems.at[1]).wait()
    for copy in [flags] + state:
        copy.start()
    for n in range(3):
        for c in range(2):
            high, low = split(surf[n, c])
            otab[128 * n : 128 * n + 128, c * 128 : (c + 1) * 128] = high
            otab[384 + 128 * n : 512 + 128 * n, c * 128 : (c + 1) * 128] = low

    def columns(m):
        lane = lanes()
        rows = pl.ds(pl.multiple_of(8 * m, 8), 8)
        west = jnp.zeros((8, 128), f32)
        east = jnp.zeros((8, 128), f32)
        for fk in range(FK):
            both = jnp.where(lane == 127, full[1, fk, rows, :], full[0, fk, rows, :])
            both = pltpu.roll(both, fk, 1) if fk else both
            west = jnp.where(lane == fk, both, west)
            east = jnp.where(lane == (fk - 1) % 128, both, east)
        colw[rows, :] = west
        cole[rows, :] = east

    @pl.loop(0, 4)
    def _(t):
        for j in range(4):
            gather(4 * t + j, opack, otab, 3, 128, ogot)

    for copy in state:
        copy.wait()

    @pl.loop(4, 8)
    def _(t):
        for j in range(4):
            gather(4 * t + j, opack, otab, 3, 128, ogot)
        for j in range(4):
            columns(4 * (t - 4) + j)

    for fk in range(FK):
        for c in range(2):
            rowlo[fk : fk + 1, c * 128 : (c + 1) * 128] = full[c, fk, 0:1, :]
            rowhi[fk : fk + 1, c * 128 : (c + 1) * 128] = full[c, fk, 127:128, :]
    for copy in stores[1:]:
        copy.start()
    flags.wait()

    @pl.loop(0, 32)
    def _(t):
        @pl.when(long_pairs(oflag, 4 * t, 4))
        def _():
            gather(32 + t, opack, otab, 3, 128, ogot)

    for g in range(8):
        for n in range(3):
            even, odd = unpack(ogot, n, g)
            tuv[pl.ds(128 * n + 16 * g, 8, stride=2), :] = even
            tuv[pl.ds(128 * n + 16 * g + 1, 8, stride=2), :] = odd
    stores[0].start()


def stencil_row(m, buf, q, canopy, east_col, west_col, drag, lat):
    lane = lanes()
    sub = lax.broadcasted_iota(i32, (8, 128), 0)
    first, last = lane == 0, lane == 127
    rows = pl.ds(pl.multiple_of(8 * m, 8), 8)
    east_halo, west_halo = east_col[rows, :], west_col[rows, :]
    kind = [canopy[rows, c * 128 : (c + 1) * 128] for c in range(2)]
    row = (lat * CJ + 8 * m + sub).astype(f32)
    cor = 4.0 * (2.0 * (row + 0.5) / (CJ * NLAT) - 1.0)
    for c in range(2):
        elim = [None] * NF
        gx = gy = None
        for k in range(K):
            C, E, W, N, S = ([None] * NF for _ in range(5))
            for f in range(NF):
                fk = f * K + k
                mine, other = (buf[d, fk, pl.ds(pl.multiple_of(8 + 8 * m, 8), 8), :] for d in (c, 1 - c))
                C[f] = mine
                N[f] = buf[c, fk, pl.ds(9 + 8 * m, 8), :]
                S[f] = buf[c, fk, pl.ds(7 + 8 * m, 8), :]
                if c == 0:
                    E[f] = pltpu.roll(jnp.where(first, other, mine), 127, 1)
                    W[f] = jnp.where(first, pltpu.roll(west_halo, (1 - fk) % 128, 1), pltpu.roll(mine, 1, 1))
                else:
                    E[f] = jnp.where(last, pltpu.roll(east_halo, (127 - fk) % 128, 1), pltpu.roll(mine, 127, 1))
                    W[f] = pltpu.roll(jnp.where(last, other, mine), 1, 1)
            u, v = C[2], C[3]
            eE = (0.4 - u) - E[2]
            eW = (0.4 + u) + W[2]
            eN = (0.4 - v) - N[3]
            eS = (0.4 + v) + S[3]
            mid = 36.8 + ((eE + eW) + (eN + eS))
            new = [(C[f] * mid + E[f] * eE) + (W[f] * eW + N[f] * eN) + S[f] * eS for f in range(NF)]
            hx = 0.4 * (E[1] - W[1]) - 0.1 * (E[0] - W[0])
            hy = 0.4 * (N[1] - S[1]) - 0.1 * (N[0] - S[0])
            px = hx if k == 0 else gx + hx
            py = hy if k == 0 else gy + hy
            gx, gy = px + hx, py + hy
            new[2] = new[2] + (cor * v - px)
            new[3] = new[3] - (cor * u + py)
            if k > 0:
                x = new[2] * new[2] + (new[3] * new[3] + 0.01 * SCALE * SCALE)
                damp = 1.0 / (1.0 + take(drag[k], kind[c], 0) * (x * lax.rsqrt(x)))
                new[2], new[3] = new[2] * damp, new[3] * damp
            for f in range(NF):
                if k > 1:
                    new[f] = new[f] + FWD[k] * elim[f]
                elim[f] = new[f]
                q[m, f * K + k, c * 8 : (c + 1) * 8, :] = new[f]


def drag_levels(table, drag):
    for k in range(K):
        drag[k] = jnp.broadcast_to(table[:, k : k + 1] * (0.1 / SCALE), (8, 128))


def ice_messages(ilist, wlist, area, itemp, icond, ivel, msg, itab, ipack, igot):
    @pl.loop(0, 64, step=8)
    def _(t):
        for j in range(8):
            gather(t + j, ipack, itab, 4, 32, igot)

    areas = jnp.broadcast_to(jnp.concatenate([area[...], area[...]], axis=1), (8, 128))
    for g in range(8):
        for f in range(4):
            even, odd = unpack(igot, f, g)
            msg[pl.ds(128 * g + 2 + f, 8, stride=16), :] = even
            msg[pl.ds(128 * g + 10 + f, 8, stride=16), :] = odd
    for g in range(16):
        index = wlist[8 * g : 8 * g + 8, :]
        value = jnp.where(index >= 0, take(areas, index & 63, 1), 0.0)
        msg[pl.ds(64 * g + 1, 8, stride=8), :] = value
        for f in range(SENT, ROWS):
            msg[pl.ds(64 * g + f, 8, stride=8), :] = jnp.zeros((8, 128), f32)


def stencil_kernel(
    operands, _, st, tuv, ilist, wlist, area, itemp, icond, ivel, canopy, table, rowlo, rowhi, colw, cole,
    q_any, inb, out,
    buf, q, drag, msg, temps, itab, ipack, igot, mid_a, mid_b, north, south, east_col, west_col, sems, hops, halo_send, halo_recv,
):
    lon, lat = lax.axis_index("lon"), lax.axis_index("lat")
    loads = [
        [
            pltpu.make_async_copy(
                st.at[:, 32 * g : 32 * g + 32, c * 128 : (c + 1) * 128],
                buf.at[c, :, 8 + 32 * g : 40 + 32 * g, :],
                sems.at[g, c],
            )
            for c in range(2)
        ]
        for g in range(4)
    ]
    surface = pltpu.make_async_copy(tuv.at[0:128], temps, hops.at[13])
    surface.start()
    barrier = pltpu.get_barrier_semaphore()
    for i in range(1, NLON):
        pl.semaphore_signal(barrier, inc=1, device_id=(lax.rem(lon + i, NLON), lat), device_id_type=MESH)
    for i in range(1, NLAT):
        pl.semaphore_signal(barrier, inc=1, device_id=(lon, lax.rem(lat + i, NLAT)), device_id_type=MESH)
    for copy in operands:
        copy.wait()
    for pair in loads:
        for copy in pair:
            copy.start()
    pack_list(ilist, ipack)
    for f in range(4):
        for c in range(2):
            if f < 2:
                x = (icond, itemp)[f][pl.ds(c, 32, stride=2), :]
            else:
                x = ivel[pl.ds(2 * c + f - 2, 32, stride=4), :]
            high, low = split(x)
            itab[32 * f : 32 * f + 32, c * 128 : (c + 1) * 128] = high
            itab[128 + 32 * f : 160 + 32 * f, c * 128 : (c + 1) * 128] = low
    pl.semaphore_wait(barrier, NLON + NLAT - 2)

    def halo(src, dst, n, target):
        return pltpu.make_async_remote_copy(
            src_ref=src, dst_ref=dst, send_sem=halo_send.at[n], recv_sem=halo_recv.at[n],
            device_id=target, device_id_type=MESH,
        )

    to_west = halo(colw, east_col, 0, (lax.rem(lon + NLON - 1, NLON), lat))
    to_east = halo(cole, west_col, 1, (lax.rem(lon + 1, NLON), lat))
    to_north = halo(rowhi, south, 2, (lon, lax.rem(lat + 1, NLAT)))
    to_south = halo(rowlo, north, 3, (lon, lax.rem(lat + NLAT - 1, NLAT)))
    to_fold = halo(rowhi, north, 3, (NLON - 1 - lon, lat))
    to_west.start()
    to_east.start()
    to_north.start()

    @pl.when(lat > 0)
    def _():
        to_south.start()

    @pl.when(lat == NLAT - 1)
    def _():
        pltpu.make_async_remote_copy(
            src_ref=rowhi, dst_ref=north, send_sem=halo_send.at[4], recv_sem=halo_recv.at[3],
            device_id=(NLON - 1 - lon, lat), device_id_type=MESH,
        ).start()

    def hop(src, dst, n, target):
        return pltpu.make_async_remote_copy(
            src_ref=src, dst_ref=dst, send_sem=hops.at[n], recv_sem=hops.at[n + 1],
            device_id=target, device_id_type=MESH,
        )

    ice_messages(ilist, wlist, area, itemp, icond, ivel, msg, itab, ipack, igot)
    surface.wait()
    for g in range(16):
        msg[pl.ds(64 * g, 8, stride=8), :] = temps[8 * g : 8 * g + 8, :]
    keep = pltpu.make_async_copy(msg, out, hops.at[12])
    keep.start()
    even = lax.rem(lon + lat, 2) == 0
    by_a = msg.reshape(NLON, NLAT // 2, 2, ROWS, 128)
    by_b = msg.reshape(NLON // 2, 2, NLAT, ROWS, 128)

    def first_a(peer):
        return by_a.at[peer, :, lax.rem(peer, 2), 0:SENT], mid_a.at[lon, :, 0:SENT]

    def first_b(peer):
        return by_b.at[:, 1 - lax.rem(peer, 2), peer, 0:SENT], mid_b.at[lat, :, 0:SENT]

    for i in range(1, NLON):
        peer = lax.rem(lon + i, NLON)
        hop(*first_a(peer), 0, (peer, lat)).start()
    for i in range(1, NLAT):
        peer = lax.rem(lat + i, NLAT)
        hop(*first_b(peer), 2, (lon, peer)).start()
    own_a = pltpu.make_async_copy(*first_a(lon), hops.at[8])
    own_b = pltpu.make_async_copy(*first_b(lat), hops.at[9])
    own_a.start()
    own_b.start()
    in4 = inb.reshape(NLON, NLAT, ROWS, 128)

    def second_a(peer):
        return mid_a.at[:, peer // 2, 0:SENT], in4.at[:, lat, 0:SENT]

    def second_b(peer):
        return mid_b.at[:, peer // 2, 0:SENT], in4.at[lon, :, 0:SENT]

    def blocks(ref, n):
        part = ref.at[0:n, 0:SENT]
        return part, part

    def taken(n, sem):
        pltpu.make_async_copy(*blocks(inb, n), hops.at[sem]).wait()

    drag_levels(table, drag)
    to_west.wait_recv()
    to_east.wait_recv()
    to_north.wait_recv()
    to_fold.wait_recv()
    top = lat == NLAT - 1
    inside = jnp.where(lat > 0, 1.0, 0.0)
    back = 127 - lanes()
    for g in range(10):
        part = slice(8 * g, 8 * g + 8)
        sign = 1.0 if g < 5 else -1.0
        halves = [north[part, c * 128 : (c + 1) * 128] for c in range(2)]
        for c in range(2):
            turned = sign * take(halves[1 - c], back, 1)
            value = jnp.where(top, turned, halves[c])
            below = south[part, c * 128 : (c + 1) * 128] * inside
            for r in range(8):
                buf[c, 8 * g + r, 136:137, :] = value[r : r + 1]
                buf[c, 8 * g + r, 7:8, :] = below[r : r + 1]
    for copy in loads[0]:
        copy.wait()

    @pl.loop(0, 8)
    def _(g):
        @pl.when(lax.rem(g, 2) - jnp.where(g > 5, 1, 0) == 1)
        def _():
            for c in range(2):
                pltpu.make_async_copy(
                    st.at[:, 0:32, 0:128], buf.at[c, :, 8:40, :], sems.at[g // 2 + 1, c]
                ).wait()

        @pl.when(g == 4)
        def _():
            taken((NLON - 1) * NLAT // 2, 1)
            taken((NLAT - 1) * NLON // 2, 3)
            own_a.wait()
            own_b.wait()

            @pl.when(even)
            def _():
                pltpu.make_async_copy(*second_a(lat), hops.at[10]).start()
                for i in range(2, NLAT, 2):
                    peer = lax.rem(lat + i, NLAT)
                    hop(*second_a(peer), 4, (lon, peer)).start()
                for i in range(1, NLON, 2):
                    peer = lax.rem(lon + i, NLON)
                    hop(*second_b(peer), 6, (peer, lat)).start()

            @pl.when(jnp.logical_not(even))
            def _():
                pltpu.make_async_copy(*second_b(lon), hops.at[11]).start()
                for i in range(1, NLAT, 2):
                    peer = lax.rem(lat + i, NLAT)
                    hop(*second_a(peer), 4, (lon, peer)).start()
                for i in range(2, NLON, 2):
                    peer = lax.rem(lon + i, NLON)
                    hop(*second_b(peer), 6, (peer, lat)).start()

        for j in range(2):
            stencil_row(2 * g + j, buf, q, canopy, east_col, west_col, drag, lat)
        for j in range(2):
            pltpu.make_async_copy(q.at[2 * g + j], q_any.at[2 * g + j], hops.at[14]).start()

    pltpu.make_async_copy(q, q_any, hops.at[14]).wait()
    keep.wait()
    @pl.when(even)
    def _():
        taken((NLAT - 1) * NLON, 5)
        taken(NLON, 10)
        taken((NLAT // 2 - 1) * NLON, 4)
        taken((NLON // 2) * NLAT, 6)

    @pl.when(jnp.logical_not(even))
    def _():
        taken((NLON - 1) * NLAT, 7)
        taken(NLAT, 11)
        taken((NLAT // 2) * NLON, 4)
        taken((NLON // 2 - 1) * NLAT, 6)

    taken((NLON - 1) * NLAT // 2, 0)
    taken((NLAT - 1) * NLON // 2, 2)
    to_west.wait_send()
    to_east.wait_send()
    to_north.wait_send()

    @pl.when(lat > 0)
    def _():
        to_south.wait_send()

    @pl.when(lat == NLAT - 1)
    def _():
        pltpu.make_async_copy(rowhi, rowhi, halo_send.at[4]).wait()


def finish_kernel(
    loads, stores, st, olist_any, ilist_any, q_any, inb, out, tuv, olist, ilist, canopy, table, itemp,
    y, itemp_next,
    q, ybuf, salt, drag, opack, ipack, oval, ival, oacc, iacc, owide, ocols, iwide, icols, oflag, iflag, sems,
):
    flags = [
        pltpu.make_async_copy(olist_any, oflag, sems.at[0]),
        pltpu.make_async_copy(ilist_any, iflag, sems.at[1]),
    ]
    salts = [
        pltpu.make_async_copy(st.at[K, :, c * 128 : (c + 1) * 128], salt.at[c], sems.at[2 + c])
        for c in range(2)
    ]
    state = pltpu.make_async_copy(q_any, q, sems.at[6])
    oacc[...] = jnp.zeros_like(oacc)
    iacc[...] = jnp.zeros_like(iacc)
    for copy in loads[3:5]:
        copy.wait()
    pack_list(olist, opack)
    pack_list(ilist, ipack)
    for copy in loads[0:3] + loads[5:]:
        copy.wait()
    for copy in flags + salts + [state]:
        copy.start()
    drag_levels(table, drag)
    for g in range(8):
        sides, ices = [], []
        for odd in range(2):
            block = lambda ref, f: ref[pl.ds(128 * g + 8 * odd + f, 8, stride=16), :]
            slot = [tuv[pl.ds(128 * n + 16 * g + odd, 8, stride=2), :] for n in range(3)]
            a, cond, temp, iu, iv = (block(inb, f) for f in range(1, 6))
            du, dv = iu - slot[1], iv - slot[2]
            x = du * du + dv * dv + 0.01
            drift = 0.5 * a * (x * lax.rsqrt(x))
            heat = a * cond
            sides.append([heat * (temp - slot[0]), heat, drift * du, drift * dv])
            ices.append(block(out, 1) * block(out, 2) * (block(out, 3) - block(inb, 0)))
        for f in range(4):
            first, second = pack(sides[0][f], sides[1][f])
            oval[128 * f + 8 * g : 128 * f + 8 * g + 8, :] = first
            oval[128 * f + 64 + 8 * g : 128 * f + 72 + 8 * g, :] = second
        first, second = pack(*ices)
        ival[8 * g : 8 * g + 8, :] = first
        ival[64 + 8 * g : 72 + 8 * g, :] = second

    def hot_columns(tile, packed, width, cols):
        for h in range(4):
            index = packed[pl.ds(4 * tile + h, 1), :] & (width - 1)
            cols[:, 128 * h : 128 * h + 128] = jnp.where(one_hot(index, width), 1.0, 0.0).astype(bf16)

    def add(wide, cols, acc):
        acc[...] += lax.dot_general(wide, cols, (((1,), (1,)), ((), ())), preferred_element_type=f32)

    def scatter_ocean(tile, p=0):
        hot_columns(tile, opack, CI, ocols.at[p])
        for h in range(4):
            mask = one_hot(opack[pl.ds(4 * tile + h, 1), :] >> 8, CJ)
            for f in range(4):
                value = oval[pl.ds(128 * f + 4 * tile + h, 1), :]
                high = value.astype(bf16).astype(f32)
                for n, part in enumerate((high, value - high)):
                    part = jnp.where(mask, jnp.broadcast_to(part, (CJ, 128)), 0.0).astype(bf16)
                    owide[p, 512 * n + CJ * f : 512 * n + CJ * (f + 1), 128 * h : 128 * h + 128] = part
        add(owide[p], ocols[p], oacc)

    def scatter_ice(tile, p=0):
        hot_columns(tile, ipack, 128, icols.at[p])
        for h in range(4):
            mask = one_hot(ipack[pl.ds(4 * tile + h, 1), :] >> 7, 64)
            value = ival[pl.ds(4 * tile + h, 1), :]
            high = value.astype(bf16).astype(f32)
            for n, part in enumerate((high, value - high)):
                part = jnp.where(mask, jnp.broadcast_to(part, (64, 128)), 0.0).astype(bf16)
                iwide[p, 64 * n : 64 * n + 64, 128 * h : 128 * h + 128] = part
        add(iwide[p], icols[p], iacc)

    @pl.loop(0, 16, step=4)
    def _(t):
        for j in range(4):
            scatter_ocean(t + j, j)
            scatter_ice(t + j, j)

    for copy in flags:
        copy.wait()

    @pl.loop(0, 16)
    def _(t):
        @pl.when(long_pairs(oflag, 8 * t, 8))
        def _():
            scatter_ocean(16 + t)


    @pl.loop(0, 16, step=4)
    def _(t):
        @pl.when(long_pairs(iflag, 8 * t, 32))
        def _():
            for j in range(4):
                scatter_ice(16 + t + j, j)

    itemp_next[...] = itemp[...] - 0.25 * (iacc[0:64, :] + iacc[64:128, :])
    stores[0].start()
    for copy in salts + [state]:
        copy.wait()

    @pl.loop(0, 16)
    def _(m):
        rows = pl.ds(pl.multiple_of(8 * m, 8), 8)
        sides = []
        for c in range(2):
            here = slice(8 * c, 8 * c + 8)
            flux = []
            for f in range(4):
                high, low = (pl.ds(pl.multiple_of(part + CJ * f + 8 * m, 8), 8) for part in (0, 4 * CJ))
                flux.append(oacc[high, c * 128 : (c + 1) * 128] + oacc[low, c * 128 : (c + 1) * 128])
            top = [q[m, f * K, here, :] for f in range(4)]
            top[0] = top[0] + 20.0 * flux[0]
            top[1] = top[1] - 10.0 * (salt[c, rows, :] * flux[1])
            top[2] = top[2] + 20.0 * flux[2]
            top[3] = top[3] + 20.0 * flux[3]
            x = top[2] * top[2] + (top[3] * top[3] + 0.01 * SCALE * SCALE)
            damp = 1.0 / (1.0 + take(drag[0], canopy[rows, c * 128 : (c + 1) * 128], 0) * (x * lax.rsqrt(x)))
            top[2], top[3] = top[2] * damp, top[3] * damp
            sides.append(top)
        solved = [[None] * 4 for _ in range(2)]
        for k in range(K - 1, -1, -1):
            for c in range(2):
                for f in range(4):
                    here = slice(8 * c, 8 * c + 8)
                    value = sides[c][f] if k == 0 else q[m, f * K + k, here, :] + TOP[k] * sides[c][f]
                    value = value * (1.0 / (SCALE * DIAG[k]))
                    if k < K - 1:
                        value = value + (0.5 / DIAG[k]) * solved[c][f]
                    solved[c][f] = value
                    ybuf[m, f * K + k, here, :] = value
        for c in range(2):
            pltpu.make_async_copy(
                ybuf.at[m, :, 8 * c : 8 * c + 8, :], y.at[:, rows, c * 128 : (c + 1) * 128], sems.at[4 + c]
            ).start()

    for c in range(2):
        part = y.at[:, :, c * 128 : (c + 1) * 128]
        pltpu.make_async_copy(part, part, sems.at[4 + c]).wait()


def staged(kernel, args, moved, outs, kept, scratch, **options):
    count, given = len(args), len(outs)

    def body(*refs):
        ins, results, rest = list(refs[:count]), list(refs[count : count + given]), list(refs[count + given :])
        sems = rest.pop()
        loads, stores = [], []
        for i in moved:
            place = rest.pop(0)
            loads.append(pltpu.make_async_copy(ins[i], place, sems.at[len(loads)]))
            ins[i] = place
        for i in range(given):
            if i not in kept:
                place = rest.pop(0)
                stores.append(pltpu.make_async_copy(place, results[i], sems.at[len(loads) + len(stores)]))
                results[i] = place
        for copy in loads:
            copy.start()
        kernel(loads, stores, *ins, *results, *rest)
        for copy in stores:
            copy.wait()

    places = [pltpu.VMEM(args[i].shape, args[i].dtype) for i in moved]
    places += [pltpu.VMEM(o.shape, o.dtype) for i, o in enumerate(outs) if i not in kept]
    return pl.pallas_call(
        body,
        out_shape=outs,
        in_specs=[ANY] * count,
        out_specs=(ANY,) * given,
        scratch_shapes=places + scratch + [pltpu.SemaphoreType.DMA((len(places),))],
        **options,
    )(*args)


def shards(
    ocean_state, canopy_type, drag_table, ocean_list, ice_list, weight_list, area_table, ice_temp, ice_cond, ice_vel
):
    st = ocean_state.reshape(FK, CJ, CI)
    olist, ilist, wlist = (x.reshape(DEV, SLOTS) for x in (ocean_list, ice_list, weight_list))
    itemp, icond = (x.reshape(64, 128) for x in (ice_temp, ice_cond))
    ivel = ice_vel.reshape(2, 64, 128).transpose(1, 0, 2).reshape(128, 128)
    area = area_table.reshape(1, 64)
    S = jax.ShapeDtypeStruct
    V = pltpu.VMEM
    tuv, rowlo, rowhi, colw, cole = staged(
        gather_kernel,
        (st, olist, olist),
        (2,),
        (S((3 * 128, 128), f32), S((FK, CI), f32), S((FK, CI), f32), S((CJ, 128), f32), S((CJ, 128), f32)),
        (),
        [
            V((2, FK, CJ, 128), f32), V((3, 2, CJ, 128), f32), V((768, 256), bf16), V((128, 128), i32),
            V((3 * 128, 128), f32), pltpu.SMEM((128, 128), i32), pltpu.SemaphoreType.DMA((4,)),
        ],
        compiler_params=pltpu.CompilerParams(vmem_limit_bytes=LIMIT),
        name="gather_slots",
    )
    q, inb, out = staged(
        stencil_kernel,
        (st, tuv, ilist, wlist, area, itemp, icond, ivel, canopy_type, drag_table, rowlo, rowhi, colw, cole),
        range(2, 10),
        (S((16, FK, 16, 128), f32), S((DEV, ROWS, 128), f32), S((DEV * ROWS, 128), f32)),
        range(3),
        [
            V((2, FK, 144, 128), f32), V((16, FK, 16, 128), f32), V((K, 8, 128), f32), V((DEV * ROWS, 128), f32),
            V((128, 128), f32), V((256, 256), bf16), V((128, 128), i32), V((4 * 128, 128), f32),
            V((NLON, NLAT // 2, ROWS, 128), f32), V((NLAT, NLON // 2, ROWS, 128), f32),
            V((FK, CI), f32), V((FK, CI), f32), V((CJ, 128), f32), V((CJ, 128), f32),
            pltpu.SemaphoreType.DMA((4, 2)), pltpu.SemaphoreType.DMA((15,)),
            pltpu.SemaphoreType.DMA((5,)), pltpu.SemaphoreType.DMA((4,)),
        ],
        compiler_params=pltpu.CompilerParams(vmem_limit_bytes=LIMIT, collective_id=0, has_side_effects=True),
        name="exchange_stencil",
    )
    y, itemp_next = staged(
        finish_kernel,
        (st, olist, ilist, q, inb.reshape(DEV * ROWS, 128), out, tuv, olist, ilist, canopy_type, drag_table, itemp),
        range(4, 12),
        (S((FK, CJ, CI), f32), S((64, 128), f32)),
        (0,),
        [
            V((16, FK, 16, 128), f32), V((16, FK, 16, 128), f32), V((2, CJ, 128), f32), V((K, 8, 128), f32),
            V((128, 128), i32), V((128, 128), i32), V((4 * 128, 128), f32), V((128, 128), f32),
            V((8 * CJ, CI), f32), V((128, 128), f32), V((4, 8 * CJ, 512), bf16), V((4, CI, 512), bf16),
            V((4, 128, 512), bf16), V((4, 128, 512), bf16),
            pltpu.SMEM((128, 128), i32), pltpu.SMEM((128, 128), i32), pltpu.SemaphoreType.DMA((7,)),
        ],
        compiler_params=pltpu.CompilerParams(vmem_limit_bytes=LIMIT),
        name="scatter_solve",
    )
    return y.reshape(ocean_state.shape), itemp_next.reshape(ice_temp.shape)


def solution(mesh):
    return jax.shard_map(
        shards,
        mesh=mesh,
        in_specs=(
            P(None, None, "lat", "lon"),
            P("lat", "lon"),
            P(),
            P(("lon", "lat"), None),
            P(("lon", "lat"), None),
            P(("lon", "lat"), None),
            P(),
            P(("lon", "lat"), None),
            P(("lon", "lat"), None),
            P(("lon", "lat"), None, None),
        ),
        out_specs=(P(None, None, "lat", "lon"), P(("lon", "lat"), None)),
        check_vma=False,
    )
```
